32 devices in a mesh: dp: 16 (over z, y, core), head: 2 (over x).
Axes of the slice: x: 2, y: 2, z: 4, core: 2. Of those that a mesh axis runs over, the one named last changes fastest.
Arguments:
- tokens: bfloat16 [32, 1024, 512], P('dp', 'head'), may hold values from -6 to 6
- memory: bfloat16 [32, 1024, 512], P('dp', 'head'), may hold values from -6 to 6
- lengths: int32 [32, 4], P('dp'), may hold values from 1 to 1021, as said below
- slot_mask: int32 [32, 1024], P('dp', 'head'), may hold values 0 or 1
- self_qkv: bfloat16 [3, 512, 512], replicated, may hold values from -0.25 to 0.25
- self_out: bfloat16 [512, 512], replicated, may hold values from -1.5 to 1.5
- cross_qkv: bfloat16 [3, 512, 512], replicated, may hold values from -0.25 to 0.25
- cross_out: bfloat16 [512, 512], replicated, may hold values from -1.5 to 1.5
- norm_gain: float32 [3, 512], replicated, may hold values from 0.5 to 1.5
- norm_bias: float32 [3, 512], replicated, may hold values from -0.5 to 0.5
- ffn_in: bfloat16 [512, 2048], replicated, may hold values from -0.25 to 0.25
- ffn_out: bfloat16 [2048, 512], replicated, may hold values from -0.125 to 0.125
- slot_proj: bfloat16 [1024, 512], replicated, may hold values from -0.1875 to 0.1875
- out_cot: bfloat16 [32, 1024, 512], P('dp', 'head'), may hold values from -6 to 6
- slot_cot: bfloat16 [32, 1024, 512], P('dp', 'head'), may hold values from -6 to 6
Outputs:
- out: bfloat16 [32, 1024, 512], P('dp', 'head')
- slots: bfloat16 [32, 1024, 512], P('dp', 'head')
- grad_tokens: float32 [32, 1024, 512], P('dp', 'head')
- grad_memory: float32 [32, 1024, 512], P('dp', 'head')
- grad_self_qkv: float32 [3, 512, 512], P(None, None, 'head')
- grad_self_out: float32 [512, 512], P('head')
- grad_cross_qkv: float32 [3, 512, 512], P(None, None, 'head')
- grad_cross_out: float32 [512, 512], P('head')
- grad_norm_gain: float32 [3, 512], P(None, 'head')
- grad_norm_bias: float32 [3, 512], P(None, 'head')
- grad_ffn_in: float32 [512, 2048], P(None, 'head')
- grad_ffn_out: float32 [2048, 512], P('head')
- grad_slot_proj: float32 [1024, 512], P('head')
The draws below stay inside these ranges and needn't reach their ends.
Inputs may be any that keep to these rules, and one draw needn't show every extreme that they name: Each row's 4 lengths sum to 1024. In every aligned block of 2 rows, one row, drawn from the seed, holds one document of 1021 tokens, at a place among its 4 drawn from the seed, and documents of one token at the other places.
All inputs are finite; a program needn't handle non-finite values. No bound on the sum of `slot_mask` on one device may be relied on, other than what follows from the above.
Results may differ from the reference program's by a relative error of at most 0.024.
Values may be sent and summed in bfloat16 or wider, within the bound.
A program may use at most 256 MiB of HBM per device.

```python
import jax
import jax.numpy as jnp
from jax import lax

D = 512
HEADS = 8
FF = 2048
L = 1024
DOCS = 4
ROWS_DEV = 2
HEAD_DIM = 64
ROWS = 32


def draw_lengths(key, part):
    key = jax.random.fold_in(key, 7)
    weight_key, pick_key, place_key = jax.random.split(key, 3)
    portions = jax.random.randint(weight_key, (ROWS, DOCS), 1, 9).astype(jnp.int32)
    cumulative = jnp.cumsum(portions, axis=1)
    total_weight = cumulative[:, -1:]
    doc_ends = cumulative * L // total_weight
    doc_starts = jnp.concatenate([jnp.zeros((ROWS, 1), jnp.int32), doc_ends[:, :-1]], axis=1)
    ragged = doc_ends - doc_starts
    blocks = ROWS // ROWS_DEV
    long_place = jax.random.randint(place_key, (blocks,), 0, DOCS).astype(jnp.int32)
    place_rows = jnp.repeat(long_place, ROWS_DEV, total_repeat_length=ROWS)
    doc_index = jnp.arange(DOCS, dtype=jnp.int32)
    spanning = jnp.where(doc_index[None, :] == place_rows[:, None], L - DOCS + 1, 1).astype(jnp.int32)
    chosen_row = jax.random.randint(pick_key, (blocks,), 0, ROWS_DEV).astype(jnp.int32)
    within = jnp.arange(ROWS, dtype=jnp.int32) % ROWS_DEV
    picked = within == jnp.repeat(chosen_row, ROWS_DEV, total_repeat_length=ROWS)
    return jnp.where(picked[:, None], spanning, ragged).astype(jnp.int32)


def place_ends(values, rng, smallest, top_value):
    dims = values.shape
    index_at = [jax.random.randint(jax.random.fold_in(rng, axis), (), 0, dims[axis]) for axis in range(len(dims))]
    values = values.at[tuple(index_at)].set(smallest)
    longest = dims.index(max(dims))
    index_at[longest] = (index_at[longest] + 1) % dims[longest]
    return values.at[tuple(index_at)].set(top_value)


def levels(stream_key, shape, shards, least, top_value):
    level, own = 1.0, jax.random.fold_in(stream_key, 6)
    for dim, shards_of in shards:
        steps = jnp.exp(jax.random.uniform(jax.random.fold_in(own, dim), (shards_of,), jnp.float32, least / len(shards), top_value / len(shards)))
        level = level * jnp.repeat(steps, shape[dim] // shards_of).reshape([-1 if axis == dim else 1 for axis in range(len(shape))])
    return level


def noise(stream_key, extent, deviation, most, cuts=(), kind=jnp.bfloat16):
    result = jax.random.normal(stream_key, extent, jnp.float32) * deviation
    if len(cuts) > 0:
        result = levels(stream_key, extent, cuts, -0.22, 0.18) * result
    return jnp.clip(result, min=-most, max=most).astype(kind)


def setup_inputs(seed: int = 0) -> dict:
    key_of = jax.random.split(jax.random.key(seed), 16)
    tokens = noise(key_of[0], (ROWS, L, D), 1.0, 6.0, ((0, 16), (1, 2)))
    memory = noise(key_of[1], (ROWS, L, D), 1.0, 6.0, ((0, 16), (1, 2)))
    lengths = draw_lengths(jax.random.fold_in(key_of[15], 71), 0)
    slot_mask = place_ends((jax.random.randint(key_of[3], (ROWS, L), 0, 4) < 3).astype(jnp.int32), jax.random.fold_in(key_of[3], 1), 0, 1)
    self_qkv = noise(key_of[4], (3, D, D), D ** -0.5, 0.25)
    self_out = noise(key_of[5], (D, D), 16 ** -0.5, 1.5)
    cross_qkv = noise(key_of[6], (3, D, D), D ** -0.5, 0.25)
    cross_out = noise(key_of[7], (D, D), 16 ** -0.5, 1.5)
    norm_gain = jnp.clip(1.0 + 0.1 * jax.random.normal(key_of[8], (3, D), jnp.float32), 0.5, 1.5)
    norm_bias = noise(key_of[9], (3, D), 0.1, 0.5, (), jnp.float32)
    ffn_in = noise(key_of[10], (D, FF), D ** -0.5, 0.25)
    ffn_out = noise(key_of[11], (FF, D), FF ** -0.5, 0.125)
    slot_proj = noise(key_of[12], (2 * D, D), (2 * D) ** -0.5, 0.1875)
    out_cot = noise(key_of[13], (ROWS, L, D), 1.0, 6.0, ((0, 16), (1, 2)))
    slot_cot = noise(key_of[14], (ROWS, L, D), 1.0, 6.0, ((0, 16), (1, 2)))
    return {"tokens": tokens, "memory": memory, "lengths": lengths, "slot_mask": slot_mask, "self_qkv": self_qkv, "self_out": self_out, "cross_qkv": cross_qkv, "cross_out": cross_out, "norm_gain": norm_gain, "norm_bias": norm_bias, "ffn_in": ffn_in, "ffn_out": ffn_out, "slot_proj": slot_proj, "out_cot": out_cot, "slot_cot": slot_cot}


@jax.custom_vjp
def low(v):
    return lax.optimization_barrier(v.astype(jnp.bfloat16)).astype(jnp.float32)

@jax.custom_vjp
def low_back(v):
    return v

def low_keep(v):
    return (low(v), None)

def low_pass(kept, grad):
    return (grad,)

def back_keep(v):
    return (v, None)

def back_low(kept, grad):
    return (low(grad),)
low.defvjp(low_keep, low_pass)
low_back.defvjp(back_keep, back_low)
precise = lax.Precision.HIGHEST

def norm_layer(incoming, gain_row, shift_bias):
    average = lax.optimization_barrier(jnp.mean(incoming, axis=-1, keepdims=True))
    centred = incoming - average
    variance = lax.optimization_barrier(jnp.mean(centred * centred, axis=-1, keepdims=True))
    return centred * lax.rsqrt(variance + 1e-05) * gain_row + shift_bias

def attend(queries, key_rows, values, same_doc):
    scores = jnp.einsum('qhe,khe->hqk', queries, key_rows, precision=precise) * HEAD_DIM ** (-0.5)
    scores = low_back(scores)
    scores = jnp.where(same_doc[None], scores, -1e+30)
    attn_prob = low(jax.nn.softmax(scores, axis=-1))
    return jnp.einsum('hqk,khe->qhe', attn_prob, values, precision=precise)

def layer_row(params, row_data):
    self_qkv, self_out, cross_qkv, cross_out, norm_gain, norm_bias, ffn_in, ffn_out, slot_proj = params
    tokens, memory, lengths, slot_mask = row_data
    doc_ends = jnp.cumsum(lengths)
    position = jnp.arange(L, dtype=jnp.int32)
    segment = lax.optimization_barrier(jnp.sum((position[:, None] >= doc_ends[None, :]).astype(jnp.int32), axis=1))
    same_doc = segment[:, None] == segment[None, :]
    next_live = jnp.concatenate([segment[1:] == segment[:-1], jnp.zeros((1,), jnp.bool_)])
    split_qkv = low_back(low(jnp.einsum('td,cdf->tcf', tokens, self_qkv, precision=precise)))
    split_qkv = split_qkv.reshape(L, 3, HEADS, HEAD_DIM)
    self_mix = attend(split_qkv[:, 0], split_qkv[:, 1], split_qkv[:, 2], same_doc)
    self_mix = low_back(low(self_mix.reshape(L, D)))
    branch = low_back(jnp.dot(self_mix, self_out, precision=precise))
    after_self = norm_layer(tokens + branch, norm_gain[0], norm_bias[0])
    cross_kv = low_back(low(jnp.einsum('td,cdf->tcf', memory, cross_qkv[1:], precision=precise)))
    cross_kv = cross_kv.reshape(L, 2, HEADS, HEAD_DIM)
    cross_query = low_back(low(jnp.dot(low(after_self), cross_qkv[0], precision=precise)))
    cross_query = cross_query.reshape(L, HEADS, HEAD_DIM)
    cross_mix = attend(cross_query, cross_kv[:, 0], cross_kv[:, 1], same_doc)
    cross_mix = low_back(low(cross_mix.reshape(L, D)))
    branch = low_back(jnp.dot(cross_mix, cross_out, precision=precise))
    after_cross = norm_layer(after_self + branch, norm_gain[1], norm_bias[1])
    inner = low_back(jnp.dot(low(after_cross), ffn_in, precision=precise))
    hidden = low(jax.nn.gelu(inner))
    branch = low_back(jnp.dot(hidden, ffn_out, precision=precise))
    after_ffn = norm_layer(after_cross + branch, norm_gain[2], norm_bias[2])
    ffn_low = low(after_ffn)
    following = jnp.concatenate([ffn_low[1:], jnp.zeros((1, D), jnp.float32)], axis=0)
    following = low_back(jnp.where(next_live[:, None], following, 0.0))
    slot_value = jnp.dot(ffn_low, slot_proj[:D], precision=precise) + jnp.dot(following, slot_proj[D:], precision=precise)
    slots = slot_mask[:, None].astype(jnp.float32) * slot_value
    return (after_ffn, slots)

def reference(tokens, memory, lengths, slot_mask, self_qkv, self_out, cross_qkv, cross_out, norm_gain, norm_bias, ffn_in, ffn_out, slot_proj, out_cot, slot_cot):
    params = (self_qkv.astype(jnp.float32), self_out.astype(jnp.float32), cross_qkv.astype(jnp.float32), cross_out.astype(jnp.float32), norm_gain.astype(jnp.float32), norm_bias.astype(jnp.float32), ffn_in.astype(jnp.float32), ffn_out.astype(jnp.float32), slot_proj.astype(jnp.float32))
    tokens_wide = tokens.astype(jnp.float32)
    memory_wide = memory.astype(jnp.float32)
    checked_row = jax.checkpoint(layer_row)

    def forward(weights, token_rows, memory_rows):

        def scan_step(carried, row_data):
            return (carried, checked_row(weights, row_data))
        _, results = lax.scan(scan_step, jnp.zeros((), jnp.float32), (token_rows, memory_rows, lengths, slot_mask))
        return results
    (after_ffn, slots), pullback = jax.vjp(forward, params, tokens_wide, memory_wide)
    gradients, grad_tokens, grad_memory = pullback((out_cot.astype(jnp.float32), slot_cot.astype(jnp.float32)))
    return (after_ffn.astype(jnp.bfloat16), slots.astype(jnp.bfloat16), grad_tokens, grad_memory, gradients[0], gradients[1], gradients[2], gradients[3], gradients[4], gradients[5], gradients[6], gradients[7], gradients[8])
```

```python
import functools

import jax
import jax.numpy as jnp
from jax import lax
from jax.experimental import pallas as pl
from jax.experimental.pallas import tpu as pltpu
from jax.sharding import PartitionSpec as P

HEADS = 8
BF = jnp.bfloat16
F32 = jnp.float32
MESH = pl.DeviceIdType.MESH
NT = (((1,), (1,)), ((), ()))
TN = (((0,), (0,)), ((), ()))
BIG = 2.0**20
VMEM = 58 * 2**20
ROWS = 256
QBLOCK = 512


def dot(a, b):
    return jnp.dot(a, b, preferred_element_type=F32)


def dot_nt(a, b):
    return lax.dot_general(a, b, NT, preferred_element_type=F32)


def dot_tn(a, b):
    return lax.dot_general(a, b, TN, preferred_element_type=F32)


def at(i, size):
    return pl.ds(pl.multiple_of(i * size, size), size)


def loop(count, body, unroll=1):
    def step(i, carry):
        body(i)
        return carry

    lax.fori_loop(0, count, step, 0, unroll=unroll)


def thirds(value):
    first = value.astype(BF)
    rest = value - first.astype(F32)
    second = rest.astype(BF)
    third = (rest - second.astype(F32)).astype(BF)
    return first, second, third


def normalise(value):
    average = jnp.mean(value, axis=-1, keepdims=True)
    centred = value - average
    inverse = lax.rsqrt(jnp.mean(centred * centred, axis=-1, keepdims=True) + 1e-05)
    return centred * inverse, inverse


def norm_back(gradient, normed, inverse, gain_row):
    scaled = gradient * gain_row
    inner_mean = jnp.mean(scaled, axis=-1, keepdims=True)
    cross_mean = jnp.mean(scaled * normed, axis=-1, keepdims=True)
    return inverse * (scaled - inner_mean - normed * cross_mean)


def attend(q_s, k_s, v_s, qe_ref, ke_ref, mix_s, ext_s, kx_s, vx_s):
    row_length = k_s.shape[0]
    block = QBLOCK
    lane = lax.broadcasted_iota(jnp.int32, (row_length, 128), 1)
    wide_low = lane < 64
    lane = lax.broadcasted_iota(jnp.int32, (block, 128), 1)
    low = lane < 64
    spare = lax.rem(lane, 64)

    def pair(p):
        lanes = at(p, 128)
        for h in range(2):
            mine = wide_low if h == 0 else ~wide_low
            part = slice(h * 128, (h + 1) * 128)
            kx_s[:, part] = jnp.where(mine, k_s[:, lanes], ke_ref[...])
            vx_s[:, part] = jnp.where(mine, v_s[:, lanes], jnp.ones((), BF))
        for i in range(row_length // block):
            rows = slice(i * block, (i + 1) * block)
            scaled = q_s[rows, lanes]
            extra = qe_ref[rows, :]
            tops, sums = [], []
            for h in range(2):
                part = slice(h * 128, (h + 1) * 128)
                query = jnp.where(low if h == 0 else ~low, scaled, extra)
                scores = dot_nt(query, kx_s[:, part])
                top = jnp.max(scores, axis=1, keepdims=True)
                probs = jnp.exp(scores - top).astype(BF)
                tops.append(top)
                sums.append(dot(probs, vx_s[:, part]))
            mixed = jnp.where(low, sums[0], sums[1])
            totals = jnp.where(low, sums[1], sums[0])
            log_total = jnp.where(low, tops[1], tops[0]) + jnp.log(totals)
            first, second, third = thirds(log_total)
            ext_s[rows, lanes] = jnp.where(
                spare == 4, -first, jnp.where(spare == 5, -second, jnp.where(spare == 6, -third, extra))
            )
            mix_s[rows, lanes] = (mixed / pltpu.roll(totals, 64, 1)).astype(BF)

    loop(HEADS // 2, pair)


def attend_back(q_s, k_s, v_s, ext_s, ke_ref, mix_s, gmix_s, dq_s, dk_s, dv_s, kx_s, vx_s, qx_s, dx_s, kt_s, dqt_s, hooks):
    row_length = k_s.shape[0]
    block = QBLOCK
    lane = lax.broadcasted_iota(jnp.int32, (row_length, 128), 1)
    low = lane < 64
    spare = lax.rem(lane, 64)
    zero = jnp.zeros((), BF)

    def pair(p):
        lanes = at(p, 128)
        product = gmix_s[:, lanes].astype(F32) * mix_s[:, lanes].astype(F32)
        inner_low = jnp.sum(jnp.where(low, product, 0.0), axis=1, keepdims=True)
        inner_high = jnp.sum(jnp.where(low, 0.0, product), axis=1, keepdims=True)
        first, second, third = thirds(jnp.where(low, inner_high, inner_low))
        extra = jnp.where(spare == 0, -first, jnp.where(spare == 1, -second, jnp.where(spare == 2, -third, zero)))
        for h in range(2):
            part = slice(h * 128, (h + 1) * 128)
            mine = low if h == 0 else ~low
            keys = jnp.where(mine, k_s[:, lanes], ke_ref[...])
            kx_s[:, part] = keys
            vx_s[:, part] = jnp.where(mine, v_s[:, lanes], jnp.ones((), BF))
            qx_s[:, part] = jnp.where(mine, q_s[:, lanes], ext_s[:, lanes])
            dx_s[:, part] = jnp.where(mine, gmix_s[:, lanes], extra)
        kt_s[...] = k_s[:, lanes].T
        sum_k, sum_v = [], []
        for h in range(2):
            part = slice(h * 128, (h + 1) * 128)
            own = slice(h * 64, (h + 1) * 64)
            for j in range(row_length // block):
                cols = slice(j * block, (j + 1) * block)
                probs = jnp.exp(dot_nt(kx_s[:, part], qx_s[cols, part]))
                ds = (probs * dot_nt(vx_s[:, part], dx_s[cols, part])).astype(BF)
                dv = dot(probs.astype(BF), dx_s[cols, part])
                dk = dot(ds, qx_s[cols, part])
                acc_v, acc_k = (dv, dk) if j == 0 else (acc_v + dv, acc_k + dk)
                dqt_s[own, cols] = dot(kt_s[own, :], ds) * 0.125
            sum_k.append(acc_k)
            sum_v.append(acc_v)
        dk_s[:, lanes] = jnp.where(low, sum_k[0], sum_k[1]).astype(BF)
        dv_s[:, lanes] = jnp.where(low, sum_v[0], sum_v[1]).astype(BF)
        dq_s[:, lanes] = dqt_s[...].T.astype(BF)
        for done, hook in hooks.items():
            if done >= 0:
                pl.when(p == done)(hook)

    if -1 in hooks:
        hooks[-1]()
    loop(HEADS // 2, pair)


def whole(mine_ref, theirs_ref, row_s):
    half = mine_ref.shape[0]
    row_s[:half, :] = mine_ref[...]
    row_s[half:, :] = theirs_ref[...]


def self_fwd_kernel(
    mine, theirs, qkv_w, out_w, cq_w, gain, bias, qe, ke,
    q, k, v, mix, ext, normed, inverse, cq, row_s, kx_s, vx_s,
):
    whole(mine, theirs, row_s)
    blocks = row_s.shape[0] // ROWS

    def project(i):
        rows = at(i, ROWS)
        x = row_s[rows, :]
        q[rows, :] = (dot(x, qkv_w[0]).astype(BF) * jnp.asarray(0.125, BF))
        k[rows, :] = dot(x, qkv_w[1]).astype(BF)
        v[rows, :] = dot(x, qkv_w[2]).astype(BF)

    loop(blocks, project)
    attend(q, k, v, qe, ke, mix, ext, kx_s, vx_s)

    def after(i):
        rows = at(i, ROWS)
        n, s = normalise(row_s[rows, :].astype(F32) + dot(mix[rows, :], out_w[...]))
        normed[rows, :] = n
        inverse[rows, :] = s
        low = (n * gain[0:1, :] + bias[0:1, :]).astype(BF)
        cq[rows, :] = dot(low, cq_w[0]).astype(BF) * jnp.asarray(0.125, BF)

    loop(blocks, after)


def cross_fwd_kernel(
    mine, theirs, q, kv_w, out_w, gain, bias, normed_one, qe, ke,
    k, v, mix, ext, normed, inverse, row_s, kx_s, vx_s,
):
    whole(mine, theirs, row_s)
    blocks = row_s.shape[0] // ROWS

    def project(i):
        rows = at(i, ROWS)
        x = row_s[rows, :]
        k[rows, :] = dot(x, kv_w[1]).astype(BF)
        v[rows, :] = dot(x, kv_w[2]).astype(BF)

    loop(blocks, project)
    attend(q, k, v, qe, ke, mix, ext, kx_s, vx_s)

    def after(i):
        rows = at(i, ROWS)
        before = normed_one[rows, :] * gain[0:1, :] + bias[0:1, :]
        n, s = normalise(before + dot(mix[rows, :], out_w[...]))
        normed[rows, :] = n
        inverse[rows, :] = s

    loop(blocks, after)


def ffn_kernel(
    normed_two, inverse_two, cross_mix, in_w, out_w, slot_w, cross_out_w, gain, bias, live,
    slot_mine, slot_theirs, cot_mine, cot_theirs,
    out, slots, res_two, grad_mix, grads, sums,
    low_s, hidden_s, slope_s, normed_s, inverse_s, pair_s, next_s, slot_s, cot_s, gnext_s, res_s, ginner_s, res_two_s,
):
    row_length, width = low_s.shape
    blocks = row_length // ROWS
    units = in_w.shape[1]
    whole(slot_mine, slot_theirs, slot_s)
    whole(cot_mine, cot_theirs, cot_s)
    scale = 0.7978845608028654

    def forward(i):
        rows = at(i, ROWS)
        after_cross = normed_two[rows, :] * gain[1:2, :] + bias[1:2, :]
        low = after_cross.astype(BF)
        low_s[rows, :] = low
        branch = jnp.zeros((ROWS, width), F32)
        for c in range(units // 512):
            cols = slice(c * 512, (c + 1) * 512)
            inner = dot(low, in_w[:, cols])
            square = inner * inner
            bent = jnp.tanh(inner * (scale + (scale * 0.044715) * square))
            half = 0.5 + 0.5 * bent
            hidden = (inner * half).astype(BF)
            hidden_s[rows, cols] = hidden
            slope = half + inner * (0.5 - 0.5 * bent * bent) * (scale + (3 * scale * 0.044715) * square)
            slope_s[rows, cols] = slope.astype(BF)
            branch = branch + dot(hidden, out_w[cols, :])
        n, s = normalise(after_cross + branch)
        normed_s[rows, :] = n
        inverse_s[rows, :] = s
        final = (n * gain[2:3, :] + bias[2:3, :]).astype(BF)
        out[rows, :] = final
        pair_s[rows, :width] = final
        next_s[rows, :] = final.astype(F32)

    loop(blocks, forward)
    next_s[pl.ds(row_length, 8), :] = next_s[pl.ds(0, 8), :]

    def slot(i):
        rows = at(i, ROWS)
        alive = live[rows, 0:1].astype(F32)
        following = (next_s[pl.ds(pl.multiple_of(i * ROWS, ROWS), ROWS + 8), :][1 : ROWS + 1] * alive).astype(BF)
        pair_s[rows, width:] = following
        slots[rows, :] = dot(pair_s[rows, :], slot_w[...]).astype(BF)
        back = (dot_nt(slot_s[rows, :], slot_w[width:, :]) * alive).astype(BF)
        gnext_s[pl.ds(pl.multiple_of(i * ROWS + 8, 8), ROWS), :] = back.astype(F32)

    loop(blocks, slot)
    gnext_s[pl.ds(0, 8), :] = gnext_s[pl.ds(row_length, 8), :]
    sums[...] = jnp.zeros(sums.shape, F32)

    def backward(i):
        rows = at(i, ROWS)
        gradient = (
            cot_s[rows, :].astype(F32)
            + dot_nt(slot_s[rows, :], slot_w[:width, :])
            + gnext_s[pl.ds(pl.multiple_of(i * ROWS, ROWS), ROWS + 8), :][7 : ROWS + 7]
        )
        n = normed_s[rows, :]
        sums[0:1, :] += jnp.sum(gradient * n, axis=0, keepdims=True)
        sums[1:2, :] += jnp.sum(gradient, axis=0, keepdims=True)
        res = norm_back(gradient, n, inverse_s[rows, :], gain[2:3, :])
        res_low = res.astype(BF)
        res_s[rows, :] = res_low
        for c in range(units // 512):
            cols = slice(c * 512, (c + 1) * 512)
            ginner = (dot_nt(res_low, out_w[cols, :]) * slope_s[rows, cols].astype(F32)).astype(BF)
            ginner_s[rows, cols] = ginner
            res = res + dot_nt(ginner, in_w[:, cols])
        n = normed_two[rows, :]
        sums[2:3, :] += jnp.sum(res * n, axis=0, keepdims=True)
        sums[3:4, :] += jnp.sum(res, axis=0, keepdims=True)
        res = norm_back(res, n, inverse_two[rows, :], gain[1:2, :])
        res_two[rows, :] = res
        res_low = res.astype(BF)
        res_two_s[rows, :] = res_low
        grad_mix[rows, :] = dot_nt(res_low, cross_out_w[...]).astype(BF)

    loop(blocks, backward)
    half_units = units // 2
    base_out = width * half_units // 512
    base_slot = base_out + half_units
    base_cross = base_slot + width

    for c in range(units // 512):
        def tile(r, c=c):
            half, block = divmod(c, units // 1024)
            grads[half, pl.ds(block * width + r * 256, 256), :] = dot_tn(
                low_s[:, at(r, 256)], ginner_s[:, c * 512 : (c + 1) * 512]
            ).astype(BF)

        loop(width // 256, tile)

    for half in range(2):
        def tile_out(r, half=half):
            grads[half, pl.ds(base_out + r * 256, 256), :] = dot_tn(
                hidden_s[:, at(half * (half_units // 256) + r, 256)], res_s[...]
            ).astype(BF)

        loop(half_units // 256, tile_out)

        def tile_slot(r, half=half):
            grads[half, pl.ds(base_slot + r * 256, 256), :] = dot_tn(
                pair_s[:, at(half * (width // 256) + r, 256)], slot_s[...]
            ).astype(BF)

        loop(width // 256, tile_slot)
        grads[half, pl.ds(base_cross, width // 2), :] = dot_tn(
            cross_mix[:, half * 256 : (half + 1) * 256], res_two_s[...]
        ).astype(BF)
    rest = grads.shape[1] - base_cross - width // 2
    if rest:
        grads[:, base_cross + width // 2 :, :] = jnp.zeros((2, rest, 512), BF)


def cross_bwd_kernel(
    q, k, v, ext, ke, mix, gmix, mine, theirs, qkv_w, res_two, normed_one, inverse_one, gain, bias, self_mix, self_out_w,
    grad_mem, res_one, grad_self_mix, grads, sums,
    row_s, low_s, dq_s, dk_s, dv_s, res_s, kx_s, vx_s, qx_s, dx_s, kt_s, dqt_s, hooks={},
):
    row_length, width = row_s.shape
    blocks = row_length // ROWS
    whole(mine, theirs, row_s)
    attend_back(q, k, v, ext, ke, mix, gmix, dq_s, dk_s, dv_s, kx_s, vx_s, qx_s, dx_s, kt_s, dqt_s, hooks)
    sums[...] = jnp.zeros(sums.shape, F32)

    def backward(i):
        rows = at(i, ROWS)
        grad_mem[rows, :] = dot_nt(dk_s[rows, :], qkv_w[1]) + dot_nt(dv_s[rows, :], qkv_w[2])
        n = normed_one[rows, :]
        low_s[rows, :] = (n * gain[0:1, :] + bias[0:1, :]).astype(BF)
        gradient = res_two[rows, :] + dot_nt(dq_s[rows, :], qkv_w[0])
        sums[0:1, :] += jnp.sum(gradient * n, axis=0, keepdims=True)
        sums[1:2, :] += jnp.sum(gradient, axis=0, keepdims=True)
        res = norm_back(gradient, n, inverse_one[rows, :], gain[0:1, :])
        res_one[rows, :] = res
        res_low = res.astype(BF)
        res_s[rows, :] = res_low
        grad_self_mix[rows, :] = dot_nt(res_low, self_out_w[...]).astype(BF)

    loop(blocks, backward)

    def tile(r):
        cols = at(r, 256)
        store_qkv(grads, r, dot_tn(low_s[:, cols], dq_s[...]), 0)
        store_qkv(grads, r, dot_tn(row_s[:, cols], dk_s[...]), 1)
        store_qkv(grads, r, dot_tn(row_s[:, cols], dv_s[...]), 2)

    loop(width // 256, tile)
    for half in range(2):
        block = dot_tn(self_mix[:, half * 256 : (half + 1) * 256], res_s[...]).astype(BF)
        for c in range(2):
            grads[half, 3 * width + c * 256 : 3 * width + (c + 1) * 256, :] = block[:, c * 256 : (c + 1) * 256]
    rest = grads.shape[1] - 4 * width
    if rest:
        grads[:, 4 * width :, :] = jnp.zeros((2, rest, 256), BF)


def store_qkv(grads, r, block, part):
    block = block.astype(BF)
    for half in range(2):
        grads[half, pl.ds(part * 512 + r * 256, 256), :] = block[:, half * 256 : (half + 1) * 256]


def self_bwd_kernel(
    q, k, v, ext, ke, mix, gmix, mine, theirs, qkv_w, res_one, sums_one, sums_two,
    grad_row, grads,
    row_s, dq_s, dk_s, dv_s, kx_s, vx_s, qx_s, dx_s, kt_s, dqt_s, hooks={},
):
    row_length, width = row_s.shape
    whole(mine, theirs, row_s)
    attend_back(q, k, v, ext, ke, mix, gmix, dq_s, dk_s, dv_s, kx_s, vx_s, qx_s, dx_s, kt_s, dqt_s, hooks)

    def backward(i):
        rows = at(i, ROWS)
        grad_row[rows, :] = (
            res_one[rows, :] + dot_nt(dq_s[rows, :], qkv_w[0]) + dot_nt(dk_s[rows, :], qkv_w[1])
            + dot_nt(dv_s[rows, :], qkv_w[2])
        )

    loop(row_length // ROWS, backward)

    def tile(r):
        cols = at(r, 256)
        for part, d in enumerate((dq_s, dk_s, dv_s)):
            store_qkv(grads, r, dot_tn(row_s[:, cols], d[...]), part)

    loop(width // 256, tile)
    norms = jnp.concatenate(
        [sums_one[0:1, :], sums_two[2:3, :], sums_two[0:1, :], sums_one[1:2, :], sums_two[3:4, :], sums_two[1:2, :],
         jnp.zeros((10, width), F32)], axis=0
    ).astype(BF)
    for half in range(2):
        grads[half, 3 * width : 3 * width + 16, :] = norms[:, half * 256 : (half + 1) * 256]
    rest = grads.shape[1] - 3 * width - 16
    if rest:
        grads[:, 3 * width + 16 :, :] = jnp.zeros((2, rest, 256), BF)


def kernel_call(kernel, name, args, outs, scratch, flops):
    return pl.pallas_call(
        kernel,
        out_shape=[jax.ShapeDtypeStruct(shape, kind) for shape, kind in outs],
        in_specs=[pl.BlockSpec(memory_space=pltpu.VMEM)] * len(args),
        out_specs=[pl.BlockSpec(memory_space=pltpu.VMEM)] * len(outs),
        scratch_shapes=[pltpu.VMEM(shape, kind) for shape, kind in scratch],
        compiler_params=pltpu.CompilerParams(vmem_limit_bytes=VMEM),
        cost_estimate=pl.CostEstimate(flops=flops, bytes_accessed=2**20, transcendentals=0),
        name=name,
    )(*args)


class Place:
    def __init__(self, deep):
        dp = lax.axis_index("dp")
        self.deep = deep
        self.h = lax.axis_index("head")
        self.core = lax.rem(dp, 2)
        self.y = lax.rem(lax.div(dp, 2), 2)
        self.z = lax.div(dp, 4)

    def device(self, dh=0, dcore=0, dy=0, dz=0):
        h = 1 - self.h if dh else self.h
        core = 1 - self.core if dcore else self.core
        y = 1 - self.y if dy else self.y
        z = lax.rem(self.z + dz, self.deep) if dz else self.z
        return ((z * 2 + y) * 2 + core, h)

    def peers(self):
        plane = [self.device(dh=1), self.device(dy=1), self.device(dh=1, dy=1)]
        return [self.device(dcore=1)] + plane + [self.device(dz=j) for j in range(1, self.deep)]

    def greet(self):
        barrier = pltpu.get_barrier_semaphore()
        for peer in self.peers():
            pl.semaphore_signal(barrier, inc=1, device_id=peer, device_id_type=MESH)

    def met(self):
        pl.semaphore_wait(pltpu.get_barrier_semaphore(), len(self.peers()))


def remote(src, dst, send, recv, device):
    return pltpu.make_async_remote_copy(
        src_ref=src, dst_ref=dst, send_sem=send, recv_sem=recv, device_id=device, device_id_type=MESH
    )


class Gather:
    SEMS = 9

    def __init__(self, place, src, own, came, parts, total, sem):
        self.place, self.src, self.own, self.came, self.parts, self.total, self.sem = place, src, own, came, parts, total, sem

    @staticmethod
    def scratch(deep, rows, width):
        return [
            pltpu.VMEM((2, 2, deep, rows, width), BF), pltpu.VMEM((2, 2, deep, rows, width), BF),
            pltpu.VMEM((3, deep, rows, width), BF), pltpu.VMEM((deep, rows, width), BF),
            pltpu.SemaphoreType.DMA((Gather.SEMS,)),
        ]

    def load(self):
        return pltpu.make_async_copy(self.src.at[:, self.place.core], self.own, self.sem.at[0])

    def cross(self):
        return remote(self.src.at[:, 1 - self.place.core], self.came, self.sem.at[1], self.sem.at[2], self.place.device(dcore=1))

    def plane(self):
        p = self.place
        copies = []
        for j, (dh, dy) in enumerate(((1, 0), (0, 1), (1, 1))):
            part = self.own.at[1 - p.h if dh else p.h, 1 - p.y if dy else p.y]
            copies.append(remote(part, self.parts.at[j], self.sem.at[3 + j], self.sem.at[6 + j], p.device(dh=dh, dy=dy)))
        return copies

    def begin(self):
        self.load().start()
        self.cross().start()

    def middle(self):
        self.load().wait()
        self.cross().wait()
        deep = self.place.deep

        def add(i):
            hh, yy, zz = lax.div(i, 2 * deep), lax.rem(lax.div(i, deep), 2), lax.rem(i, deep)
            self.own[hh, yy, zz] = (self.own[hh, yy, zz].astype(F32) + self.came[hh, yy, zz].astype(F32)).astype(BF)

        loop(4 * deep, add)
        for copy in self.plane():
            copy.start()

    def finish(self):
        copies = self.plane()
        for copy in copies:
            copy.wait_recv()
        p = self.place

        def add(i):
            value = self.own[p.h, p.y, i].astype(F32)
            for j in range(3):
                value = value + self.parts[j, i].astype(F32)
            self.total[i] = value.astype(BF)

        loop(p.deep, add)
        for copy in copies:
            copy.wait_send()


class Column:
    def __init__(self, place, total, came, held, sem):
        self.place, self.total, self.came, self.held, self.sem = place, total, came, held, sem

    @staticmethod
    def scratch(deep, rows, width):
        return [
            pltpu.VMEM((max(deep - 1, 1), rows, width), BF), pltpu.VMEM((deep, rows, width), BF),
            pltpu.SemaphoreType.DMA((4 * deep,)),
        ]

    def split(self):
        p, n = self.place, self.place.deep
        return [
            remote(self.total.at[lax.rem(p.z + j, n)], self.came.at[j - 1], self.sem.at[j], self.sem.at[n + j], p.device(dz=j))
            for j in range(1, n)
        ]

    def spread(self):
        p, n = self.place, self.place.deep
        return [
            remote(self.held.at[p.z], self.held.at[p.z], self.sem.at[2 * n + j], self.sem.at[3 * n + j], p.device(dz=j))
            for j in range(1, n)
        ]

    def begin(self):
        for copy in self.split():
            copy.start()

    def middle(self):
        for copy in self.split():
            copy.wait_recv()
        p = self.place
        value = self.total[p.z].astype(F32)
        for j in range(p.deep - 1):
            value = value + self.came[j].astype(F32)
        self.held[p.z] = value.astype(BF)
        for copy in self.spread():
            copy.start()

    def finish(self):
        for copy in self.spread():
            copy.wait_recv()
        for copy in self.split() + self.spread():
            copy.wait_send()


class Spread:
    SEMS = 5

    def __init__(self, place, held, out, sem):
        self.place, self.held, self.out, self.sem = place, held, out, sem

    @staticmethod
    def scratch():
        return [pltpu.SemaphoreType.DMA((Spread.SEMS,))]

    def keep(self):
        return pltpu.make_async_copy(self.held, self.out.at[self.place.core, self.place.y], self.sem.at[0])

    def along(self):
        p = self.place
        return remote(self.held, self.out.at[p.core, p.y], self.sem.at[1], self.sem.at[2], p.device(dy=1))

    def cross(self):
        p = self.place
        return remote(self.out.at[p.core], self.out.at[p.core], self.sem.at[3], self.sem.at[4], p.device(dcore=1))

    def begin(self):
        self.keep().start()
        self.along().start()

    def middle(self):
        self.keep().wait()
        self.along().wait()
        self.cross().start()

    def finish(self):
        self.cross().wait()


def cross_bwd_hosting(deep, *refs):
    early, refs = refs[0], refs[1:]
    refs, gather = refs[:-5], refs[-5:]
    inputs, outputs, scratch = refs[:17], refs[17:22], refs[23:]
    place = Place(deep)
    work = Gather(place, early, *gather[:3], refs[22], gather[4])
    place.greet()

    def before():
        place.met()
        work.begin()

    cross_bwd_kernel(*inputs, *outputs, *scratch, hooks={-1: before, 0: work.middle})
    work.finish()


def self_bwd_hosting(deep, *refs):
    total, late = refs[0], refs[1]
    inputs, (grad_row, grads, held, second) = refs[2:15], refs[15:19]
    scratch = refs[19:29]
    column_came, column_sem = refs[29:31]
    gather = refs[31:]
    place = Place(deep)
    column = Column(place, total, column_came, held, column_sem)
    work = Gather(place, late, *gather[:3], second, gather[3])
    place.greet()

    def before():
        place.met()
        work.begin()
        column.begin()

    def after_two():
        column.middle()

    self_bwd_kernel(*inputs, grad_row, grads, *scratch, hooks={-1: before, 0: work.middle, 2: after_two})
    column.finish()
    work.finish()


def tail_kernel(deep, held_c, total_d, src_e, out_c, out_d, out_e, came_d, held_d, sem_d, *refs):
    gather, refs = refs[:5], refs[5:]
    came_e, held_e, sem_e = refs[:3]
    place = Place(deep)
    spread_c = Spread(place, held_c, out_c, refs[3])
    spread_d = Spread(place, held_d, out_d, refs[4])
    spread_e = Spread(place, held_e, out_e, refs[5])
    column_d = Column(place, total_d, came_d, held_d, sem_d)
    gather_e = Gather(place, src_e, *gather)
    column_e = Column(place, gather[3], came_e, held_e, sem_e)
    place.greet()
    place.met()
    gather_e.begin()
    column_d.begin()
    spread_c.begin()
    gather_e.middle()
    column_d.middle()
    gather_e.finish()
    column_e.begin()
    column_d.finish()
    spread_d.begin()
    column_e.middle()
    spread_c.middle()
    column_e.finish()
    spread_e.begin()
    spread_d.middle()
    spread_e.middle()
    spread_c.finish()
    spread_d.finish()
    spread_e.finish()


ANY = pl.BlockSpec(memory_space=pl.ANY)
INNER = pl.BlockSpec(memory_space=pltpu.VMEM)


def remote_call(kernel, name, cid, args, in_specs, outs, out_specs, scratch, flops=0):
    return pl.pallas_call(
        kernel,
        out_shape=[jax.ShapeDtypeStruct(shape, kind) for shape, kind in outs],
        in_specs=in_specs,
        out_specs=out_specs,
        scratch_shapes=scratch,
        compiler_params=pltpu.CompilerParams(collective_id=cid, has_side_effects=True, vmem_limit_bytes=VMEM),
        cost_estimate=pl.CostEstimate(flops=flops, bytes_accessed=2**20, transcendentals=0),
        name=name,
    )(*args)


def swap(value):
    return lax.ppermute(value, "head", [(0, 1), (1, 0)])


def padded(count, unit):
    return -(-count // unit) * unit


def per_device(
    tokens, memory, lengths, slot_mask, self_qkv, self_out, cross_qkv, cross_out,
    norm_gain, norm_bias, ffn_in, ffn_out, slot_proj, out_cot, slot_cot,
):
    local_len, width = tokens.shape[1:]
    units = ffn_in.shape[1]
    h = lax.axis_index("head")
    deep = lax.axis_size("dp") // 4
    row_length = 2 * local_len

    def halves(value):
        mine = lax.dynamic_index_in_dim(value, h, 0, keepdims=False)
        theirs = lax.dynamic_index_in_dim(value, 1 - h, 0, keepdims=False)
        return mine, swap(theirs)

    live = slot_mask.astype(BF)[:, :, None]
    token_halves = halves(tokens)
    memory_halves = halves(memory)
    slot_halves = halves(slot_cot * live)
    cot_halves = halves(out_cot)

    place = jnp.arange(row_length, dtype=jnp.int32)
    place = jnp.where(h == 0, place, lax.rem(place + local_len, row_length))
    doc_ends = jnp.cumsum(lax.dynamic_index_in_dim(lengths, h, 0, keepdims=False))
    segment = jnp.sum((place[:, None] >= doc_ends[None, :]).astype(jnp.int32), axis=1)
    next_segment = jnp.sum((place[:, None] + 1 >= doc_ends[None, :]).astype(jnp.int32), axis=1)
    next_live = (place + 1 < row_length) & (segment == next_segment)
    spare = jnp.arange(128) % 64
    hit = segment[:, None] == spare[None, :]
    coded = spare[None, :] < 4
    query_extra = jnp.where(hit & coded, BIG, 0.0).astype(BF)
    key_extra = jnp.where(coded, jnp.where(hit, 0.0, -BIG), jnp.where(spare[None, :] < 7, 1.0, 0.0)).astype(BF)
    next_live = jnp.broadcast_to(next_live[:, None], (row_length, 128)).astype(BF)

    row, wide, column = ((row_length, width), BF), ((row_length, width), F32), ((row_length, 1), F32)
    two = ((row_length, 256), BF)
    unit = 64 * deep
    rows_c = padded(width * units // 1024 + units // 2 + width + width // 2, unit)
    rows_d = padded(4 * width, unit)
    rows_e = padded(3 * width + 16, unit)
    dense = 2 * row_length * width * width
    scores = 2 * row_length * row_length * width

    q, k, v, mix, ext, normed_one, inverse_one, cq = kernel_call(
        self_fwd_kernel, "self_fwd",
        (*token_halves, self_qkv, self_out, cross_qkv, norm_gain, norm_bias, query_extra, key_extra),
        [row] * 5 + [wide, column, row], [row, two, two], 5 * dense + 8 * scores,
    )
    ck, cv, cmix, cext, normed_two, inverse_two = kernel_call(
        cross_fwd_kernel, "cross_fwd",
        (*memory_halves, cq, cross_qkv, cross_out, norm_gain, norm_bias, normed_one, query_extra, key_extra),
        [row] * 4 + [wide, column], [row, two, two], 3 * dense + 8 * scores,
    )
    tall = ((row_length, units), BF)
    ring = ((row_length + 8, width), F32)
    out_row, slots_row, res_two, grad_cmix, grads_c, sums_two = kernel_call(
        ffn_kernel, "ffn",
        (normed_two, inverse_two, cmix, ffn_in, ffn_out, slot_proj, cross_out, norm_gain, norm_bias, next_live,
         *slot_halves, *cot_halves),
        [row, row, wide, row, ((2, rows_c, 512), BF), ((8, width), F32)],
        [row, tall, tall, wide, column, ((row_length, 2 * width), BF), ring, row, row, ring, row, tall, row], 32 * dense,
    )
    back = [pltpu.VMEM((row_length, 256), BF)] * 4 + [pltpu.VMEM((128, row_length), BF), pltpu.VMEM((128, row_length), F32)]
    row_s = pltpu.VMEM((row_length, width), BF)

    def shards(grads):
        return grads.reshape(2, 2, 2, deep, -1, grads.shape[-1])

    def shard(rows, lanes):
        return deep, rows // (4 * deep), lanes

    gather_c = Gather.scratch(*shard(rows_c, 512))
    grad_mem, res_one, grad_smix, grads_d, sums_one, total_c = remote_call(
        functools.partial(cross_bwd_hosting, deep), "cross_bwd", 0,
        (shards(grads_c), cq, ck, cv, cext, key_extra, cmix, grad_cmix, *memory_halves, cross_qkv, res_two, normed_one, inverse_one,
         norm_gain, norm_bias, mix, self_out),
        [ANY] + [INNER] * 17,
        [wide, wide, row, ((2, rows_d, 256), BF), ((8, width), F32), (shard(rows_c, 512), BF)],
        [INNER] * 6,
        [row_s] * 6 + back + gather_c, 12 * dense + 20 * scores,
    )
    gather_d = Gather.scratch(*shard(rows_d, 256))
    column_c = Column.scratch(*shard(rows_c, 512))
    grad_row, grads_e, held_c, total_d = remote_call(
        functools.partial(self_bwd_hosting, deep), "self_bwd", 1,
        (total_c, shards(grads_d), q, k, v, ext, key_extra, mix, grad_smix, *token_halves, self_qkv, res_one, sums_one, sums_two),
        [INNER, ANY] + [INNER] * 13,
        [wide, ((2, rows_e, 256), BF), (shard(rows_c, 512), BF), (shard(rows_d, 256), BF)],
        [INNER] * 4,
        [row_s] * 4 + back + [column_c[0], column_c[2]] + gather_d[:3] + gather_d[4:], 10 * dense + 20 * scores,
    )

    def results(rows, lanes):
        return (2, 2) + shard(rows, lanes), BF

    out_c, out_d, out_e = remote_call(
        functools.partial(tail_kernel, deep), "tail", 2,
        (held_c, total_d, shards(grads_e)),
        [INNER, INNER, ANY],
        [results(rows_c, 512), results(rows_d, 256), results(rows_e, 256)],
        [ANY] * 3,
        Column.scratch(*shard(rows_d, 256)) + Gather.scratch(*shard(rows_e, 256)) + Column.scratch(*shard(rows_e, 256))
        + Spread.scratch() * 3,
    )

    def home(value, kind):
        theirs = swap(value[local_len:].astype(BF)).astype(kind)
        mine = value[:local_len]
        return jnp.stack([jnp.where(h == 0, mine, theirs), jnp.where(h == 0, theirs, mine)], axis=0)

    out = home(out_row, BF)
    slots = home(slots_row, BF) * live
    grad_tokens = home(grad_row, F32)
    grad_memory = home(grad_mem, F32)

    c = out_c.reshape(rows_c, 512).astype(F32)
    d = out_d.reshape(rows_d, 256).astype(F32)
    e = out_e.reshape(rows_e, 256).astype(F32)
    half = units // 2
    base = width * half // 512
    return (
        out, slots, grad_tokens, grad_memory,
        e[: 3 * width].reshape(3, width, 256),
        jnp.concatenate([d[3 * width : 3 * width + 256], d[3 * width + 256 : 4 * width]], axis=1),
        d[: 3 * width].reshape(3, width, 256),
        c[base + half + width : base + half + width + width // 2],
        e[3 * width : 3 * width + 3],
        e[3 * width + 3 : 3 * width + 6],
        jnp.concatenate([c[i * width : (i + 1) * width] for i in range(half // 512)], axis=1),
        c[base : base + half],
        c[base + half : base + half + width],
    )


def solution(mesh):
    split = P("dp", "head", None)
    placed = (split, split, P("dp", None), P("dp", "head")) + (P(),) * 9 + (split, split)
    return jax.shard_map(
        per_device,
        mesh=mesh,
        in_specs=placed,
        out_specs=(
            split, split, split, split,
            P(None, None, "head"), P("head", None), P(None, None, "head"), P("head", None),
            P(None, "head"), P(None, "head"), P(None, "head"), P("head", None), P("head", None),
        ),
        check_vma=False,
    )
```

```python
import functools

import jax
import jax.numpy as jnp
from jax import lax
from jax.experimental import pallas as pl
from jax.experimental.pallas import tpu as pltpu
from jax.sharding import PartitionSpec as P

HEADS = 8
BF = jnp.bfloat16
F32 = jnp.float32
MESH = pl.DeviceIdType.MESH
NT = (((1,), (1,)), ((), ()))
TN = (((0,), (0,)), ((), ()))
BIG = 2.0**20
VMEM = 58 * 2**20
ROWS = 256
QBLOCK = 512
ANY = pl.BlockSpec(memory_space=pl.ANY)
INNER = pl.BlockSpec(memory_space=pltpu.VMEM)
SCALARS = pl.BlockSpec(memory_space=pltpu.SMEM)


def dot(a, b):
    return jnp.dot(a, b, preferred_element_type=F32)


def dot_nt(a, b):
    return lax.dot_general(a, b, NT, preferred_element_type=F32)


def dot_tn(a, b):
    return lax.dot_general(a, b, TN, preferred_element_type=F32)


def at(i, size):
    return pl.ds(pl.multiple_of(i * size, size), size)


def loop(count, body, first=0):
    def step(i, carry):
        body(i)
        return carry

    lax.fori_loop(first, count, step, 0)


def thirds(value):
    first = value.astype(BF)
    rest = value - first.astype(F32)
    second = rest.astype(BF)
    third = (rest - second.astype(F32)).astype(BF)
    return first, second, third


def normalise(value):
    average = jnp.mean(value, axis=-1, keepdims=True)
    centred = value - average
    inverse = lax.rsqrt(jnp.mean(centred * centred, axis=-1, keepdims=True) + 1e-05)
    return centred * inverse, inverse


def norm_back(gradient, normed, inverse, gain_row):
    scaled = gradient * gain_row
    inner_mean = jnp.mean(scaled, axis=-1, keepdims=True)
    cross_mean = jnp.mean(scaled * normed, axis=-1, keepdims=True)
    return inverse * (scaled - inner_mean - normed * cross_mean)


def run_hooks(hooks, step):
    for done, hook in hooks.items():
        if done >= 0:
            pl.when(step == done)(hook)


def attend(q_s, k_s, v_s, qe_ref, ke_ref, mix_s, ext_s, kx_s, vx_s, hooks):
    row_length = k_s.shape[0]
    block = QBLOCK
    lane = lax.broadcasted_iota(jnp.int32, (row_length, 128), 1)
    wide_low = lane < 64
    lane = lax.broadcasted_iota(jnp.int32, (block, 128), 1)
    low = lane < 64
    spare = lax.rem(lane, 64)

    def pair(p):
        lanes = at(p, 128)
        for h in range(2):
            mine = wide_low if h == 0 else ~wide_low
            part = slice(h * 128, (h + 1) * 128)
            kx_s[:, part] = jnp.where(mine, k_s[:, lanes], ke_ref[...])
            vx_s[:, part] = jnp.where(mine, v_s[:, lanes], jnp.ones((), BF))
        for i in range(row_length // block):
            rows = slice(i * block, (i + 1) * block)
            scaled = q_s[rows, lanes]
            extra = qe_ref[rows, :]
            tops, sums = [], []
            for h in range(2):
                part = slice(h * 128, (h + 1) * 128)
                query = jnp.where(low if h == 0 else ~low, scaled, extra)
                scores = dot_nt(query, kx_s[:, part])
                top = jnp.max(scores, axis=1, keepdims=True)
                probs = jnp.exp(scores - top).astype(BF)
                tops.append(top)
                sums.append(dot(probs, vx_s[:, part]))
            mixed = jnp.where(low, sums[0], sums[1])
            totals = jnp.where(low, sums[1], sums[0])
            log_total = jnp.where(low, tops[1], tops[0]) + jnp.log(totals)
            first, second, third = thirds(log_total)
            ext_s[rows, lanes] = jnp.where(
                spare == 4, -first, jnp.where(spare == 5, -second, jnp.where(spare == 6, -third, extra))
            )
            mix_s[rows, lanes] = (mixed / pltpu.roll(totals, 64, 1)).astype(BF)
        run_hooks(hooks, p)

    loop(HEADS // 2, pair)


def head_pair(i):
    return lax.rem(i, 2) * 2 + lax.div(i, 2)


def attend_back(q_s, k_s, v_s, ext_s, ke_ref, mix_s, gmix_s, dq_s, dk_s, dv_s, kx_s, vx_s, qx_s, dx_s, kt_s, dqt_s, hooks):
    row_length = k_s.shape[0]
    block = QBLOCK
    lane = lax.broadcasted_iota(jnp.int32, (row_length, 128), 1)
    low = lane < 64
    spare = lax.rem(lane, 64)
    zero = jnp.zeros((), BF)

    def pair(i):
        lanes = at(head_pair(i), 128)
        product = gmix_s[:, lanes].astype(F32) * mix_s[:, lanes].astype(F32)
        inner_low = jnp.sum(jnp.where(low, product, 0.0), axis=1, keepdims=True)
        inner_high = jnp.sum(jnp.where(low, 0.0, product), axis=1, keepdims=True)
        first, second, third = thirds(jnp.where(low, inner_high, inner_low))
        extra = jnp.where(spare == 0, -first, jnp.where(spare == 1, -second, jnp.where(spare == 2, -third, zero)))
        kt_s[...] = k_s[:, lanes].T
        sum_k, sum_v = [], []
        for h in range(2):
            part = slice(h * 128, (h + 1) * 128)
            mine = low if h == 0 else ~low
            kx_s[:, part] = jnp.where(mine, k_s[:, lanes], ke_ref[...])
            vx_s[:, part] = jnp.where(mine, v_s[:, lanes], jnp.ones((), BF))
            qx_s[:, part] = jnp.where(mine, q_s[:, lanes], ext_s[:, lanes])
            dx_s[:, part] = jnp.where(mine, gmix_s[:, lanes], extra)
        for h in range(2):
            part = slice(h * 128, (h + 1) * 128)
            own = slice(h * 64, (h + 1) * 64)
            for j in range(row_length // block):
                cols = slice(j * block, (j + 1) * block)
                probs = jnp.exp(dot_nt(kx_s[:, part], qx_s[cols, part]))
                ds = (probs * dot_nt(vx_s[:, part], dx_s[cols, part])).astype(BF)
                dv = dot(probs.astype(BF), dx_s[cols, part])
                dk = dot(ds, qx_s[cols, part])
                acc_v, acc_k = (dv, dk) if j == 0 else (acc_v + dv, acc_k + dk)
                dqt_s[own, cols] = dot(kt_s[own, :], ds) * 0.125
            sum_k.append(acc_k)
            sum_v.append(acc_v)
            if h == 0:
                run_hooks(hooks, 2 * i)
        dk_s[:, lanes] = jnp.where(low, sum_k[0], sum_k[1]).astype(BF)
        dv_s[:, lanes] = jnp.where(low, sum_v[0], sum_v[1]).astype(BF)
        dq_s[:, lanes] = dqt_s[...].T.astype(BF)
        run_hooks(hooks, 2 * i + 1)

    loop(HEADS // 2, pair)


class Place:
    def __init__(self, deep):
        dp = lax.axis_index("dp")
        self.deep = deep
        self.h = lax.axis_index("head")
        self.core = lax.rem(dp, 2)
        self.y = lax.rem(lax.div(dp, 2), 2)
        self.z = lax.div(dp, 4)

    def device(self, dh=0, dcore=0, dy=0, dz=0):
        h = 1 - self.h if dh else self.h
        core = 1 - self.core if dcore else self.core
        y = 1 - self.y if dy else self.y
        z = lax.rem(self.z + dz, self.deep) if dz else self.z
        return ((z * 2 + y) * 2 + core, h)

    def greet(self, *kinds):
        self.peers = []
        for kind in kinds:
            steps = range(1, self.deep) if kind == "dz" else (1,)
            self.peers += [self.device(**{kind: j}) for j in steps]
        barrier = pltpu.get_barrier_semaphore()
        for peer in self.peers:
            pl.semaphore_signal(barrier, inc=1, device_id=peer, device_id_type=MESH)

    def met(self):
        pl.semaphore_wait(pltpu.get_barrier_semaphore(), len(self.peers))


def remote(src, dst, send, recv, device):
    return pltpu.make_async_remote_copy(
        src_ref=src, dst_ref=dst, send_sem=send, recv_sem=recv, device_id=device, device_id_type=MESH
    )


DMA = pltpu.SemaphoreType.DMA


class CoreSum:
    def __init__(self, place, src, own, came, sem):
        self.place, self.src, self.own, self.came, self.sem = place, src, own, came, sem

    @staticmethod
    def scratch(rows, width):
        return [pltpu.VMEM((2, rows // 2, width), BF), DMA((2,))]

    def cross(self):
        size = self.src.shape[1] // 2
        return remote(
            self.src.at[:, at(1 - self.place.core, size)], self.came, self.sem.at[0], self.sem.at[1], self.place.device(dcore=1)
        )

    def begin(self):
        self.cross().start()

    def finish(self):
        self.cross().wait()
        size = self.own.shape[2]
        tile = size // self.place.deep

        def add(i):
            hh, rest = lax.div(i, 2 * self.place.deep), lax.rem(i, 2 * self.place.deep)
            yy, zz = lax.div(rest, self.place.deep), lax.rem(rest, self.place.deep)
            here = self.src[hh, at(self.place.core * 2 * self.place.deep + rest, tile), :].astype(F32)
            self.own[hh, yy, at(zz, tile), :] = (here + self.came[hh, at(rest, tile), :].astype(F32)).astype(BF)

        loop(4 * self.place.deep, add)


class Plane:
    def __init__(self, place, own, kept, came_a, came_b, total, sem, x_first):
        self.place, self.own, self.kept, self.came_a, self.came_b = place, own, kept, came_a, came_b
        self.total, self.sem, self.x_first = total, sem, x_first

    @staticmethod
    def scratch(rows, width):
        block = rows // 4
        return [pltpu.VMEM((2, block, width), BF)] * 2 + [pltpu.VMEM((block, width), BF)] * 2 + [DMA((5,))]

    def load(self):
        p = self.place
        part = self.own.at[p.h] if self.x_first else self.own.at[:, p.y]
        return pltpu.make_async_copy(part, self.kept, self.sem.at[0])

    def hop_a(self):
        p = self.place
        if self.x_first:
            part, device = self.own.at[1 - p.h], p.device(dh=1)
        else:
            part, device = self.own.at[:, 1 - p.y], p.device(dy=1)
        return remote(part, self.came_a, self.sem.at[1], self.sem.at[2], device)

    def hop_b(self):
        p = self.place
        if self.x_first:
            part, device = self.kept.at[1 - p.y], p.device(dy=1)
        else:
            part, device = self.kept.at[1 - p.h], p.device(dh=1)
        return remote(part, self.came_b, self.sem.at[3], self.sem.at[4], device)

    def begin(self):
        self.hop_a().start()
        self.load().start()

    def middle(self):
        self.load().wait()
        self.hop_a().wait()
        deep = self.place.deep
        tile = self.kept.shape[1] // deep

        def add(i):
            side, rows = lax.div(i, deep), at(lax.rem(i, deep), tile)
            self.kept[side, rows, :] = (self.kept[side, rows, :].astype(F32) + self.came_a[side, rows, :].astype(F32)).astype(BF)

        loop(2 * deep, add)
        self.hop_b().start()

    def finish(self):
        self.hop_b().wait()
        p = self.place
        side = p.y if self.x_first else p.h
        tile = self.kept.shape[1] // p.deep

        def add(i):
            rows = at(i, tile)
            self.total[rows, :] = (self.kept[side, rows, :].astype(F32) + self.came_b[rows, :].astype(F32)).astype(BF)

        loop(p.deep, add)


class Split:
    def __init__(self, place, total, came, share, sem):
        self.place, self.total, self.came, self.share, self.sem = place, total, came, share, sem

    @staticmethod
    def scratch(deep, rows, width):
        return [pltpu.VMEM((max(deep - 1, 1), rows // (4 * deep), width), BF), DMA((2 * deep,))]

    def copies(self):
        p, n = self.place, self.place.deep
        tile = self.share.shape[0]
        return [
            remote(
                self.total.at[at(lax.rem(p.z + j, n), tile)], self.came.at[j - 1], self.sem.at[j], self.sem.at[n + j], p.device(dz=j)
            )
            for j in range(1, n)
        ]

    def begin(self):
        for copy in self.copies():
            copy.start()

    def finish(self):
        copies = self.copies()
        for copy in copies:
            copy.wait()
        p = self.place
        value = self.total[at(p.z, self.share.shape[0]), :].astype(F32)
        for j in range(p.deep - 1):
            value = value + self.came[j].astype(F32)
        self.share[...] = value.astype(BF)


class Spread:
    def __init__(self, place, share, held, out, sem):
        self.place, self.share, self.held, self.out, self.sem = place, share, held, out, sem

    @staticmethod
    def scratch(deep, rows, width):
        return [pltpu.VMEM((rows // 4, width), BF), DMA((2 * deep + 6,))]

    def copies(self):
        p, n = self.place, self.place.deep
        slot = self.held.at[at(p.z, self.share.shape[0])]
        return [remote(self.share, slot, self.sem.at[j], self.sem.at[n + j], p.device(dz=j)) for j in range(1, n)]

    def mine(self):
        slot = self.held.at[at(self.place.z, self.share.shape[0])]
        return pltpu.make_async_copy(self.share, slot, self.sem.at[2 * self.place.deep])

    def keep(self):
        p = self.place
        return pltpu.make_async_copy(self.held, self.quarter(), self.sem.at[2 * p.deep + 1])

    def quarter(self):
        p = self.place
        return self.out.at[at(p.core * 2 + p.y, self.held.shape[0])]

    def along(self):
        p, n = self.place, 2 * self.place.deep
        return remote(self.held, self.quarter(), self.sem.at[n + 2], self.sem.at[n + 3], p.device(dy=1))

    def cross(self):
        p, n = self.place, 2 * self.place.deep
        part = self.out.at[at(p.core, 2 * self.held.shape[0])]
        return remote(part, part, self.sem.at[n + 4], self.sem.at[n + 5], p.device(dcore=1))

    def begin(self):
        for copy in self.copies():
            copy.start()
        self.mine().start()

    def middle(self):
        for copy in self.copies():
            copy.wait()
        self.mine().wait()
        self.keep().start()
        self.along().start()

    def third(self):
        self.keep().wait()
        self.along().wait()
        self.cross().start()

    def finish(self):
        self.cross().wait()


def self_fwd_kernel(
    deep, tokens, memory, slot_cot, lengths, slot_mask, qkv_w, out_w, cq_w, gain, bias,
    row, memory_row, slot_row, q, k, v, mix, ext, normed, inverse, cq, qe, ke, live,
    masked, kx_s, vx_s, sem,
):
    place = Place(deep)
    h = place.h
    half = tokens.shape[1]
    row_length, width = row.shape
    place.greet("dh")
    own = [
        pltpu.make_async_copy(src.at[h], dst.at[pl.ds(0, half)], sem.at[i])
        for i, (src, dst) in enumerate(((tokens, row), (memory, memory_row)))
    ]
    own.append(pltpu.make_async_copy(slot_cot, masked, sem.at[2]))
    for copy in own:
        copy.start()
    partner = place.device(dh=1)

    def exchange(src, dst, i):
        return remote(src, dst.at[pl.ds(half, half)], sem.at[3 + 2 * i], sem.at[4 + 2 * i], partner)

    sends = [exchange(tokens.at[1 - h], row, 0), exchange(memory.at[1 - h], memory_row, 1), exchange(masked.at[1 - h], slot_row, 2)]
    place.met()
    sends[0].start()

    position = lax.broadcasted_iota(jnp.int32, (row_length, 128), 0)
    position = jnp.where(h == 0, position, lax.rem(position + half, row_length))
    segment = jnp.zeros((row_length, 128), jnp.int32)
    following = jnp.zeros((row_length, 128), jnp.int32)
    end = 0
    for j in range(lengths.shape[1]):
        end = end + lengths[h, j]
        segment = segment + (position >= end).astype(jnp.int32)
        following = following + (position + 1 >= end).astype(jnp.int32)
    live[...] = ((following == segment) & (position + 1 < row_length)).astype(F32).astype(BF)
    spare = lax.rem(lax.broadcasted_iota(jnp.int32, (row_length, 128), 1), 64)
    coded, hit = spare < lengths.shape[1], segment == spare
    qe[...] = jnp.where(coded & hit, BIG, 0.0).astype(BF)
    ke[...] = jnp.where(coded, jnp.where(hit, 0.0, -BIG), jnp.where(spare < 7, 1.0, 0.0)).astype(BF)

    def project(i):
        rows = at(i, ROWS)
        x = row[rows, :]
        q[rows, :] = dot(x, qkv_w[0]).astype(BF) * jnp.asarray(0.125, BF)
        k[rows, :] = dot(x, qkv_w[1]).astype(BF)
        v[rows, :] = dot(x, qkv_w[2]).astype(BF)

    own[0].wait()
    loop(half // ROWS, project)
    own[2].wait()
    columns = slot_mask[...].astype(F32).T
    for r in range(2):
        masked[r] = masked[r] * columns[:, r : r + 1].astype(BF)
    slot_row[:half, :] = masked[h]
    sends[0].wait()
    sends[1].start()
    loop(row_length // ROWS, project, half // ROWS)

    def next_send():
        sends[1].wait()
        sends[2].start()

    attend(q, k, v, qe, ke, mix, ext, kx_s, vx_s, {2: next_send})

    def after(i):
        rows = at(i, ROWS)
        n, s = normalise(row[rows, :].astype(F32) + dot(mix[rows, :], out_w[...]))
        normed[rows, :] = n
        inverse[rows, :] = s
        low = (n * gain[0:1, :] + bias[0:1, :]).astype(BF)
        cq[rows, :] = dot(low, cq_w[0]).astype(BF) * jnp.asarray(0.125, BF)

    loop(row_length // ROWS, after)
    own[1].wait()
    sends[2].wait()


def cross_fwd_kernel(
    deep, out_cot, memory_row, q, kv_w, out_w, gain, bias, normed_one, qe, ke,
    cot_row, k, v, mix, ext, normed, inverse, kx_s, vx_s, sem,
):
    place = Place(deep)
    half = out_cot.shape[1]
    place.greet("dh")
    own = pltpu.make_async_copy(out_cot.at[place.h], cot_row.at[pl.ds(0, half)], sem.at[0])
    send = remote(out_cot.at[1 - place.h], cot_row.at[pl.ds(half, half)], sem.at[1], sem.at[2], place.device(dh=1))
    own.start()
    blocks = memory_row.shape[0] // ROWS

    def project(i):
        rows = at(i, ROWS)
        x = memory_row[rows, :]
        k[rows, :] = dot(x, kv_w[1]).astype(BF)
        v[rows, :] = dot(x, kv_w[2]).astype(BF)

    loop(blocks, project)
    place.met()
    send.start()
    attend(q, k, v, qe, ke, mix, ext, kx_s, vx_s, {})

    def after(i):
        rows = at(i, ROWS)
        before = normed_one[rows, :] * gain[0:1, :] + bias[0:1, :]
        n, s = normalise(before + dot(mix[rows, :], out_w[...]))
        normed[rows, :] = n
        inverse[rows, :] = s

    loop(blocks, after)
    own.wait()
    send.wait()


def ffn_kernel(
    deep, normed_two, inverse_two, cross_mix, in_w, out_w, slot_w, cross_out_w, gain, bias, live, slot_row, cot_row,
    out_home, slots_home, res_two, grad_mix, sum_out, sum_slot, sum_in, sums,
    low_s, hidden_s, slope_s, normed_s, inverse_s, pair_s, next_s, gnext_s, res_s, ginner_s, res_two_s, out_s, slots_s,
    g_out, g_slot, g_in, came_out, sem_out, came_slot, sem_slot, came_in, sem_in, sem,
):
    row_length, width = low_s.shape
    blocks = row_length // ROWS
    units = in_w.shape[1]
    half = row_length // 2
    place = Place(deep)
    place.greet("dh", "dcore")
    h = place.h
    scale = 0.7978845608028654
    work_out = CoreSum(place, g_out, sum_out, came_out, sem_out)
    work_slot = CoreSum(place, g_slot, sum_slot, came_slot, sem_slot)
    work_in = CoreSum(place, g_in, sum_in, came_in, sem_in)

    def home(src, dst, i):
        return (
            pltpu.make_async_copy(src.at[pl.ds(0, half)], dst.at[h], sem.at[3 * i]),
            remote(src.at[pl.ds(half, half)], dst.at[h], sem.at[3 * i + 1], sem.at[3 * i + 2], place.device(dh=1)),
        )

    homeward = home(out_s, out_home, 0) + home(slots_s, slots_home, 1)

    def forward(i):
        rows = at(i, ROWS)
        after_cross = normed_two[rows, :] * gain[1:2, :] + bias[1:2, :]
        low = after_cross.astype(BF)
        low_s[rows, :] = low
        branch = jnp.zeros((ROWS, width), F32)
        for c in range(units // 512):
            cols = slice(c * 512, (c + 1) * 512)
            inner = dot(low, in_w[:, cols])
            square = inner * inner
            bent = jnp.tanh(inner * (scale + (scale * 0.044715) * square))
            part = 0.5 + 0.5 * bent
            hidden = (inner * part).astype(BF)
            hidden_s[rows, cols] = hidden
            slope = part + inner * (0.5 - 0.5 * bent * bent) * (scale + (3 * scale * 0.044715) * square)
            slope_s[rows, cols] = slope.astype(BF)
            branch = branch + dot(hidden, out_w[cols, :])
        n, s = normalise(after_cross + branch)
        normed_s[rows, :] = n
        inverse_s[rows, :] = s
        final = (n * gain[2:3, :] + bias[2:3, :]).astype(BF)
        out_s[rows, :] = final
        pair_s[rows, :width] = final
        next_s[rows, :] = final.astype(F32)

    loop(blocks, forward)
    place.met()
    for copy in homeward[:2]:
        copy.start()
    next_s[pl.ds(row_length, 8), :] = next_s[pl.ds(0, 8), :]

    def slot(i):
        rows = at(i, ROWS)
        window = pl.ds(pl.multiple_of(i * ROWS, ROWS), ROWS + 8)
        alive = live[rows, 0:1].astype(F32)
        pair_s[rows, width:] = (next_s[window, :][1 : ROWS + 1] * alive).astype(BF)
        slots_s[rows, :] = dot(pair_s[rows, :], slot_w[...]).astype(BF)
        back = (dot_nt(slot_row[rows, :], slot_w[width:, :]) * alive).astype(BF)
        gnext_s[pl.ds(pl.multiple_of(i * ROWS + 8, 8), ROWS), :] = back.astype(F32)

    loop(blocks, slot)
    for copy in homeward[2:]:
        copy.start()
    gnext_s[pl.ds(0, 8), :] = gnext_s[pl.ds(row_length, 8), :]
    sums[...] = jnp.zeros(sums.shape, F32)

    def backward(i):
        rows = at(i, ROWS)
        window = pl.ds(pl.multiple_of(i * ROWS, ROWS), ROWS + 8)
        gradient = (
            cot_row[rows, :].astype(F32)
            + dot_nt(slot_row[rows, :], slot_w[:width, :])
            + gnext_s[window, :][7 : ROWS + 7]
        )
        n = normed_s[rows, :]
        sums[0:1, :] += jnp.sum(gradient * n, axis=0, keepdims=True)
        sums[1:2, :] += jnp.sum(gradient, axis=0, keepdims=True)
        res = norm_back(gradient, n, inverse_s[rows, :], gain[2:3, :])
        res_low = res.astype(BF)
        res_s[rows, :] = res_low
        for c in range(units // 512):
            cols = slice(c * 512, (c + 1) * 512)
            ginner = (dot_nt(res_low, out_w[cols, :]) * slope_s[rows, cols].astype(F32)).astype(BF)
            ginner_s[rows, cols] = ginner
            res = res + dot_nt(ginner, in_w[:, cols])
        n = normed_two[rows, :]
        sums[2:3, :] += jnp.sum(res * n, axis=0, keepdims=True)
        sums[3:4, :] += jnp.sum(res, axis=0, keepdims=True)
        res = norm_back(res, n, inverse_two[rows, :], gain[1:2, :])
        res_two[rows, :] = res
        res_low = res.astype(BF)
        res_two_s[rows, :] = res_low
        grad_mix[rows, :] = dot_nt(res_low, cross_out_w[...]).astype(BF)

    loop(blocks, backward)
    fill(g_out, units // 2)
    fill(g_slot, width + width // 2)
    fill(g_in, width * units // 1024)
    for side in range(2):
        def tile_out(r, side=side):
            g_out[side, at(r, 256), :] = dot_tn(hidden_s[:, at(side * (units // 512) + r, 256)], res_s[...]).astype(BF)

        loop(units // 512, tile_out)
    work_out.begin()
    for side in range(2):
        def tile_slot(r, side=side):
            g_slot[side, at(r, 256), :] = dot_tn(pair_s[:, at(side * (width // 256) + r, 256)], slot_row[...]).astype(BF)

        loop(width // 256, tile_slot)
        g_slot[side, width : width + width // 2, :] = dot_tn(cross_mix[:, side * 256 : (side + 1) * 256], res_two_s[...]).astype(BF)
    work_slot.begin()
    for c in range(units // 512):
        def tile_in(r, c=c):
            side, block = divmod(c, units // 1024)
            g_in[side, pl.ds(pl.multiple_of(block * width + r * 256, 256), 256), :] = dot_tn(
                low_s[:, at(r, 256)], ginner_s[:, c * 512 : (c + 1) * 512]
            ).astype(BF)

        loop(width // 256, tile_in)
    work_in.begin()
    work_out.finish()
    work_slot.finish()
    work_in.finish()
    for copy in homeward:
        copy.wait()


def fill(grads, used):
    rest = grads.shape[1] - used
    if rest:
        grads[:, used:, :] = jnp.zeros((2, rest, grads.shape[2]), BF)


def cross_bwd_kernel(
    deep, sum_out, sum_slot, sum_in,
    q, k, v, ext, ke, mix, gmix, memory_row, qkv_w, res_two, normed_one, inverse_one, gain, bias, self_mix, self_out_w,
    mem_mine, mem_theirs, res_one, grad_self_mix, grads, sums, share_out, share_slot, share_in,
    low_s, dq_s, dk_s, dv_s, res_s, kx_s, vx_s, qx_s, dx_s, kt_s, dqt_s, *comm,
):
    row_length, width = memory_row.shape
    blocks = row_length // ROWS
    place = Place(deep)
    place.greet("dh", "dy", "dz")
    planes, splits = [], []
    for i, (own, share, x_first) in enumerate(((sum_out, share_out, False), (sum_slot, share_slot, False), (sum_in, share_in, True))):
        part = comm[7 * i : 7 * i + 7]
        planes.append(Plane(place, own, *part[:5], x_first))
        splits.append(Split(place, part[3], part[5], share, part[6]))
    place.met()
    planes[0].begin()
    planes[2].begin()

    def first():
        planes[0].middle()
        planes[1].begin()
        planes[2].middle()

    def second():
        planes[0].finish()
        splits[0].begin()
        planes[1].middle()

    def third():
        planes[2].finish()
        splits[2].begin()

    def fourth():
        planes[1].finish()
        splits[1].begin()

    attend_back(
        q, k, v, ext, ke, mix, gmix, dq_s, dk_s, dv_s, kx_s, vx_s, qx_s, dx_s, kt_s, dqt_s,
        {3: first, 5: second, 6: third, 7: fourth},
    )
    sums[...] = jnp.zeros(sums.shape, F32)

    def memory_grad(i):
        rows = at(i, ROWS)
        return dot_nt(dk_s[rows, :], qkv_w[1]) + dot_nt(dv_s[rows, :], qkv_w[2])

    def store_mine(i):
        mem_mine[at(i, ROWS), :] = memory_grad(i)

    def store_theirs(i):
        mem_theirs[at(i, ROWS), :] = memory_grad(i + blocks // 2).astype(BF)

    loop(blocks // 2, store_mine)
    loop(blocks // 2, store_theirs)

    def backward(i):
        rows = at(i, ROWS)
        n = normed_one[rows, :]
        low_s[rows, :] = (n * gain[0:1, :] + bias[0:1, :]).astype(BF)
        gradient = res_two[rows, :] + dot_nt(dq_s[rows, :], qkv_w[0])
        sums[0:1, :] += jnp.sum(gradient * n, axis=0, keepdims=True)
        sums[1:2, :] += jnp.sum(gradient, axis=0, keepdims=True)
        res = norm_back(gradient, n, inverse_one[rows, :], gain[0:1, :])
        res_one[rows, :] = res
        res_low = res.astype(BF)
        res_s[rows, :] = res_low
        grad_self_mix[rows, :] = dot_nt(res_low, self_out_w[...]).astype(BF)

    loop(blocks, backward)
    splits[0].finish()
    splits[2].finish()

    def tile(r):
        cols = at(r, 256)
        for part, (left, right) in enumerate(((low_s, dq_s), (memory_row, dk_s), (memory_row, dv_s))):
            block = dot_tn(left[:, cols], right[...]).astype(BF)
            for side in range(2):
                grads[side, pl.ds(pl.multiple_of(part * width + r * 256, 256), 256), :] = block[:, side * 256 : (side + 1) * 256]

    loop(width // 256, tile)
    for side in range(2):
        block = dot_tn(self_mix[:, side * 256 : (side + 1) * 256], res_s[...]).astype(BF)
        for c in range(2):
            grads[side, 3 * width + c * 256 : 3 * width + (c + 1) * 256, :] = block[:, c * 256 : (c + 1) * 256]
    fill(grads, 4 * width)
    splits[1].finish()


def self_bwd_kernel(
    deep, share_out, share_slot, share_in, grads_d, mem_theirs,
    q, k, v, ext, ke, mix, gmix, row, qkv_w, res_one, sums_one, sums_two,
    done_out, done_slot, done_in, done_d, done_e, done_f, mem_came, row_mine, row_came,
    dq_s, dk_s, dv_s, kx_s, vx_s, qx_s, dx_s, kt_s, dqt_s, row_theirs, grads_e, grads_f, grads_d_s, sem, *comm,
):
    row_length, width = row.shape
    blocks = row_length // ROWS
    place = Place(deep)
    place.greet("dh", "dy", "dz", "dcore")
    early = []
    for i, (share, done) in enumerate(((share_out, done_out), (share_slot, done_slot), (share_in, done_in))):
        early.append(Spread(place, share, comm[2 * i], done, comm[2 * i + 1]))
    comm = comm[6:]
    chains = []
    for grads, done in ((grads_d_s, done_d), (grads_e, done_e), (grads_f, done_f)):
        own, came, core_sem, kept, came_a, came_b, total, plane_sem, came_z, split_sem, share, held, spread_sem = comm[:13]
        comm = comm[13:]
        core = CoreSum(place, grads, own, came, core_sem)
        plane = Plane(place, own, kept, came_a, came_b, total, plane_sem, False)
        split = Split(place, total, came_z, share, split_sem)
        spread = Spread(place, share, held, done, spread_sem)

        def stages(core=core, plane=plane, split=split, spread=spread):
            def to_plane():
                core.finish()
                plane.begin()

            def to_split():
                plane.finish()
                split.begin()

            def to_spread():
                split.finish()
                spread.begin()

            return [core.begin, to_plane, plane.middle, to_split, to_spread, spread.middle, spread.third, spread.finish]

        chains.append(stages())
    chain_d, chain_e, chain_f = chains
    load_d = pltpu.make_async_copy(grads_d, grads_d_s, sem.at[0])
    load_d.start()
    mem_send = remote(mem_theirs, mem_came, sem.at[1], sem.at[2], place.device(dh=1))
    row_send = remote(row_theirs, row_came, sem.at[3], sem.at[4], place.device(dh=1))
    norms = jnp.concatenate(
        [sums_one[0:1, :], sums_two[2:3, :], sums_two[0:1, :], sums_one[1:2, :], sums_two[3:4, :], sums_two[1:2, :],
         jnp.zeros((10, width), F32)], axis=0
    ).astype(BF)
    for side in range(2):
        for part in range(2):
            lanes = slice(side * 256 + part * 128, side * 256 + (part + 1) * 128)
            (grads_e, grads_f)[part][side, 3 * width : 3 * width + 16, :] = norms[:, lanes]
    fill(grads_e, 3 * width + 16)
    fill(grads_f, 3 * width + 16)
    load_d.wait()
    place.met()
    chain_d[0]()
    for spread in early:
        spread.begin()
    mem_send.start()

    def weight_grads(grads, pairs):
        parts = [d[:, p * 128 : (p + 1) * 128] for d in (dq_s, dk_s, dv_s) for p in pairs]
        right = jnp.concatenate(parts, axis=1)
        for r in range(width // 256):
            block = dot_tn(row[:, r * 256 : (r + 1) * 256], right).astype(BF)
            for part in range(3):
                for side in range(2):
                    lane = (part * 2 + side) * 128
                    grads[side, part * width + r * 256 : part * width + (r + 1) * 256, :] = block[:, lane : lane + 128]

    def at_three():
        weight_grads(grads_e, (0, 2))
        chain_e[0]()
        chain_d[2]()

    def at_four():
        early[0].middle()
        chain_e[1]()

    def at_five():
        early[1].middle()
        early[2].middle()
        chain_d[3]()

    def at_six():
        chain_e[2]()
        chain_d[4]()

    def at_seven():
        early[0].third()
        chain_e[3]()

    attend_back(
        q, k, v, ext, ke, mix, gmix, dq_s, dk_s, dv_s, kx_s, vx_s, qx_s, dx_s, kt_s, dqt_s,
        {0: chain_d[1], 3: at_three, 4: at_four, 5: at_five, 6: at_six, 7: at_seven},
    )
    weight_grads(grads_f, (1, 3))
    chain_f[0]()

    def row_grad(i):
        rows = at(i, ROWS)
        return (
            res_one[rows, :] + dot_nt(dq_s[rows, :], qkv_w[0]) + dot_nt(dk_s[rows, :], qkv_w[1])
            + dot_nt(dv_s[rows, :], qkv_w[2])
        )

    def store_theirs(i):
        row_theirs[at(i, ROWS), :] = row_grad(i + blocks // 2).astype(BF)

    def store_mine(i):
        row_mine[at(i, ROWS), :] = row_grad(i)

    loop(blocks // 2, store_theirs)
    row_send.start()
    chain_f[1]()
    chain_d[5]()
    chain_e[4]()
    loop(blocks // 2, store_mine)
    chain_f[2]()
    early[1].third()
    early[2].third()
    chain_e[5]()
    chain_d[6]()
    chain_f[3]()
    chain_f[4]()
    chain_e[6]()
    chain_f[5]()
    chain_f[6]()
    for spread in early:
        spread.finish()
    for chain in chains:
        chain[7]()
    mem_send.wait()
    row_send.wait()


def call(kernel, name, cid, args, outs, scratch, flops):
    return pl.pallas_call(
        kernel,
        out_shape=[jax.ShapeDtypeStruct(shape, kind) for shape, kind, _ in outs],
        in_specs=[spec for _, spec in args],
        out_specs=[spec for _, _, spec in outs],
        scratch_shapes=scratch,
        compiler_params=pltpu.CompilerParams(collective_id=cid, has_side_effects=True, vmem_limit_bytes=VMEM),
        cost_estimate=pl.CostEstimate(flops=flops, bytes_accessed=2**20, transcendentals=0),
        name=name,
    )(*[arg for arg, _ in args])


def padded(count, unit):
    return -(-count // unit) * unit


def per_device(
    tokens, memory, lengths, slot_mask, self_qkv, self_out, cross_qkv, cross_out,
    norm_gain, norm_bias, ffn_in, ffn_out, slot_proj, out_cot, slot_cot,
):
    local_len, width = tokens.shape[1:]
    units = ffn_in.shape[1]
    h = lax.axis_index("head")
    deep = lax.axis_size("dp") // 4
    row_length = 2 * local_len
    unit = 64 * deep
    rows_out, rows_slot, rows_in = padded(units // 2, unit), padded(width + width // 2, unit), padded(width * units // 1024, unit)
    rows_d, rows_e = padded(4 * width, unit), padded(3 * width + 16, unit)
    dense = 2 * row_length * width * width
    scores = 2 * row_length * row_length * width

    def inner(*values):
        return [(value, INNER) for value in values]

    def outer(*values):
        return [(value, ANY) for value in values]

    def new(*shape, kind=BF, spec=INNER):
        return (shape, kind, spec)

    def scratch(*shape, kind=BF):
        return pltpu.VMEM(shape, kind)

    row, wide, column = new(row_length, width), new(row_length, width, kind=F32), new(row_length, 1, kind=F32)
    small = new(row_length, 128)
    row_s, wide_s, two_s = scratch(row_length, width), scratch(row_length, width, kind=F32), scratch(row_length, 256)
    tall_s, ring_s = scratch(row_length, units), scratch(row_length + 8, width, kind=F32)

    row_in, memory_row, slot_row, q, k, v, mix, ext, normed_one, inverse_one, cq, qe, ke, live = call(
        functools.partial(self_fwd_kernel, deep), "self_fwd", 0,
        outer(tokens, memory, slot_cot) + [(lengths, SCALARS)]
        + inner(slot_mask, self_qkv, self_out, cross_qkv, norm_gain, norm_bias),
        [row] * 8 + [wide, column, row] + [small] * 3,
        [scratch(2, local_len, width), two_s, two_s, DMA((9,))], 5 * dense + 8 * scores,
    )
    cot_row, ck, cv, cmix, cext, normed_two, inverse_two = call(
        functools.partial(cross_fwd_kernel, deep), "cross_fwd", 1,
        outer(out_cot) + inner(memory_row, cq, cross_qkv, cross_out, norm_gain, norm_bias, normed_one, qe, ke),
        [row] * 5 + [wide, column], [two_s, two_s, DMA((3,))], 3 * dense + 8 * scores,
    )
    home = new(2, local_len, width, spec=ANY)
    groups = ((rows_out, 512), (rows_slot, 512), (rows_in, 512))
    out, slots, res_two, grad_cmix, sum_out, sum_slot, sum_in, sums_two = call(
        functools.partial(ffn_kernel, deep), "ffn", 2,
        inner(normed_two, inverse_two, cmix, ffn_in, ffn_out, slot_proj, cross_out, norm_gain, norm_bias, live, slot_row, cot_row),
        [home, home, wide, row] + [new(2, 2, rows // 4, lanes) for rows, lanes in groups] + [new(8, width, kind=F32)],
        [row_s, tall_s, tall_s, wide_s, scratch(row_length, 1, kind=F32), scratch(row_length, 2 * width), ring_s, ring_s, row_s,
         tall_s, row_s, row_s, row_s]
        + [scratch(2, rows, lanes) for rows, lanes in groups]
        + [part for group in groups for part in CoreSum.scratch(*group)] + [DMA((6,))], 32 * dense,
    )
    back = [two_s] * 4 + [scratch(128, row_length), scratch(128, row_length, kind=F32)]

    def shares(rows, lanes):
        return new(rows // (4 * deep), lanes)

    half = new(local_len, width)
    mem_mine, mem_theirs, res_one, grad_smix, grads_d, sums_one, share_out, share_slot, share_in = call(
        functools.partial(cross_bwd_kernel, deep), "cross_bwd", 3,
        outer(sum_out, sum_slot, sum_in)
        + inner(cq, ck, cv, cext, ke, cmix, grad_cmix, memory_row, cross_qkv, res_two, normed_one, inverse_one,
                norm_gain, norm_bias, mix, self_out),
        [new(local_len, width, kind=F32), half, wide, row, new(2, rows_d, 256), new(8, width, kind=F32)] + [shares(*group) for group in groups],
        [row_s] * 5 + back + [part for group in groups for part in Plane.scratch(*group) + Split.scratch(deep, *group)],
        12 * dense + 20 * scores,
    )

    def whole(rows, lanes):
        return new(rows, lanes, spec=ANY)

    def chain(rows, lanes):
        return (
            [scratch(2, 2, rows // 4, lanes)] + CoreSum.scratch(rows, lanes) + Plane.scratch(rows, lanes)
            + Split.scratch(deep, rows, lanes) + [scratch(rows // (4 * deep), lanes)] + Spread.scratch(deep, rows, lanes)
        )

    late = ((rows_d, 256), (rows_e, 128), (rows_e, 128))
    away = new(local_len, width, spec=ANY)
    done_out, done_slot, done_in, done_d, done_e, done_f, mem_came, row_mine, row_came = call(
        functools.partial(self_bwd_kernel, deep), "self_bwd", 4,
        inner(share_out, share_slot, share_in) + outer(grads_d, mem_theirs)
        + inner(q, k, v, ext, ke, mix, grad_smix, row_in, self_qkv, res_one, sums_one, sums_two),
        [whole(*group) for group in groups + late] + [away, new(local_len, width, kind=F32), away],
        [row_s] * 3 + back
        + [scratch(local_len, width), scratch(2, rows_e, 128), scratch(2, rows_e, 128), scratch(2, rows_d, 256), DMA((5,))]
        + [part for group in groups for part in Spread.scratch(deep, *group)] + [part for group in late for part in chain(*group)],
        10 * dense + 20 * scores,
    )

    def joined(mine, theirs):
        theirs = theirs.astype(F32)
        return jnp.stack([jnp.where(h == 0, mine, theirs), jnp.where(h == 0, theirs, mine)], axis=0)

    d = done_d.astype(F32)
    e = jnp.concatenate([done_e[: 3 * width], done_f[: 3 * width]], axis=1).astype(F32)
    norms = jnp.concatenate([done_e[3 * width : 3 * width + 6], done_f[3 * width : 3 * width + 6]], axis=1).astype(F32)
    return (
        out,
        slots * slot_mask.astype(BF)[:, :, None],
        joined(row_mine, row_came),
        joined(mem_mine, mem_came),
        e.reshape(3, width, 256),
        jnp.concatenate([d[3 * width : 3 * width + 256], d[3 * width + 256 : 4 * width]], axis=1),
        d[: 3 * width].reshape(3, width, 256),
        done_slot[width : width + width // 2].astype(F32),
        norms[:3],
        norms[3:],
        jnp.concatenate([done_in[i * width : (i + 1) * width] for i in range(units // 1024)], axis=1).astype(F32),
        done_out[: units // 2].astype(F32),
        done_slot[:width].astype(F32),
    )


def solution(mesh):
    split = P("dp", "head", None)
    placed = (split, split, P("dp", None), P("dp", "head")) + (P(),) * 9 + (split, split)
    return jax.shard_map(
        per_device,
        mesh=mesh,
        in_specs=placed,
        out_specs=(
            split, split, split, split,
            P(None, None, "head"), P("head", None), P(None, None, "head"), P("head", None),
            P(None, "head"), P(None, "head"), P(None, "head"), P("head", None), P("head", None),
        ),
        check_vma=False,
    )
```

```python
import functools

import jax
import jax.numpy as jnp
from jax import lax
from jax.experimental import pallas as pl
from jax.experimental.pallas import tpu as pltpu
from jax.sharding import PartitionSpec as P

HEADS = 8
BF = jnp.bfloat16
F32 = jnp.float32
MESH = pl.DeviceIdType.MESH
NT = (((1,), (1,)), ((), ()))
TN = (((0,), (0,)), ((), ()))
BIG = 2.0**20
VMEM = 60 * 2**20
ROWS = 512
QBLOCK = 512
ANY = pl.BlockSpec(memory_space=pl.ANY)
INNER = pl.BlockSpec(memory_space=pltpu.VMEM)
SCALARS = pl.BlockSpec(memory_space=pltpu.SMEM)


def dot(a, b):
    return jnp.dot(a, b, preferred_element_type=F32)


def dot_nt(a, b):
    return lax.dot_general(a, b, NT, preferred_element_type=F32)


def dot_tn(a, b):
    return lax.dot_general(a, b, TN, preferred_element_type=F32)


def at(i, size):
    return pl.ds(pl.multiple_of(i * size, size), size)


def loop(count, body, first=0):
    def step(i, carry):
        body(i)
        return carry

    lax.fori_loop(first, count, step, 0)


def thirds(value):
    first = value.astype(BF)
    rest = value - first.astype(F32)
    second = rest.astype(BF)
    third = (rest - second.astype(F32)).astype(BF)
    return first, second, third


def normalise(value):
    average = jnp.mean(value, axis=-1, keepdims=True)
    centred = value - average
    inverse = lax.rsqrt(jnp.mean(centred * centred, axis=-1, keepdims=True) + 1e-05)
    return centred * inverse, inverse


def norm_back(gradient, normed, inverse, gain_row):
    scaled = gradient * gain_row
    inner_mean = jnp.mean(scaled, axis=-1, keepdims=True)
    cross_mean = jnp.mean(scaled * normed, axis=-1, keepdims=True)
    return inverse * (scaled - inner_mean - normed * cross_mean)


def run_hooks(hooks, step):
    for done, hook in hooks.items():
        if done >= 0:
            pl.when(step == done)(hook)


def attend(q_s, k_s, v_s, qe_ref, ke_ref, mix_s, ext_s, kx_s, vx_s, hooks):
    row_length = k_s.shape[0]
    block = QBLOCK
    lane = lax.broadcasted_iota(jnp.int32, (row_length, 128), 1)
    wide_low = lane < 64
    lane = lax.broadcasted_iota(jnp.int32, (block, 128), 1)
    low = lane < 64
    spare = lax.rem(lane, 64)

    def pair(p):
        lanes = at(p, 128)
        for h in range(2):
            mine = wide_low if h == 0 else ~wide_low
            part = slice(h * 128, (h + 1) * 128)
            kx_s[:, part] = jnp.where(mine, k_s[:, lanes], ke_ref[...])
            vx_s[:, part] = jnp.where(mine, v_s[:, lanes], jnp.ones((), BF))
        for i in range(row_length // block):
            rows = slice(i * block, (i + 1) * block)
            scaled = q_s[rows, lanes]
            extra = qe_ref[rows, :]
            tops, sums = [], []
            for h in range(2):
                part = slice(h * 128, (h + 1) * 128)
                query = jnp.where(low if h == 0 else ~low, scaled, extra)
                scores = dot_nt(query, kx_s[:, part])
                top = jnp.max(scores, axis=1, keepdims=True)
                probs = jnp.exp(scores - top).astype(BF)
                tops.append(top)
                sums.append(dot(probs, vx_s[:, part]))
            mixed = jnp.where(low, sums[0], sums[1])
            totals = jnp.where(low, sums[1], sums[0])
            log_total = jnp.where(low, tops[1], tops[0]) + jnp.log(totals)
            first, second, third = thirds(log_total)
            ext_s[rows, lanes] = jnp.where(
                spare == 4, -first, jnp.where(spare == 5, -second, jnp.where(spare == 6, -third, extra))
            )
            mix_s[rows, lanes] = (mixed / pltpu.roll(totals, 64, 1)).astype(BF)
        run_hooks(hooks, p)

    loop(HEADS // 2, pair)


def head_pair(i):
    return lax.rem(i, 2) * 2 + lax.div(i, 2)


def attend_back(q_s, k_s, v_s, ext_s, ke_ref, mix_s, gmix_s, dq_s, dk_s, dv_s, kx_s, vx_s, qx_s, dx_s, kt_s, dqt_s, hooks, get_pair):
    row_length = k_s.shape[0]
    block = QBLOCK
    lane = lax.broadcasted_iota(jnp.int32, (row_length, 128), 1)
    spare = lax.rem(lane, 64)
    zero = jnp.zeros((), BF)

    def head(step):
        i, odd = lax.div(step, 2), lax.rem(step, 2)
        lanes = at(head_pair(i), 128)
        mine = lax.div(lane, 64) == odd

        @pl.when(odd == 0)
        def arrive():
            for copy in get_pair(i):
                copy.wait()

        product = gmix_s[:, lanes].astype(F32) * mix_s[:, lanes].astype(F32)
        first, second, third = thirds(jnp.sum(jnp.where(mine, product, 0.0), axis=1, keepdims=True))
        extra = jnp.where(spare == 0, -first, jnp.where(spare == 1, -second, jnp.where(spare == 2, -third, zero)))
        kt_s[...] = k_s[:, lanes].T
        kx_s[...] = jnp.where(mine, k_s[:, lanes], ke_ref[...])
        vx_s[...] = jnp.where(mine, v_s[:, lanes], jnp.ones((), BF))
        qx_s[...] = jnp.where(mine, q_s[:, lanes], ext_s[:, lanes])
        dx_s[...] = jnp.where(mine, gmix_s[:, lanes], extra)
        own = at(odd, 64)
        for j in range(row_length // block):
            cols = slice(j * block, (j + 1) * block)
            probs = jnp.exp(dot_nt(kx_s[...], qx_s[cols, :]))
            ds = (probs * dot_nt(vx_s[...], dx_s[cols, :])).astype(BF)
            dv = dot(probs.astype(BF), dx_s[cols, :])
            dk = dot(ds, qx_s[cols, :])
            acc_v, acc_k = (dv, dk) if j == 0 else (acc_v + dv, acc_k + dk)
            dqt_s[own, cols] = dot(kt_s[own, :], ds) * 0.125
        dk_s[:, lanes] = jnp.where(mine, acc_k.astype(BF), dk_s[:, lanes])
        dv_s[:, lanes] = jnp.where(mine, acc_v.astype(BF), dv_s[:, lanes])

        @pl.when(odd == 1)
        def turn():
            dq_s[:, lanes] = dqt_s[...].T.astype(BF)

        run_hooks(hooks, step)

    loop(HEADS, head)


class Place:
    def __init__(self, deep):
        dp = lax.axis_index("dp")
        self.deep = deep
        self.h = lax.axis_index("head")
        self.core = lax.rem(dp, 2)
        self.y = lax.rem(lax.div(dp, 2), 2)
        self.z = lax.div(dp, 4)

    def device(self, dh=0, dcore=0, dy=0, dz=None):
        h = 1 - self.h if dh else self.h
        core = 1 - self.core if dcore else self.core
        y = 1 - self.y if dy else self.y
        z = self.z if dz is None else lax.rem(self.z + dz, self.deep)
        return ((z * 2 + y) * 2 + core, h)

    def greet(self, *kinds):
        self.peers = []
        for kind in kinds:
            if kind == "dz":
                bits = [1 << i for i in range(self.deep.bit_length() - 1)]
                self.peers += [self.device(dz=self.deep + b - 2 * b * lax.rem(lax.div(self.z, b), 2)) for b in bits]
            else:
                self.peers.append(self.device(**{kind: 1}))
        barrier = pltpu.get_barrier_semaphore()
        for peer in self.peers:
            pl.semaphore_signal(barrier, inc=1, device_id=peer, device_id_type=MESH)

    def met(self):
        pl.semaphore_wait(pltpu.get_barrier_semaphore(), len(self.peers))


def remote(src, dst, send, recv, device):
    return pltpu.make_async_remote_copy(
        src_ref=src, dst_ref=dst, send_sem=send, recv_sem=recv, device_id=device, device_id_type=MESH
    )


DMA = pltpu.SemaphoreType.DMA


class CoreSum:
    def __init__(self, place, src, own, came, sem):
        self.place, self.src, self.own, self.came, self.sem = place, src, own, came, sem

    @staticmethod
    def scratch(rows, width, sides=2):
        return [pltpu.VMEM((sides, rows // 2, width), BF), DMA((2,))]

    def cross(self):
        size = self.src.shape[1] // 2
        return remote(
            self.src.at[:, at(1 - self.place.core, size)], self.came, self.sem.at[0], self.sem.at[1], self.place.device(dcore=1)
        )

    def begin(self):
        self.cross().start()

    def finish(self):
        self.cross().wait()
        size = self.own.shape[2]
        for side in range(self.own.shape[0]):
            for yy in range(2):
                here = self.src[side, at(self.place.core * 2 + yy, size), :]
                self.own[side, yy] = here + self.came[side, yy * size : (yy + 1) * size, :]


class Plane:
    def __init__(self, place, own, kept, came_a, came_b, total, sem, x_first):
        self.place, self.own, self.kept, self.came_a, self.came_b = place, own, kept, came_a, came_b
        self.total, self.sem, self.x_first = total, sem, x_first

    @staticmethod
    def scratch(rows, width):
        block = rows // 4
        return [pltpu.VMEM((2, block, width), BF)] * 2 + [pltpu.VMEM((block, width), BF)] * 2 + [DMA((5,))]

    def load(self):
        p = self.place
        part = self.own.at[p.h] if self.x_first else self.own.at[:, p.y]
        return pltpu.make_async_copy(part, self.kept, self.sem.at[0])

    def hop_a(self):
        p = self.place
        if self.x_first:
            part, device = self.own.at[1 - p.h], p.device(dh=1)
        else:
            part, device = self.own.at[:, 1 - p.y], p.device(dy=1)
        return remote(part, self.came_a, self.sem.at[1], self.sem.at[2], device)

    def hop_b(self):
        p = self.place
        if self.x_first:
            part, device = self.kept.at[1 - p.y], p.device(dy=1)
        else:
            part, device = self.kept.at[1 - p.h], p.device(dh=1)
        return remote(part, self.came_b, self.sem.at[3], self.sem.at[4], device)

    def begin_a(self):
        self.hop_a().start()
        self.load().start()

    def finish_a(self):
        self.load().wait()
        self.hop_a().wait()
        self.kept[...] = self.kept[...] + self.came_a[...]

    def begin_b(self):
        self.hop_b().start()

    def finish_b(self):
        self.hop_b().wait()
        side = self.place.y if self.x_first else self.place.h
        self.total[...] = self.kept[side] + self.came_b[...]


class SidePlane:
    def __init__(self, place, own, kept, came_a, came_b, total, sem, side):
        self.place, self.own, self.kept, self.came_a, self.came_b = place, own, kept, came_a, came_b
        self.total, self.sem, self.side = total, sem, side

    @staticmethod
    def scratch(rows, width):
        return [pltpu.VMEM((rows // 4, width), BF)] * 4 + [DMA((4,))]

    def hop_a(self):
        p = self.place
        return remote(self.own.at[0, 1 - p.y], self.came_a, self.sem.at[0], self.sem.at[1], p.device(dy=1))

    def hop_b(self):
        return remote(self.kept, self.came_b, self.sem.at[2], self.sem.at[3], self.place.device(dh=1))

    def begin_a(self):
        self.hop_a().start()

    def finish_a(self):
        self.hop_a().wait()
        self.kept[...] = self.own[0, self.place.y] + self.came_a[...]

    def begin_b(self):
        pl.when(self.place.h != self.side)(lambda: self.hop_b().start())

    def finish_b(self):
        pl.when(self.place.h != self.side)(lambda: self.hop_b().wait_send())

        def arrived():
            self.hop_b().wait_recv()
            self.total[...] = self.kept[...] + self.came_b[...]

        pl.when(self.place.h == self.side)(arrived)


class Column:
    def __init__(self, place, total, came, held, sem):
        self.place, self.total, self.came, self.held, self.sem = place, total, came, held, sem
        self.steps = place.deep.bit_length() - 1

    @staticmethod
    def scratch(deep, rows, width):
        return [pltpu.VMEM((rows // 4, width), BF)] * 2 + [DMA((4 * deep,))]

    def block(self, k):
        size, first = self.total.shape[0], 0
        for i in range(k):
            size //= 2
            first = first + lax.rem(lax.div(self.place.z, 1 << i), 2) * size
        return first

    def partner(self, k):
        bit = lax.rem(lax.div(self.place.z, 1 << k), 2)
        return self.place.device(dz=self.place.deep + (1 << k) - 2 * (1 << k) * bit)

    def rows(self, first, k):
        size = self.total.shape[0] >> k
        return pl.ds(pl.multiple_of(first, size), size)

    def fold(self, k):
        size = self.total.shape[0] >> (k + 1)
        other = 2 * self.block(k) + size - self.block(k + 1)
        arrived = self.came.at[pl.ds(self.total.shape[0] - 2 * size, size)]
        return remote(self.total.at[self.rows(other, k + 1)], arrived, self.sem.at[2 * k], self.sem.at[2 * k + 1], self.partner(k))

    def unfold(self, k):
        mine = self.held.at[self.rows(self.block(k + 1), k + 1)]
        n = 2 * self.steps + 2 * k
        return remote(mine, mine, self.sem.at[n], self.sem.at[n + 1], self.partner(k))

    def folded(self, k):
        self.fold(k).wait()
        size = self.total.shape[0] >> (k + 1)
        rows = self.rows(self.block(k + 1), k + 1)
        out = self.held if k == self.steps - 1 else self.total
        out[rows, :] = self.total[rows, :] + self.came[self.total.shape[0] - 2 * size : self.total.shape[0] - size, :]

    def hops(self):
        down = [(lambda k=k: self.fold(k).start(), lambda k=k: self.folded(k)) for k in range(self.steps)]
        up = [(lambda k=k: self.unfold(k).start(), lambda k=k: self.unfold(k).wait()) for k in reversed(range(self.steps))]
        return down + up


class Spread:
    def __init__(self, place, held, out, sem):
        self.place, self.held, self.out, self.sem = place, held, out, sem

    def quarter(self):
        return self.out.at[at(self.place.core * 2 + self.place.y, self.held.shape[0])]

    def keep(self):
        return pltpu.make_async_copy(self.held, self.quarter(), self.sem.at[0])

    def along(self):
        return remote(self.held, self.quarter(), self.sem.at[1], self.sem.at[2], self.place.device(dy=1))

    def cross(self):
        part = self.out.at[at(self.place.core, 2 * self.held.shape[0])]
        return remote(part, part, self.sem.at[3], self.sem.at[4], self.place.device(dcore=1))

    def begin_y(self):
        self.keep().start()
        self.along().start()

    def finish_y(self):
        self.keep().wait()
        self.along().wait()

    def hops(self):
        return [(self.begin_y, self.finish_y), (lambda: self.cross().start(), lambda: self.cross().wait())]


def chain(place, kind, buffers, done, x_first=False, side=None, own=None):
    buffers = list(buffers)
    take = lambda n: [buffers.pop(0) for _ in range(n)]
    hops = []
    if kind is None:
        grads, own, came, sem = take(4)
        core = CoreSum(place, grads, own, came, sem)
        hops.append((core.begin, core.finish))
    if side is None:
        plane = Plane(place, own, *take(5), x_first)
    else:
        plane = SidePlane(place, own, *take(5), side)
    came, held, column_sem, spread_sem = take(4)
    if kind != "kept":
        hops.append((plane.begin_a, plane.finish_a))
    hops.append((plane.begin_b, plane.finish_b))
    rest = Column(place, plane.total, came, held, column_sem).hops() + Spread(place, held, done, spread_sem).hops()
    if side is not None:
        here = lambda stage: lambda: pl.when(place.h == side)(stage)
        rest = [(here(begin), here(finish)) for begin, finish in rest]
    hops += rest

    def joint(finish, begin):
        def stage():
            finish()
            begin()

        return stage

    return [hops[0][0]] + [joint(a[1], b[0]) for a, b in zip(hops, hops[1:])] + [hops[-1][1]]


def chain_scratch(deep, rows, width, kind=None, sides=2):
    parts = []
    if kind is None:
        parts += [pltpu.VMEM((sides, rows, width), BF), pltpu.VMEM((sides, 2, rows // 4, width), BF)] + CoreSum.scratch(rows, width, sides)
    parts += (Plane if sides == 2 else SidePlane).scratch(rows, width)
    return parts + Column.scratch(deep, rows, width) + [DMA((5,))]


class Moves:
    def __init__(self, sem):
        self.sem, self.used = sem, 0

    def copy(self, src, dst):
        self.used += 1
        return pltpu.make_async_copy(src, dst, self.sem.at[self.used - 1])

    def blocks(self, src, dst, count, size=ROWS):
        first = self.used
        self.used += count
        return lambda i: pltpu.make_async_copy(src.at[at(i, size)], dst.at[at(i, size)], self.sem.at[first + i])

    def pairs(self, sources, targets):
        first, many = self.used, len(sources)
        self.used += many * (HEADS // 2)

        def copies(i):
            lanes = at(head_pair(i), 128)
            return [
                pltpu.make_async_copy(src.at[:, lanes], dst.at[:, lanes], self.sem.at[first + i * many + j])
                for j, (src, dst) in enumerate(zip(sources, targets))
            ]

        return copies


def start(*copies):
    for copy in copies:
        copy.start()


def wait(*copies):
    for copy in copies:
        copy.wait()


def self_fwd_kernel(
    deep, tokens, memory, out_cot, qkv_w, out_w, cq_w, lengths, gain, bias,
    row_came, memory_came, cot_came, q, k, v, mix, ext, normed, inverse, cq, qe, ke, live,
    row_s, qkv_s, out_s, cqw_s, q_s, k_s, v_s, mix_s, ext_s, normed_s, inverse_s, cq_s, qe_s, ke_s, live_s, kx_s, vx_s, sem, sem_far,
):
    place = Place(deep)
    h = place.h
    half = tokens.shape[1]
    row_length, width = row_s.shape
    blocks = row_length // ROWS
    lower, upper = pl.ds(0, half), pl.ds(half, half)
    place.greet("dh")
    moves = Moves(sem)
    own_row = moves.copy(tokens.at[h], row_s.at[lower])
    get_w = moves.copy(qkv_w, qkv_s)
    late = [moves.copy(out_w, out_s), moves.copy(cq_w.at[0], cqw_s)]
    start(own_row, get_w)
    partner = place.device(dh=1)
    send_row = remote(tokens.at[1 - h], row_s.at[upper], sem_far.at[0], sem_far.at[1], partner)
    send_memory = remote(memory.at[1 - h], memory_came, sem_far.at[2], sem_far.at[3], partner)
    send_cot = remote(out_cot.at[1 - h, pl.ds(0, half // 2)], cot_came, sem_far.at[4], sem_far.at[5], partner)
    place.met()
    send_row.start()

    position = lax.broadcasted_iota(jnp.int32, (row_length, 128), 0)
    position = jnp.where(h == 0, position, lax.rem(position + half, row_length))
    segment = jnp.zeros((row_length, 128), jnp.int32)
    following = jnp.zeros((row_length, 128), jnp.int32)
    end = 0
    for j in range(lengths.shape[1]):
        end = end + lengths[h, j]
        segment = segment + (position >= end).astype(jnp.int32)
        following = following + (position + 1 >= end).astype(jnp.int32)
    live_s[...] = ((following == segment) & (position + 1 < row_length)).astype(F32).astype(BF)
    spare = lax.rem(lax.broadcasted_iota(jnp.int32, (row_length, 128), 1), 64)
    coded, hit = spare < lengths.shape[1], segment == spare
    qe_s[...] = jnp.where(coded & hit, BIG, 0.0).astype(BF)
    ke_s[...] = jnp.where(coded, jnp.where(hit, 0.0, -BIG), jnp.where(spare < 7, 1.0, 0.0)).astype(BF)

    def project(i):
        rows = at(i, ROWS)
        x = row_s[rows, :]
        q_s[rows, :] = dot(x, qkv_s[0]).astype(BF) * jnp.asarray(0.125, BF)
        k_s[rows, :] = dot(x, qkv_s[1]).astype(BF)
        v_s[rows, :] = dot(x, qkv_s[2]).astype(BF)

    wait(own_row, get_w)
    loop(blocks // 2, project)
    send_row.wait()
    start(send_memory, send_cot)
    loop(blocks, project, blocks // 2)
    pairs = ((row_s.at[upper], row_came), (q_s, q), (k_s, k), (v_s, v), (qe_s, qe), (ke_s, ke), (live_s, live))
    outward = [moves.copy(src, dst) for src, dst in pairs]
    start(*outward, *late)
    attend(q_s, k_s, v_s, qe_s, ke_s, mix_s, ext_s, kx_s, vx_s, {})
    mixed = [moves.copy(mix_s, mix), moves.copy(ext_s, ext)]
    start(*mixed)
    wait(*late)
    by_block = [moves.blocks(src, dst, blocks) for src, dst in ((normed_s, normed), (inverse_s, inverse), (cq_s, cq))]

    def after(i):
        rows = at(i, ROWS)
        n, s = normalise(row_s[rows, :].astype(F32) + dot(mix_s[rows, :], out_s[...]))
        normed_s[rows, :] = n
        inverse_s[rows, :] = s
        low = (n * gain[0:1, :] + bias[0:1, :]).astype(BF)
        cq_s[rows, :] = dot(low, cqw_s[...]).astype(BF) * jnp.asarray(0.125, BF)
        start(*[copy(i) for copy in by_block])

    loop(blocks, after)
    wait(*outward, *mixed)
    loop(blocks, lambda i: wait(*[copy(i) for copy in by_block]))
    wait(send_memory, send_cot)


def cross_fwd_kernel(
    deep, out_cot, slot_cot, memory, memory_came, kv_w, cq, qe, ke, out_w, normed_one, slot_mask, gain, bias,
    cot_came, slot_own, slot_came, k, v, mix, ext, normed, inverse,
    memory_s, kv_s, cq_s, qe_s, ke_s, out_s, first_s, k_s, v_s, mix_s, ext_s, normed_s, inverse_s, kx_s, vx_s, masked, sem, sem_far,
):
    place = Place(deep)
    h = place.h
    half = out_cot.shape[1]
    place.greet("dh")
    moves = Moves(sem)
    blocks = memory_s.shape[0] // ROWS
    get_slots = moves.copy(slot_cot, masked)
    get_memory = [moves.copy(memory.at[h], memory_s.at[pl.ds(0, half)]), moves.copy(memory_came, memory_s.at[pl.ds(half, half)])]
    get_w = moves.copy(kv_w.at[pl.ds(1, 2)], kv_s)
    soon = [moves.copy(src, dst) for src, dst in ((cq, cq_s), (qe, qe_s), (ke, ke_s))]
    late = [moves.copy(src, dst) for src, dst in ((out_w, out_s), (normed_one, first_s))]
    partner = place.device(dh=1)
    rest = out_cot.at[1 - h, pl.ds(half // 2, half // 2)]
    sends = [
        remote(rest, cot_came, sem_far.at[0], sem_far.at[1], partner), remote(masked.at[1 - h], slot_came, sem_far.at[2], sem_far.at[3], partner)
    ]
    start(get_w, get_slots, *get_memory, *soon)
    wait(get_w, *get_memory)

    def project(i):
        rows = at(i, ROWS)
        x = memory_s[rows, :]
        k_s[rows, :] = dot(x, kv_s[0]).astype(BF)
        v_s[rows, :] = dot(x, kv_s[1]).astype(BF)

    place.met()
    sends[0].start()
    get_slots.wait()
    columns = slot_mask[...].astype(F32).T
    for r in range(2):
        masked[r] = masked[r] * columns[:, r : r + 1].astype(BF)
    sends[1].start()
    loop(blocks, project)
    outward = [moves.copy(k_s, k), moves.copy(v_s, v), moves.copy(masked.at[h], slot_own)]
    wait(*soon)
    start(*outward, *late)
    attend(cq_s, k_s, v_s, qe_s, ke_s, mix_s, ext_s, kx_s, vx_s, {})
    mixed = [moves.copy(mix_s, mix), moves.copy(ext_s, ext)]
    start(*mixed)
    wait(*late)
    by_block = [moves.blocks(src, dst, blocks) for src, dst in ((normed_s, normed), (inverse_s, inverse))]

    def after(i):
        rows = at(i, ROWS)
        before = first_s[rows, :] * gain[0:1, :] + bias[0:1, :]
        n, s = normalise(before + dot(mix_s[rows, :], out_s[...]))
        normed_s[rows, :] = n
        inverse_s[rows, :] = s
        start(*[copy(i) for copy in by_block])

    loop(blocks, after)
    wait(*outward, *mixed)
    loop(blocks, lambda i: wait(*[copy(i) for copy in by_block]))
    wait(*sends)


def ffn_kernel(
    deep, normed_two, in_w, out_w, slot_w, slot_own, slot_came, out_cot, cot_first, cot_second, live, inverse_two, cross_out_w, cross_mix,
    gain, bias,
    out_home, slots_home, res_two, grad_mix, sum_out, sum_slot, sum_in, sums,
    two_s, inw_s, outw_s, slotw_s, slot_s, cot_s, live_s, inverse_two_s, crossw_s, mix_s,
    low_s, hidden_s, slope_s, normed_s, inverse_s, pair_s, next_s, gnext_s, res_s, ginner_s, res_two_s, res_low_s, gmix_s, slots_s,
    g_out, g_slot, g_in, own_out, own_slot, own_in, came_out, sem_out, came_slot, sem_slot, came_in, sem_in,
    kept_slot, hop_slot, plane_sem, sem, sem_far,
):
    row_length, width = low_s.shape
    blocks = row_length // ROWS
    units = in_w.shape[1]
    half = row_length // 2
    place = Place(deep)
    place.greet("dh", "dcore", "dy")
    h = place.h
    scale = 0.7978845608028654
    moves = Moves(sem)
    get_two = moves.blocks(normed_two, two_s, blocks)
    first = [moves.copy(in_w, inw_s), moves.copy(out_w, outw_s)]
    lower, upper, quarter = pl.ds(0, half), pl.ds(half, half), half // 2
    soon = [
        moves.copy(src, dst)
        for src, dst in ((slot_w, slotw_s), (slot_own, slot_s.at[lower]), (slot_came, slot_s.at[upper]), (live, live_s))
    ]
    late = [
        moves.copy(src, dst)
        for src, dst in ((out_cot.at[h], cot_s.at[lower]), (cot_first, cot_s.at[pl.ds(half, quarter)]),
                         (cot_second, cot_s.at[pl.ds(half + quarter, quarter)]), (inverse_two, inverse_two_s), (cross_out_w, crossw_s), (cross_mix, mix_s))
    ]
    work_out = CoreSum(place, g_out, own_out, came_out, sem_out)
    work_slot = CoreSum(place, g_slot, own_slot, came_slot, sem_slot)
    work_in = CoreSum(place, g_in, own_in, came_in, sem_in)
    plane_slot = Plane(place, own_slot, kept_slot, hop_slot, None, None, plane_sem, False)

    def home(src, dst, i):
        lanes = pl.ds(0, width)
        return (
            moves.copy(src.at[lower, lanes], dst.at[h]),
            remote(src.at[upper, lanes], dst.at[h], sem_far.at[2 * i], sem_far.at[2 * i + 1], place.device(dh=1)),
        )

    homeward = home(pair_s, out_home, 0) + home(slots_s, slots_home, 1)
    last = blocks - 1
    get_two(last).start()
    start(*first)
    loop(last, lambda i: get_two(i).start())
    start(*soon, *late)
    wait(*first)

    def forward(i):
        rows = at(i, ROWS)
        get_two(i).wait()
        after_cross = two_s[rows, :] * gain[1:2, :] + bias[1:2, :]
        low = after_cross.astype(BF)
        low_s[rows, :] = low
        for c in range(units // 512):
            cols = slice(c * 512, (c + 1) * 512)
            inner = dot(low, inw_s[:, cols])
            square = inner * inner
            bent = jnp.tanh(inner * (scale + (scale * 0.044715) * square))
            part = 0.5 + 0.5 * bent
            hidden_s[rows, cols] = (inner * part).astype(BF)
            slope = part + inner * (0.5 - 0.5 * bent * bent) * (scale + (3 * scale * 0.044715) * square)
            slope_s[rows, cols] = slope.astype(BF)
        n, s = normalise(after_cross + dot(hidden_s[rows, :], outw_s[...]))
        normed_s[rows, :] = n
        inverse_s[rows, :] = s
        final = (n * gain[2:3, :] + bias[2:3, :]).astype(BF)
        pair_s[rows, :width] = final
        next_s[rows, :] = final.astype(F32)

    def backwards(body, sent):
        def one(i):
            body(last - i)
            pl.when(i == (blocks - 1) // 2)(sent)

        loop(blocks, one)

    def out_ready():
        place.met()
        homeward[1].start()

    backwards(forward, out_ready)
    homeward[0].start()
    next_s[pl.ds(row_length, 8), :] = next_s[pl.ds(0, 8), :]
    wait(*soon)

    def slot(i):
        rows = at(i, ROWS)
        window = pl.ds(pl.multiple_of(i * ROWS, ROWS), ROWS + 8)
        alive = live_s[rows, 0:1].astype(F32)
        pair_s[rows, width:] = (next_s[window, :][1 : ROWS + 1] * alive).astype(BF)
        slots_s[rows, :] = dot(pair_s[rows, :], slotw_s[...]).astype(BF)
        back = (dot_nt(slot_s[rows, :], slotw_s[width:, :]) * alive).astype(BF)
        gnext_s[pl.ds(pl.multiple_of(i * ROWS + 8, 8), ROWS), :] = back.astype(F32)

    backwards(slot, lambda: homeward[3].start())
    homeward[2].start()
    gnext_s[pl.ds(0, 8), :] = gnext_s[pl.ds(row_length, 8), :]
    sums[...] = jnp.zeros(sums.shape, F32)
    fill(g_slot, width)
    for side in range(2):
        g_slot[side, :width, :] = dot_tn(pair_s[:, side * width : (side + 1) * width], slot_s[...]).astype(BF)
    work_slot.begin()
    wait(*late)
    by_block = [moves.blocks(src, dst, blocks) for src, dst in ((res_two_s, res_two), (gmix_s, grad_mix))]

    def backward(i):
        @pl.when(i == 1)
        def slot_hop():
            work_slot.finish()
            plane_slot.begin_a()

        rows = at(i, ROWS)
        window = pl.ds(pl.multiple_of(i * ROWS, ROWS), ROWS + 8)
        gradient = (
            cot_s[rows, :].astype(F32)
            + dot_nt(slot_s[rows, :], slotw_s[:width, :])
            + gnext_s[window, :][7 : ROWS + 7]
        )
        n = normed_s[rows, :]
        sums[0:1, :] += jnp.sum(gradient * n, axis=0, keepdims=True)
        sums[1:2, :] += jnp.sum(gradient, axis=0, keepdims=True)
        res = norm_back(gradient, n, inverse_s[rows, :], gain[2:3, :])
        res_low = res.astype(BF)
        res_s[rows, :] = res_low
        for c in range(units // 512):
            cols = slice(c * 512, (c + 1) * 512)
            ginner_s[rows, cols] = (dot_nt(res_low, outw_s[cols, :]) * slope_s[rows, cols].astype(F32)).astype(BF)
        res = res + dot_nt(ginner_s[rows, :], inw_s[...])
        n = two_s[rows, :]
        sums[2:3, :] += jnp.sum(res * n, axis=0, keepdims=True)
        sums[3:4, :] += jnp.sum(res, axis=0, keepdims=True)
        res = norm_back(res, n, inverse_two_s[rows, :], gain[1:2, :])
        res_two_s[rows, :] = res
        res_low = res.astype(BF)
        res_low_s[rows, :] = res_low
        gmix_s[rows, :] = dot_nt(res_low, crossw_s[...]).astype(BF)
        start(*[copy(i) for copy in by_block])

    loop(blocks, backward)
    fill(g_out, units // 2 + width // 2)
    fill(g_in, width * units // 1024)
    for side in range(2):
        g_out[side, units // 2 : units // 2 + width // 2, :] = dot_tn(
            mix_s[:, side * 256 : (side + 1) * 256], res_low_s[...]
        ).astype(BF)
    for side in range(2):
        g_out[side, : units // 2, :] = dot_tn(hidden_s[:, side * (units // 2) : (side + 1) * (units // 2)], res_s[...]).astype(BF)
    work_out.begin()
    for c in range(units // 512):
        side, block = divmod(c, units // 1024)
        g_in[side, block * width : (block + 1) * width, :] = dot_tn(low_s[...], ginner_s[:, c * 512 : (c + 1) * 512]).astype(BF)
    work_in.begin()
    done = [moves.copy(src, dst) for src, dst in ((own_out, sum_out), (kept_slot, sum_slot), (own_in, sum_in))]
    for finish, copy in zip((work_out.finish, plane_slot.finish_a, work_in.finish), done):
        finish()
        copy.start()
    loop(blocks, lambda i: wait(*[copy(i) for copy in by_block]))
    wait(*done, *homeward)


def fill(grads, used):
    rest = grads.shape[1] - used
    if rest:
        grads[:, used:, :] = jnp.zeros((grads.shape[0], rest, grads.shape[2]), BF)


def weight_grads(grads, pairs, sources):
    for left, rights, first in sources:
        right = jnp.concatenate([d[:, p * 128 : (p + 1) * 128] for d in rights for p in pairs], axis=1)
        width = left.shape[1]
        block = dot_tn(left[...], right).astype(BF)
        for i in range(len(rights)):
            for side in range(len(pairs)):
                lane = (i * len(pairs) + side) * 128
                grads[side, (first + i) * width : (first + i + 1) * width, :] = block[:, lane : lane + 128]


PLAN = {
    "begin": (("out", 0), ("in", 0), ("slot", 0),),
    "c1": (("slot", 1),),
    "c3": (("d1", 0), ("slot", 2),),
    "c4": (("d1", 1), ("slot", 3),),
    "c6": (("slot", 4),),
    "c7": (("d1", 2), ("out", 1), ("in", 1),),
    "c8": (("slot", 5),),
    "c9": (("d2", 0), ("d1", 3),),
    "c10": (("mem", 0),),
    "s0": (("d2", 1), ("d1", 4), ("slot", 6),),
    "s2": (("d1", 5), ("in", 2),),
    "s3": (("e1", 0), ("d2", 2), ("out", 2),),
    "s4": (("e1", 1), ("d1", 6), ("in", 3),),
    "s5": (("e2", 0), ("out", 3),),
    "s6": (("e2", 1), ("d2", 3), ("d1", 7), ("in", 4),),
    "s7": (("e1", 2), ("out", 4),),
    "s8": (("f", 0),),
    "s9": (("d2", 4), ("in", 5), ("row", 0),),
    "s10": (("f", 1), ("e2", 2), ("d1", 8),),
    "tail": (("e1", 3), ("out", 5), ("in", 6), ("d2", 5), ("f", 2), ("e1", 4), ("e2", 3), ("d2", 6), ("e1", 5), ("out", 6),
        ("e2", 4), ("f", 3), ("in", 7), ("d2", 7), ("e2", 5), ("e1", 6), ("f", 4), ("e2", 6), ("f", 5), ("e1", 7), ("e2", 7),
        ("f", 6), ("f", 7), ("d2", 8), ("out", 7), ("e1", 8), ("e2", 8), ("f", 8), ("out", 8), ("in", 8), ("slot", 7),
        ("d1", 9), ("d2", 9), ("e1", 9), ("e2", 9), ("row", 1), ("mem", 1), ("f", 9),),
}


def back_kernel(
    deep, own_out, own_in, own_slot, cq, ck, cv, cext, cmix, gcmix, memory, memory_came, cross_w, res_two, normed_one, inverse_one,
    q, k, v, ext, mix, out_w, tokens, tokens_came, self_w, ke, gain, bias, sums_two,
    done_out, done_in, done_slot, done_d1, done_d2, done_e, done_f, mem_mine, mem_came, row_mine, row_came,
    q_s, k_s, v_s, ext_s, mix_s, gmix_s, memory_s, row_s, low_s, dq_s, dk_s, dv_s, res_s, cross_ws, self_ws, outw_s,
    res_two_s, normed_s, res_one_s, inverse_s, sums, mine_s, theirs_s, row_theirs,
    kx_s, vx_s, qx_s, dx_s, kt_s, dqt_s, sem, sem_far, *comm,
):
    row_length, width = row_s.shape
    blocks = row_length // ROWS
    half_blocks = blocks // 2
    half = row_length // 2
    lower, upper = pl.ds(0, half), pl.ds(half, half)
    place = Place(deep)
    place.greet("dh", "dy", "dz", "dcore")
    moves = Moves(sem)
    cross_pairs = moves.pairs((cq, ck, cv, cext, cmix, gcmix), (q_s, k_s, v_s, ext_s, mix_s, gmix_s))
    late = [
        moves.copy(src, dst)
        for src, dst in ((normed_one, normed_s), (memory.at[place.h], memory_s.at[lower]), (memory_came, memory_s.at[upper]),
                         (cross_w, cross_ws), (inverse_one, inverse_s), (res_two, res_two_s), (out_w, outw_s),
                         (tokens.at[place.h], row_s.at[lower]), (tokens_came, row_s.at[upper]), (self_w, self_ws))
    ]
    again = [moves.copy(src, dst) for src, dst in ((q, q_s), (k, k_s), (v, v_s), (ext, ext_s), (mix, mix_s))]
    loop(HEADS // 2, lambda i: start(*cross_pairs(i)))
    comm = list(comm)
    take = lambda n: [comm.pop(0) for _ in range(n)]
    get_slot = moves.copy(own_slot, comm[18])
    get_slot.start()
    chains = {
        "out": chain(place, "own", take(9), done_out, False, own=own_out),
        "in": chain(place, "own", take(9), done_in, False, own=own_in),
        "slot": chain(place, "kept", take(9), done_slot, False),
    }
    grads = {}
    for name, done, x_first, side in (("d1", done_d1, True, None), ("d2", done_d2, False, None), ("e1", done_e, False, None),
                                      ("e2", done_f, False, 0), ("f", done_f, False, 1)):
        buffers = take(13)
        grads[name] = buffers[0]
        chains[name] = chain(place, None, buffers, done, x_first, side)
    mem_send = remote(theirs_s, mem_came, sem_far.at[0], sem_far.at[1], place.device(dh=1))
    row_send = remote(row_theirs, row_came, sem_far.at[2], sem_far.at[3], place.device(dh=1))
    chains["mem"] = [mem_send.start, mem_send.wait]
    chains["row"] = [row_send.start, row_send.wait]

    def run(point):
        for name, stage in PLAN.get(point, ()):
            chains[name][stage]()

    def hooks(letter, extra):
        table = {}
        for step in range(HEADS):
            point = letter + str(step)
            if step in extra or point in PLAN:
                def hook(point=point, step=step):
                    if step in extra:
                        extra[step]()
                    run(point)

                table[step] = hook
        return table

    def low_rows():
        wait(*late)

        def one(i):
            rows = at(i, ROWS)
            low_s[rows, :] = (normed_s[rows, :] * gain[0:1, :] + bias[0:1, :]).astype(BF)

        loop(blocks, one)

    cross_sources = ((low_s, (dq_s,), 0), (memory_s, (dk_s, dv_s), 1))
    self_sources = ((row_s, (dq_s, dk_s, dv_s), 0),)
    for name, used in (("d1", 3 * width), ("d2", 5 * width), ("e1", 3 * width + 16), ("e2", 3 * width), ("f", 3 * width)):
        fill(grads[name], used)
    place.met()
    get_slot.wait()
    run("begin")
    start(*late)
    scratch = (dq_s, dk_s, dv_s, kx_s, vx_s, qx_s, dx_s, kt_s, dqt_s)
    attend_back(
        q_s, k_s, v_s, ext_s, ke, mix_s, gmix_s, *scratch,
        hooks("c", {1: low_rows, 3: lambda: weight_grads(grads["d1"], (0, 2), cross_sources)}), cross_pairs,
    )
    start(*again)
    sums[...] = jnp.zeros(sums.shape, F32)

    def backward(i):
        rows = at(i, ROWS)
        n = normed_s[rows, :]
        gradient = res_two_s[rows, :] + dot_nt(dq_s[rows, :], cross_ws[0])
        sums[0:1, :] += jnp.sum(gradient * n, axis=0, keepdims=True)
        sums[1:2, :] += jnp.sum(gradient, axis=0, keepdims=True)
        res = norm_back(gradient, n, inverse_s[rows, :], gain[0:1, :])
        res_one_s[rows, :] = res
        res_low = res.astype(BF)
        res_s[rows, :] = res_low
        gmix_s[rows, :] = dot_nt(res_low, outw_s[...]).astype(BF)

    loop(blocks, backward)
    run("c8")
    weight_grads(grads["d2"], (1, 3), cross_sources)
    wait(*again)
    for side in range(2):
        block = dot_tn(mix_s[:, side * 256 : (side + 1) * 256], res_s[...]).astype(BF)
        for c in range(width // 128):
            grads["d2"][side, 3 * width + c * 256 : 3 * width + (c + 1) * 256, :] = block[:, c * 128 : (c + 1) * 128]
    run("c9")
    put_mem = moves.blocks(mine_s, mem_mine, half_blocks)
    put_row = moves.blocks(mine_s, row_mine, half_blocks)

    def memory_grad(i):
        rows = at(i, ROWS)
        return dot_nt(dk_s[rows, :], cross_ws[1]) + dot_nt(dv_s[rows, :], cross_ws[2])

    def memory_theirs(i):
        theirs_s[at(i, ROWS), :] = memory_grad(i + half_blocks).astype(BF)

    def memory_mine(i):
        mine_s[at(i, ROWS), :] = memory_grad(i)
        put_mem(i).start()

    loop(half_blocks, memory_theirs)
    run("c10")
    loop(half_blocks, memory_mine)

    def first_grads():
        weight_grads(grads["e1"], (0, 2), self_sources)
        norms = jnp.concatenate(
            [sums[0:1, :], sums_two[2:3, :], sums_two[0:1, :], sums[1:2, :], sums_two[3:4, :], sums_two[1:2, :]], axis=0
        ).astype(BF)
        for side in range(2):
            parts = [norms[:, side * 256 + c * 128 : side * 256 + (c + 1) * 128] for c in range(2)]
            grads["e1"][side, 3 * width : 3 * width + 16, :] = jnp.concatenate(parts + [jnp.zeros((4, 128), BF)], axis=0)

    attend_back(
        q_s, k_s, v_s, ext_s, ke, mix_s, gmix_s, *scratch,
        hooks("s", {3: first_grads, 5: lambda: weight_grads(grads["e2"], (1,), self_sources)}), lambda i: (),
    )
    weight_grads(grads["f"], (3,), self_sources)
    run("s8")

    def row_grad(i):
        rows = at(i, ROWS)
        return (
            res_one_s[rows, :] + dot_nt(dq_s[rows, :], self_ws[0]) + dot_nt(dk_s[rows, :], self_ws[1]) + dot_nt(dv_s[rows, :], self_ws[2])
        )

    def row_other(i):
        row_theirs[at(i, ROWS), :] = row_grad(i + half_blocks).astype(BF)

    def row_own(i):
        put_mem(i).wait()
        mine_s[at(i, ROWS), :] = row_grad(i)
        put_row(i).start()

    loop(half_blocks, row_other)
    run("s9")
    loop(half_blocks, row_own)
    run("s10")
    run("tail")
    loop(half_blocks, lambda i: put_row(i).wait())


def finish_kernel(
    deep, out, slots, row_mine, row_came, mem_mine, mem_came, done_in, done_out, done_slot, done_d1, done_d2, done_e, done_f, slot_mask,
    out_f, slots_f, tokens_f, memory_f, self_qkv_f, self_out_f, cross_qkv_f, cross_out_f, gain_f, bias_f, ffn_in_f, ffn_out_f, slot_f,
    slots_s, row_s, mem_s, in_s, outs_s, slot_s, d1_s, d2_s, e_s, f_s, masked_s, row_w, mem_w, in_w, out_w, slot_w, cross_w,
    cqkv_w, sout_w, sqkv_w, out_b, mem_b, row_b, sem,
):
    h = lax.axis_index("head")
    moves = Moves(sem)
    width = out.shape[2]
    loads = [
        moves.copy(src, dst)
        for src, dst in ((done_out, outs_s), (done_in, in_s), (done_slot, slot_s), (slots, slots_s), (mem_came, mem_s), (done_d1, d1_s),
                         (done_d2, d2_s), (row_came, row_s), (done_e, e_s), (done_f, f_s), (out, out_b), (mem_mine, mem_b), (row_mine, row_b))
    ]
    start(*loads)
    stores = []

    def put(src, dst):
        copy = moves.copy(src, dst)
        copy.start()
        stores.append(copy)

    half = out_w.shape[0]
    loads[0].wait()
    out_w[...] = outs_s[:half, :].astype(F32)
    put(out_w, ffn_out_f)
    loads[1].wait()
    for c in range(in_w.shape[1] // 512):
        in_w[:, c * 512 : (c + 1) * 512] = in_s[c * width : (c + 1) * width, :].astype(F32)
    put(in_w, ffn_in_f)
    cross_w[...] = outs_s[half : half + width // 2, :].astype(F32)
    put(cross_w, cross_out_f)
    loads[2].wait()
    slot_w[...] = slot_s[:width, :].astype(F32)
    put(slot_w, slot_f)
    loads[3].wait()
    columns = slot_mask[...].astype(F32).T
    for r in range(2):
        masked_s[r] = slots_s[r] * columns[:, r : r + 1].astype(BF)
    put(masked_s, slots_f)
    loads[4].wait()
    mem_w[...] = mem_s[...].astype(F32)
    put(mem_w, memory_f.at[1 - h])
    wait(loads[5], loads[6])
    for c, part_s in enumerate((d1_s, d2_s)):
        for part in range(3):
            cqkv_w[part, :, c * 128 : (c + 1) * 128] = part_s[part * width : (part + 1) * width, :].astype(F32)
    put(cqkv_w, cross_qkv_f)
    for c in range(width // 128):
        sout_w[:, c * 128 : (c + 1) * 128] = d2_s[3 * width + c * 256 : 3 * width + (c + 1) * 256, :].astype(F32)
    put(sout_w, self_out_f)
    loads[7].wait()
    row_w[...] = row_s[...].astype(F32)
    put(row_w, tokens_f.at[1 - h])
    wait(loads[8], loads[9])
    for c, part_s in enumerate((e_s, f_s)):
        for part in range(3):
            sqkv_w[part, :, c * 128 : (c + 1) * 128] = part_s[part * width : (part + 1) * width, :].astype(F32)
    norms = e_s[3 * width : 3 * width + 16, :].astype(F32)
    for c in range(2):
        gain_f[:, c * 128 : (c + 1) * 128] = norms[6 * c : 6 * c + 3]
        bias_f[:, c * 128 : (c + 1) * 128] = norms[6 * c + 3 : 6 * c + 6]
    put(sqkv_w, self_qkv_f)
    for load, src, dst in zip(loads[10:], (out_b, mem_b, row_b), (out_f, memory_f.at[h], tokens_f.at[h])):
        load.wait()
        put(src, dst)
    wait(*stores)


def call(kernel, name, cid, args, outs, scratch, flops):
    if cid is None:
        params = pltpu.CompilerParams(vmem_limit_bytes=VMEM)
    else:
        params = pltpu.CompilerParams(collective_id=cid, has_side_effects=True, vmem_limit_bytes=VMEM)
    return pl.pallas_call(
        kernel,
        out_shape=[jax.ShapeDtypeStruct(shape, kind) for shape, kind, _ in outs],
        in_specs=[spec for _, spec in args],
        out_specs=[spec for _, _, spec in outs],
        scratch_shapes=scratch,
        compiler_params=params,
        cost_estimate=pl.CostEstimate(flops=flops, bytes_accessed=2**20, transcendentals=0),
        name=name,
    )(*[arg for arg, _ in args])


def padded(count, unit):
    return -(-count // unit) * unit


def per_device(
    tokens, memory, lengths, slot_mask, self_qkv, self_out, cross_qkv, cross_out,
    norm_gain, norm_bias, ffn_in, ffn_out, slot_proj, out_cot, slot_cot,
):
    local_len, width = tokens.shape[1:]
    units = ffn_in.shape[1]
    deep = lax.axis_size("dp") // 4
    row_length = 2 * local_len
    unit = 64 * deep
    rows_out, rows_slot, rows_in = padded(units // 2 + width // 2, unit), padded(width, unit), padded(width * units // 1024, unit)
    rows_d1, rows_d2, rows_e = padded(3 * width, unit), padded(5 * width, unit), padded(3 * width + 16, unit)
    dense = 2 * row_length * width * width
    scores = 2 * row_length * row_length * width

    def inner(*values):
        return [(value, INNER) for value in values]

    def outer(*values):
        return [(value, ANY) for value in values]

    def new(*shape, kind=BF, spec=INNER):
        return (shape, kind, spec)

    def scratch(*shape, kind=BF):
        return pltpu.VMEM(shape, kind)

    row, wide, column = (
        new(row_length, width, spec=ANY), new(row_length, width, kind=F32, spec=ANY), new(row_length, 1, kind=F32, spec=ANY)
    )
    small = new(row_length, 128, spec=ANY)
    row_s, wide_s, two_s = scratch(row_length, width), scratch(row_length, width, kind=F32), scratch(row_length, 256)
    tall_s, ring_s = scratch(row_length, units), scratch(row_length + 8, width, kind=F32)
    column_s, small_s, half_s = scratch(row_length, 1, kind=F32), scratch(row_length, 128), scratch(local_len, width)
    square_s, three_s = scratch(width, width), scratch(3, width, width)
    half_wide_s = scratch(local_len, width, kind=F32)

    half, part = new(local_len, width, spec=ANY), new(local_len // 2, width, spec=ANY)
    tokens_came, memory_came, cot_first, q, k, v, mix, ext, normed_one, inverse_one, cq, qe, ke, live = call(
        functools.partial(self_fwd_kernel, deep), "self_fwd", 0,
        outer(tokens, memory, out_cot, self_qkv, self_out, cross_qkv) + [(lengths, SCALARS)] + inner(norm_gain, norm_bias),
        [half, half, part] + [row] * 5 + [wide, column, row] + [small] * 3,
        [row_s, three_s, square_s, square_s] + [row_s] * 5 + [wide_s, column_s, row_s]
        + [small_s] * 3 + [two_s, two_s, DMA((40,)), DMA((6,))], 5 * dense + 8 * scores,
    )
    cot_second, slot_own, slot_came, ck, cv, cmix, cext, normed_two, inverse_two = call(
        functools.partial(cross_fwd_kernel, deep), "cross_fwd", 1,
        outer(out_cot, slot_cot, memory, memory_came, cross_qkv, cq, qe, ke, cross_out, normed_one) + inner(slot_mask, norm_gain, norm_bias),
        [part, half, half] + [row] * 4 + [wide, column],
        [row_s, scratch(2, width, width), row_s, small_s, small_s, square_s, wide_s] + [row_s] * 4 + [wide_s, column_s]
        + [two_s, two_s, scratch(2, local_len, width), DMA((40,)), DMA((4,))], 3 * dense + 8 * scores,
    )
    home = new(2, local_len, width, spec=ANY)
    groups = ((rows_out, 512), (rows_slot, 512), (rows_in, 512))
    out, slots, res_two, grad_cmix, sum_out, sum_slot, sum_in, sums_two = call(
        functools.partial(ffn_kernel, deep), "ffn", 2,
        outer(normed_two, ffn_in, ffn_out, slot_proj, slot_own, slot_came, out_cot, cot_first, cot_second, live, inverse_two, cross_out, cmix) + inner(norm_gain, norm_bias),
        [home, home, wide, row, new(2, 2, rows_out // 4, 512, spec=ANY), new(2, rows_slot // 4, 512, spec=ANY),
         new(2, 2, rows_in // 4, 512, spec=ANY), new(8, width, kind=F32)],
        [wide_s, scratch(width, units), scratch(units, width), scratch(2 * width, width), row_s, row_s, small_s, column_s, square_s, row_s]
        + [row_s, tall_s, tall_s, wide_s, column_s, scratch(row_length, 2 * width), ring_s, ring_s, row_s, tall_s, wide_s]
        + [row_s] * 3
        + [scratch(2, rows, lanes) for rows, lanes in groups] + [scratch(2, 2, rows // 4, lanes) for rows, lanes in groups]
        + [part for group in groups for part in CoreSum.scratch(*group)]
        + [scratch(2, rows_slot // 4, 512), scratch(2, rows_slot // 4, 512), DMA((5,)), DMA((40,)), DMA((4,))], 32 * dense,
    )
    back = [small_s] * 4 + [scratch(128, row_length), scratch(128, row_length, kind=F32)]

    half_wide = new(local_len, width, kind=F32, spec=ANY)
    late = ((rows_d1, 128, 2), (rows_d2, 128, 2), (rows_e, 128, 2), (rows_d1, 128, 1), (rows_d1, 128, 1))

    def whole(rows, lanes):
        return new(rows, lanes, spec=ANY)

    done_out, done_in, done_slot, done_d1, done_d2, done_e, done_f, mem_mine, mem_came, row_mine, row_came = call(
        functools.partial(back_kernel, deep), "back", 3,
        outer(sum_out, sum_in, sum_slot, cq, ck, cv, cext, cmix, grad_cmix, memory, memory_came, cross_qkv, res_two, normed_one,
              inverse_one, q, k, v, ext, mix, self_out, tokens, tokens_came, self_qkv) + inner(ke, norm_gain, norm_bias, sums_two),
        [whole(rows_out, 512), whole(rows_in, 512), whole(rows_slot, 512), whole(rows_d1, 128), whole(rows_d2, 128), whole(rows_e, 128),
         whole(rows_d1, 128), half_wide, half, half_wide, half],
        [row_s] * 13 + [three_s, three_s, square_s] + [wide_s] * 3 + [column_s, scratch(8, width, kind=F32), half_wide_s, half_s, half_s]
        + back + [DMA((60,)), DMA((4,))]
        + [part for rows in (rows_out, rows_in, rows_slot) for part in chain_scratch(deep, rows, 512, "own")]
        + [part for rows, lanes, sides in late for part in chain_scratch(deep, rows, lanes, None, sides)],
        22 * dense + 40 * scores,
    )

    def final(*shape, kind=F32):
        return new(*shape, kind=kind, spec=ANY)

    def wide_scratch(*shape):
        return scratch(*shape, kind=F32)

    pair_s = scratch(2, local_len, width)
    return tuple(call(
        functools.partial(finish_kernel, deep), "finish", None,
        outer(out, slots, row_mine, row_came, mem_mine, mem_came, done_in, done_out, done_slot, done_d1, done_d2, done_e, done_f)
        + inner(slot_mask),
        [final(2, local_len, width, kind=BF)] * 2 + [final(2, local_len, width)] * 2
        + [final(3, width, 256), final(width // 2, width), final(3, width, 256), final(width // 2, width)]
        + [new(3, 256, kind=F32)] * 2 + [final(width, units // 2), final(units // 2, width), final(width, width)],
        [pair_s, half_s, half_s, scratch(rows_in, 512), scratch(rows_out, 512), scratch(rows_slot, 512), scratch(rows_d1, 128),
         scratch(rows_d2, 128), scratch(rows_e, 128), scratch(rows_d1, 128), pair_s, half_wide_s, half_wide_s, wide_scratch(width, units // 2),
         wide_scratch(units // 2, width), wide_scratch(width, width), wide_scratch(width // 2, width), wide_scratch(3, width, 256),
         wide_scratch(width // 2, width), wide_scratch(3, width, 256), pair_s, half_wide_s, half_wide_s, DMA((40,))], 0,
    ))


def solution(mesh):
    split = P("dp", "head", None)
    placed = (split, split, P("dp", None), P("dp", "head")) + (P(),) * 9 + (split, split)
    return jax.shard_map(
        per_device,
        mesh=mesh,
        in_specs=placed,
        out_specs=(
            split, split, split, split,
            P(None, None, "head"), P("head", None), P(None, None, "head"), P("head", None),
            P(None, "head"), P(None, "head"), P(None, "head"), P("head", None), P("head", None),
        ),
        check_vma=False,
    )
```

```python
import functools

import jax
import jax.numpy as jnp
from jax import lax
from jax.experimental import pallas as pl
from jax.experimental.pallas import tpu as pltpu
from jax.sharding import PartitionSpec as P

HEADS = 8
BF = jnp.bfloat16
F32 = jnp.float32
MESH = pl.DeviceIdType.MESH
NT = (((1,), (1,)), ((), ()))
TN = (((0,), (0,)), ((), ()))
BIG = 2.0**20
VMEM = 60 * 2**20
ROWS = 512
QBLOCK = 512
ANY = pl.BlockSpec(memory_space=pl.ANY)
INNER = pl.BlockSpec(memory_space=pltpu.VMEM)
SCALARS = pl.BlockSpec(memory_space=pltpu.SMEM)


def dot(a, b):
    return jnp.dot(a, b, preferred_element_type=F32)


def dot_nt(a, b):
    return lax.dot_general(a, b, NT, preferred_element_type=F32)


def dot_tn(a, b):
    return lax.dot_general(a, b, TN, preferred_element_type=F32)


def at(i, size):
    return pl.ds(pl.multiple_of(i * size, size), size)


def loop(count, body, first=0):
    def step(i, carry):
        body(i)
        return carry

    lax.fori_loop(first, count, step, 0)


def thirds(value):
    first = value.astype(BF)
    rest = value - first.astype(F32)
    second = rest.astype(BF)
    third = (rest - second.astype(F32)).astype(BF)
    return first, second, third


def normalise(value):
    average = jnp.mean(value, axis=-1, keepdims=True)
    centred = value - average
    inverse = lax.rsqrt(jnp.mean(centred * centred, axis=-1, keepdims=True) + 1e-05)
    return centred * inverse, inverse


def norm_back(gradient, normed, inverse, gain_row):
    scaled = gradient * gain_row
    inner_mean = jnp.mean(scaled, axis=-1, keepdims=True)
    cross_mean = jnp.mean(scaled * normed, axis=-1, keepdims=True)
    return inverse * (scaled - inner_mean - normed * cross_mean)


def run_hooks(hooks, step):
    for done, hook in hooks.items():
        if done >= 0:
            pl.when(step == done)(hook)


def attend(q_s, k_s, v_s, qe_ref, ke_ref, mix_s, ext_s, kx_s, vx_s):
    row_length = k_s.shape[0]
    block = 256
    wide_low = lax.broadcasted_iota(jnp.int32, (row_length, 128), 1) < 64
    lane = lax.broadcasted_iota(jnp.int32, (block, 128), 1)
    low = lane < 64
    spare = lax.rem(lane, 64)

    def pair(p):
        lanes = at(p, 128)
        parts = [slice(h * 128, (h + 1) * 128) for h in range(2)]
        for h in range(2):
            mine = wide_low if h == 0 else ~wide_low
            kx_s[:, parts[h]] = jnp.where(mine, k_s[:, lanes], ke_ref[...])
            vx_s[:, parts[h]] = jnp.where(mine, v_s[:, lanes], jnp.ones((), BF))

        def rows_of(t):
            return slice((t // 2) * block, (t // 2 + 1) * block)

        def scores_of(t):
            rows = rows_of(t)
            query = jnp.where(low if t % 2 == 0 else ~low, q_s[rows, lanes], qe_ref[rows, :])
            return dot_nt(query, kx_s[:, parts[t % 2]])

        many = 2 * (row_length // block)
        ahead, done = scores_of(0), []
        for t in range(many):
            scores = ahead
            if t + 1 < many:
                ahead = scores_of(t + 1)
            top = jnp.max(scores, axis=1, keepdims=True)
            probs = jnp.exp(scores - top).astype(BF)
            done.append((top, dot(probs, vx_s[:, parts[t % 2]])))
            if t % 2 == 1:
                rows = rows_of(t)
                (top_low, sum_low), (top_high, sum_high) = done[-2:]
                mixed = jnp.where(low, sum_low, sum_high)
                totals = jnp.where(low, sum_high, sum_low)
                first, second, third = thirds(jnp.where(low, top_high, top_low) + jnp.log(totals))
                ext_s[rows, lanes] = jnp.where(
                    spare == 4, -first, jnp.where(spare == 5, -second, jnp.where(spare == 6, -third, qe_ref[rows, :]))
                )
                mix_s[rows, lanes] = (mixed / pltpu.roll(totals, 64, 1)).astype(BF)

    loop(HEADS // 2, pair)


def head_pair(i):
    return lax.rem(i, 2) * 2 + lax.div(i, 2)


def attend_back(q_s, k_s, v_s, ext_s, ke_ref, mix_s, gmix_s, dq_s, dk_s, dv_s, kx_s, vx_s, qx_s, dx_s, extra_s, kt_s, dqt_s, hooks, get_pair):
    row_length = k_s.shape[0]
    block = QBLOCK
    lane = lax.broadcasted_iota(jnp.int32, (row_length, 128), 1)
    low = lane < 64
    spare = lax.rem(lane, 64)
    zero = jnp.zeros((), BF)

    def head(step):
        i, odd = lax.div(step, 2), lax.rem(step, 2)
        lanes = at(head_pair(i), 128)
        mine = lax.div(lane, 64) == odd

        @pl.when(odd == 0)
        def arrive():
            for copy in get_pair(i):
                copy.wait()
            product = gmix_s[:, lanes].astype(F32) * mix_s[:, lanes].astype(F32)
            inner_low = jnp.sum(jnp.where(low, product, 0.0), axis=1, keepdims=True)
            inner_high = jnp.sum(jnp.where(low, 0.0, product), axis=1, keepdims=True)
            first, second, third = thirds(jnp.where(low, inner_high, inner_low))
            extra_s[...] = jnp.where(spare == 0, -first, jnp.where(spare == 1, -second, jnp.where(spare == 2, -third, zero)))
            kt_s[...] = k_s[:, lanes].T

        kx_s[...] = jnp.where(mine, k_s[:, lanes], ke_ref[...])
        vx_s[...] = jnp.where(mine, v_s[:, lanes], jnp.ones((), BF))
        qx_s[...] = jnp.where(mine, q_s[:, lanes], ext_s[:, lanes])
        dx_s[...] = jnp.where(mine, gmix_s[:, lanes], extra_s[...])
        own = at(odd, 64)
        for j in range(row_length // block):
            cols = slice(j * block, (j + 1) * block)
            probs = jnp.exp(dot_nt(kx_s[...], qx_s[cols, :]))
            ds = (probs * dot_nt(vx_s[...], dx_s[cols, :])).astype(BF)
            dv = dot(probs.astype(BF), dx_s[cols, :])
            dk = dot(ds, qx_s[cols, :])
            acc_v, acc_k = (dv, dk) if j == 0 else (acc_v + dv, acc_k + dk)
            dqt_s[own, cols] = dot(kt_s[own, :], ds) * 0.125
        dk_s[:, lanes] = jnp.where(mine, acc_k.astype(BF), dk_s[:, lanes])
        dv_s[:, lanes] = jnp.where(mine, acc_v.astype(BF), dv_s[:, lanes])

        @pl.when(odd == 1)
        def turn():
            dq_s[:, lanes] = dqt_s[...].T.astype(BF)

        run_hooks(hooks, step)

    loop(HEADS, head)


class Place:
    def __init__(self, deep):
        dp = lax.axis_index("dp")
        self.deep = deep
        self.h = lax.axis_index("head")
        self.core = lax.rem(dp, 2)
        self.y = lax.rem(lax.div(dp, 2), 2)
        self.z = lax.div(dp, 4)

    def device(self, dh=0, dcore=0, dy=0, dz=None):
        h = 1 - self.h if dh else self.h
        core = 1 - self.core if dcore else self.core
        y = 1 - self.y if dy else self.y
        z = self.z if dz is None else lax.rem(self.z + dz, self.deep)
        return ((z * 2 + y) * 2 + core, h)

    def greet(self, *kinds):
        self.peers = []
        for kind in kinds:
            if kind == "dz":
                self.peers += [self.device(dz=j) for j in range(1, self.deep)]
            else:
                self.peers.append(self.device(**{kind: 1}))
        barrier = pltpu.get_barrier_semaphore()
        for peer in self.peers:
            pl.semaphore_signal(barrier, inc=1, device_id=peer, device_id_type=MESH)

    def met(self):
        pl.semaphore_wait(pltpu.get_barrier_semaphore(), len(self.peers))


def remote(src, dst, send, recv, device):
    return pltpu.make_async_remote_copy(
        src_ref=src, dst_ref=dst, send_sem=send, recv_sem=recv, device_id=device, device_id_type=MESH
    )


DMA = pltpu.SemaphoreType.DMA


class CoreSum:
    def __init__(self, place, src, own, came, sem):
        self.place, self.src, self.own, self.came, self.sem = place, src, own, came, sem

    @staticmethod
    def scratch(rows, width, sides=2):
        return [pltpu.VMEM((sides, rows // 2, width), BF), DMA((2,))]

    def cross(self):
        size = self.src.shape[1] // 2
        return remote(
            self.src.at[:, at(1 - self.place.core, size)], self.came, self.sem.at[0], self.sem.at[1], self.place.device(dcore=1)
        )

    def begin(self):
        self.cross().start()

    def finish(self):
        self.cross().wait()
        size = self.own.shape[2]
        for side in range(self.own.shape[0]):
            for yy in range(2):
                here = self.src[side, at(self.place.core * 2 + yy, size), :]
                self.own[side, yy] = here + self.came[side, yy * size : (yy + 1) * size, :]


class Plane:
    def __init__(self, place, own, kept, came_a, came_b, total, sem, x_first):
        self.place, self.own, self.kept, self.came_a, self.came_b = place, own, kept, came_a, came_b
        self.total, self.sem, self.x_first = total, sem, x_first

    @staticmethod
    def scratch(rows, width):
        block = rows // 4
        return [pltpu.VMEM((2, block, width), BF)] * 2 + [pltpu.VMEM((block, width), BF)] * 2 + [DMA((5,))]

    def load(self):
        p = self.place
        part = self.own.at[p.h] if self.x_first else self.own.at[:, p.y]
        return pltpu.make_async_copy(part, self.kept, self.sem.at[0])

    def hop_a(self):
        p = self.place
        if self.x_first:
            part, device = self.own.at[1 - p.h], p.device(dh=1)
        else:
            part, device = self.own.at[:, 1 - p.y], p.device(dy=1)
        return remote(part, self.came_a, self.sem.at[1], self.sem.at[2], device)

    def hop_b(self):
        p = self.place
        if self.x_first:
            part, device = self.kept.at[1 - p.y], p.device(dy=1)
        else:
            part, device = self.kept.at[1 - p.h], p.device(dh=1)
        return remote(part, self.came_b, self.sem.at[3], self.sem.at[4], device)

    def begin_a(self):
        self.hop_a().start()
        self.load().start()

    def finish_a(self):
        self.load().wait()
        self.hop_a().wait()
        self.kept[...] = self.kept[...] + self.came_a[...]

    def begin_b(self):
        self.hop_b().start()

    def finish_b(self):
        self.hop_b().wait()
        side = self.place.y if self.x_first else self.place.h
        self.total[...] = self.kept[side] + self.came_b[...]


class SidePlane:
    def __init__(self, place, own, kept, came_a, came_b, total, sem, side):
        self.place, self.own, self.kept, self.came_a, self.came_b = place, own, kept, came_a, came_b
        self.total, self.sem, self.side = total, sem, side

    @staticmethod
    def scratch(rows, width):
        return [pltpu.VMEM((rows // 4, width), BF)] * 4 + [DMA((4,))]

    def hop_a(self):
        p = self.place
        return remote(self.own.at[0, 1 - p.y], self.came_a, self.sem.at[0], self.sem.at[1], p.device(dy=1))

    def hop_b(self):
        return remote(self.kept, self.came_b, self.sem.at[2], self.sem.at[3], self.place.device(dh=1))

    def begin_a(self):
        self.hop_a().start()

    def finish_a(self):
        self.hop_a().wait()
        self.kept[...] = self.own[0, self.place.y] + self.came_a[...]

    def begin_b(self):
        pl.when(self.place.h != self.side)(lambda: self.hop_b().start())

    def finish_b(self):
        pl.when(self.place.h != self.side)(lambda: self.hop_b().wait_send())

        def arrived():
            self.hop_b().wait_recv()
            self.total[...] = self.kept[...] + self.came_b[...]

        pl.when(self.place.h == self.side)(arrived)


class Column:
    def __init__(self, place, total, came, held, sem):
        self.place, self.total, self.came, self.held, self.sem = place, total, came, held, sem
        self.steps = place.deep.bit_length() - 1

    @staticmethod
    def scratch(deep, rows, width):
        return [pltpu.VMEM((rows // 4, width), BF)] * 2 + [DMA((4 * deep,))]

    def block(self, k):
        size, first = self.total.shape[0], 0
        for i in range(k):
            size //= 2
            first = first + lax.rem(lax.div(self.place.z, 1 << i), 2) * size
        return first

    def partner(self, k):
        bit = lax.rem(lax.div(self.place.z, 1 << k), 2)
        return self.place.device(dz=self.place.deep + (1 << k) - 2 * (1 << k) * bit)

    def rows(self, first, k):
        size = self.total.shape[0] >> k
        return pl.ds(pl.multiple_of(first, size), size)

    def fold(self, k):
        size = self.total.shape[0] >> (k + 1)
        other = 2 * self.block(k) + size - self.block(k + 1)
        arrived = self.came.at[pl.ds(self.total.shape[0] - 2 * size, size)]
        return remote(self.total.at[self.rows(other, k + 1)], arrived, self.sem.at[2 * k], self.sem.at[2 * k + 1], self.partner(k))

    def unfold(self, k):
        mine = self.held.at[self.rows(self.block(k + 1), k + 1)]
        n = 2 * self.steps + 2 * k
        return remote(mine, mine, self.sem.at[n], self.sem.at[n + 1], self.partner(k))

    def folded(self, k):
        self.fold(k).wait()
        size = self.total.shape[0] >> (k + 1)
        rows = self.rows(self.block(k + 1), k + 1)
        out = self.held if k == self.steps - 1 else self.total
        out[rows, :] = self.total[rows, :] + self.came[self.total.shape[0] - 2 * size : self.total.shape[0] - size, :]

    def hops(self):
        down = [(lambda k=k: self.fold(k).start(), lambda k=k: self.folded(k)) for k in range(self.steps)]
        up = [(lambda k=k: self.unfold(k).start(), lambda k=k: self.unfold(k).wait()) for k in reversed(range(self.steps))]
        return down + up


class ColumnDirect:
    def __init__(self, place, total, came, held, sem):
        self.place, self.total, self.came, self.held, self.sem = place, total, came, held, sem
        self.size = total.shape[0] // place.deep

    def block(self, ref, z):
        return ref.at[at(z, self.size)]

    def split(self):
        p, n = self.place, self.place.deep
        return [
            remote(self.block(self.total, lax.rem(p.z + j, n)), self.came.at[pl.ds((j - 1) * self.size, self.size)],
                   self.sem.at[j], self.sem.at[n + j], p.device(dz=j))
            for j in range(1, n)
        ]

    def spread(self):
        p, n = self.place, self.place.deep
        mine = self.block(self.held, p.z)
        return [remote(mine, mine, self.sem.at[2 * n + j], self.sem.at[3 * n + j], p.device(dz=j)) for j in range(1, n)]

    def summed(self):
        copies = self.split()
        for copy in copies:
            copy.wait()
        rows = at(self.place.z, self.size)
        value = self.total[rows, :].astype(F32)
        for j in range(self.place.deep - 1):
            value = value + self.came[j * self.size : (j + 1) * self.size, :].astype(F32)
        self.held[rows, :] = value.astype(BF)

    def hops(self):
        return [
            (lambda: start(*self.split()), self.summed),
            (lambda: start(*self.spread()), lambda: wait(*self.spread())),
        ]


class Spread:
    def __init__(self, place, held, out, sem):
        self.place, self.held, self.out, self.sem = place, held, out, sem

    def quarter(self):
        return self.out.at[at(self.place.core * 2 + self.place.y, self.held.shape[0])]

    def keep(self):
        return pltpu.make_async_copy(self.held, self.quarter(), self.sem.at[0])

    def along(self):
        return remote(self.held, self.quarter(), self.sem.at[1], self.sem.at[2], self.place.device(dy=1))

    def cross(self):
        part = self.out.at[at(self.place.core, 2 * self.held.shape[0])]
        return remote(part, part, self.sem.at[3], self.sem.at[4], self.place.device(dcore=1))

    def begin_y(self):
        self.keep().start()
        self.along().start()

    def finish_y(self):
        self.keep().wait()
        self.along().wait()

    def hops(self):
        return [(self.begin_y, self.finish_y), (lambda: self.cross().start(), lambda: self.cross().wait())]


def chain(place, kind, buffers, done, x_first=False, side=None, own=None):
    buffers = list(buffers)
    take = lambda n: [buffers.pop(0) for _ in range(n)]
    hops = []
    if kind is None:
        grads, own, came, sem = take(4)
        core = CoreSum(place, grads, own, came, sem)
        hops.append((core.begin, core.finish))
    if side is None:
        plane = Plane(place, own, *take(5), x_first)
    else:
        plane = SidePlane(place, own, *take(5), side)
    came, held, column_sem, spread_sem = take(4)
    if kind != "kept":
        hops.append((plane.begin_a, plane.finish_a))
    hops.append((plane.begin_b, plane.finish_b))
    column = (Column if side is None else ColumnDirect)(place, plane.total, came, held, column_sem)
    rest = column.hops() + Spread(place, held, done, spread_sem).hops()
    if side is not None:
        here = lambda stage: lambda: pl.when(place.h == side)(stage)
        rest = [(here(begin), here(finish)) for begin, finish in rest]
    hops += rest

    def joint(finish, begin):
        def stage():
            finish()
            begin()

        return stage

    return [hops[0][0]] + [joint(a[1], b[0]) for a, b in zip(hops, hops[1:])] + [hops[-1][1]]


def chain_scratch(deep, rows, width, kind=None, sides=2):
    parts = []
    if kind is None:
        parts += [pltpu.VMEM((sides, rows, width), BF), pltpu.VMEM((sides, 2, rows // 4, width), BF)] + CoreSum.scratch(rows, width, sides)
    parts += (Plane if sides == 2 else SidePlane).scratch(rows, width)
    return parts + Column.scratch(deep, rows, width) + [DMA((5,))]


class Moves:
    def __init__(self, sem):
        self.sem, self.used = sem, 0

    def copy(self, src, dst):
        self.used += 1
        return pltpu.make_async_copy(src, dst, self.sem.at[self.used - 1])

    def blocks(self, src, dst, count, size=ROWS):
        first = self.used
        self.used += count
        return lambda i: pltpu.make_async_copy(src.at[at(i, size)], dst.at[at(i, size)], self.sem.at[first + i])

    def pairs(self, sources, targets):
        first, many = self.used, len(sources)
        self.used += many * (HEADS // 2)

        def copies(i):
            lanes = at(head_pair(i), 128)
            return [
                pltpu.make_async_copy(src.at[:, lanes], dst.at[:, lanes], self.sem.at[first + i * many + j])
                for j, (src, dst) in enumerate(zip(sources, targets))
            ]

        return copies


def start(*copies):
    for copy in copies:
        copy.start()


def wait(*copies):
    for copy in copies:
        copy.wait()


def self_fwd_kernel(
    deep, tokens, memory, out_cot, qkv_w, out_w, cq_w, lengths, gain, bias,
    row_came, memory_came, cot_came, q, k, v, mix, ext, normed, inverse, cq, qe, ke, live,
    row_s, qkv_s, out_s, cqw_s, q_s, k_s, v_s, mix_s, ext_s, normed_s, inverse_s, cq_s, qe_s, ke_s, live_s, kx_s, vx_s, sem,
    sem_far,
):
    place = Place(deep)
    h = place.h
    half = tokens.shape[1]
    row_length, width = row_s.shape
    blocks = row_length // ROWS
    lower, upper = pl.ds(0, half), pl.ds(half, half)
    place.greet("dh")
    moves = Moves(sem)
    own_row = moves.copy(tokens.at[h], row_s.at[lower])
    get_w = moves.copy(qkv_w, qkv_s)
    late = [moves.copy(out_w, out_s), moves.copy(cq_w.at[0], cqw_s)]
    start(own_row, get_w)
    partner = place.device(dh=1)
    send_row = remote(tokens.at[1 - h], row_s.at[upper], sem_far.at[0], sem_far.at[1], partner)
    send_memory = remote(memory.at[1 - h], memory_came, sem_far.at[2], sem_far.at[3], partner)
    send_cot = remote(out_cot.at[1 - h, pl.ds(0, half // 2)], cot_came, sem_far.at[4], sem_far.at[5], partner)
    place.met()
    send_row.start()

    position = lax.broadcasted_iota(jnp.int32, (row_length, 128), 0)
    position = jnp.where(h == 0, position, lax.rem(position + half, row_length))
    segment = jnp.zeros((row_length, 128), jnp.int32)
    following = jnp.zeros((row_length, 128), jnp.int32)
    end = 0
    for j in range(lengths.shape[1]):
        end = end + lengths[h, j]
        segment = segment + (position >= end).astype(jnp.int32)
        following = following + (position + 1 >= end).astype(jnp.int32)
    live_s[...] = ((following == segment) & (position + 1 < row_length)).astype(F32).astype(BF)
    spare = lax.rem(lax.broadcasted_iota(jnp.int32, (row_length, 128), 1), 64)
    coded, hit = spare < lengths.shape[1], segment == spare
    qe_s[...] = jnp.where(coded & hit, BIG, 0.0).astype(BF)
    ke_s[...] = jnp.where(coded, jnp.where(hit, 0.0, -BIG), jnp.where(spare < 7, 1.0, 0.0)).astype(BF)

    def project(i):
        rows = at(i, ROWS)
        x = row_s[rows, :]
        q_s[rows, :] = dot(x, qkv_s[0]).astype(BF) * jnp.asarray(0.125, BF)
        k_s[rows, :] = dot(x, qkv_s[1]).astype(BF)
        v_s[rows, :] = dot(x, qkv_s[2]).astype(BF)

    wait(own_row, get_w)
    loop(blocks // 2, project)
    send_row.wait()
    start(send_memory, send_cot)
    loop(blocks, project, blocks // 2)
    pairs = ((row_s.at[upper], row_came), (q_s, q), (k_s, k), (v_s, v), (qe_s, qe), (ke_s, ke), (live_s, live))
    outward = [moves.copy(src, dst) for src, dst in pairs]
    start(*outward, *late)
    attend(q_s, k_s, v_s, qe_s, ke_s, mix_s, ext_s, kx_s, vx_s)
    mixed = [moves.copy(mix_s, mix), moves.copy(ext_s, ext)]
    start(*mixed)
    wait(*late)
    by_block = [moves.blocks(src, dst, blocks) for src, dst in ((normed_s, normed), (inverse_s, inverse), (cq_s, cq))]

    def after(i):
        rows = at(i, ROWS)
        n, s = normalise(row_s[rows, :].astype(F32) + dot(mix_s[rows, :], out_s[...]))
        normed_s[rows, :] = n
        inverse_s[rows, :] = s
        low = (n * gain[0:1, :] + bias[0:1, :]).astype(BF)
        cq_s[rows, :] = dot(low, cqw_s[...]).astype(BF) * jnp.asarray(0.125, BF)
        start(*[copy(i) for copy in by_block])

    loop(blocks, after)
    wait(*outward, *mixed)
    loop(blocks, lambda i: wait(*[copy(i) for copy in by_block]))
    wait(send_memory, send_cot)


def cross_fwd_kernel(
    deep, slot_cot, memory, memory_came, kv_w, cq, qe, ke, out_w, normed_one, slot_mask, gain, bias,
    slot_own, slot_came, k, v, mix, ext, normed, inverse,
    memory_s, kv_s, cq_s, qe_s, ke_s, out_s, first_s, k_s, v_s, mix_s, ext_s, normed_s, inverse_s, kx_s, vx_s, masked, sem, sem_far,
):
    place = Place(deep)
    h = place.h
    half = slot_cot.shape[1]
    place.greet("dh")
    moves = Moves(sem)
    blocks = memory_s.shape[0] // ROWS
    get_slots = moves.copy(slot_cot, masked)
    get_memory = [moves.copy(memory.at[h], memory_s.at[pl.ds(0, half)]), moves.copy(memory_came, memory_s.at[pl.ds(half, half)])]
    get_w = moves.copy(kv_w.at[pl.ds(1, 2)], kv_s)
    soon = [moves.copy(src, dst) for src, dst in ((cq, cq_s), (qe, qe_s), (ke, ke_s))]
    late = [moves.copy(src, dst) for src, dst in ((out_w, out_s), (normed_one, first_s))]
    send = remote(masked.at[1 - h], slot_came, sem_far.at[0], sem_far.at[1], place.device(dh=1))
    start(get_w, get_slots, *get_memory, *soon)
    wait(get_w, *get_memory)

    def project(i):
        rows = at(i, ROWS)
        x = memory_s[rows, :]
        k_s[rows, :] = dot(x, kv_s[0]).astype(BF)
        v_s[rows, :] = dot(x, kv_s[1]).astype(BF)

    place.met()
    get_slots.wait()
    columns = slot_mask[...].astype(F32).T
    for r in range(2):
        masked[r] = masked[r] * columns[:, r : r + 1].astype(BF)
    send.start()
    loop(blocks, project)
    outward = [moves.copy(k_s, k), moves.copy(v_s, v), moves.copy(masked.at[h], slot_own)]
    wait(*soon)
    start(*outward, *late)
    attend(cq_s, k_s, v_s, qe_s, ke_s, mix_s, ext_s, kx_s, vx_s)
    mixed = [moves.copy(mix_s, mix), moves.copy(ext_s, ext)]
    start(*mixed)
    wait(*late)
    by_block = [moves.blocks(src, dst, blocks) for src, dst in ((normed_s, normed), (inverse_s, inverse))]

    def after(i):
        rows = at(i, ROWS)
        before = first_s[rows, :] * gain[0:1, :] + bias[0:1, :]
        n, s = normalise(before + dot(mix_s[rows, :], out_s[...]))
        normed_s[rows, :] = n
        inverse_s[rows, :] = s
        start(*[copy(i) for copy in by_block])

    loop(blocks, after)
    wait(*outward, *mixed)
    loop(blocks, lambda i: wait(*[copy(i) for copy in by_block]))
    send.wait()


def ffn_kernel(
    deep, normed_two, in_w, out_w, slot_w, slot_own, slot_came, out_cot, cot_first, live, inverse_two, cross_out_w, cross_mix,
    gain, bias,
    out_home, slots_home, res_two, grad_mix, sum_out, sum_slot, sum_in, sums,
    two_s, inw_s, outw_s, slotw_s, slot_s, cot_s, live_s, inverse_two_s, crossw_s, mix_s,
    low_s, hidden_s, slope_s, normed_s, inverse_s, pair_s, next_s, gnext_s, res_s, ginner_s, res_two_s, res_low_s, gmix_s, slots_s,
    g_out, g_slot, g_in, own_out, own_slot, own_in, came_out, sem_out, came_slot, sem_slot, came_in, sem_in,
    kept_slot, hop_slot, plane_sem, sem, sem_far,
):
    row_length, width = low_s.shape
    blocks = row_length // ROWS
    units = in_w.shape[1]
    half = row_length // 2
    place = Place(deep)
    place.greet("dh", "dcore", "dy")
    h = place.h
    scale = 0.7978845608028654
    moves = Moves(sem)
    get_two = moves.blocks(normed_two, two_s, blocks)
    first = [moves.copy(in_w, inw_s), moves.copy(out_w, outw_s)]
    lower, upper, quarter = pl.ds(0, half), pl.ds(half, half), half // 2
    soon = [
        moves.copy(src, dst)
        for src, dst in ((slot_w, slotw_s), (slot_own, slot_s.at[lower]), (slot_came, slot_s.at[upper]), (live, live_s))
    ]
    late = [
        moves.copy(src, dst)
        for src, dst in ((out_cot.at[h], cot_s.at[lower]), (cot_first, cot_s.at[pl.ds(half, quarter)]), (inverse_two, inverse_two_s), (cross_out_w, crossw_s), (cross_mix, mix_s))
    ]
    work_out = CoreSum(place, g_out, own_out, came_out, sem_out)
    work_slot = CoreSum(place, g_slot, own_slot, came_slot, sem_slot)
    work_in = CoreSum(place, g_in, own_in, came_in, sem_in)
    plane_slot = Plane(place, own_slot, kept_slot, hop_slot, None, None, plane_sem, False)

    def home(src, dst, i):
        lanes = pl.ds(0, width)
        return (
            moves.copy(src.at[lower, lanes], dst.at[h]),
            remote(src.at[upper, lanes], dst.at[h], sem_far.at[2 * i], sem_far.at[2 * i + 1], place.device(dh=1)),
        )

    homeward = home(pair_s, out_home, 0) + home(slots_s, slots_home, 1)
    cot_rest = remote(
        out_cot.at[1 - h, pl.ds(quarter, quarter)], cot_s.at[pl.ds(half + quarter, quarter)], sem_far.at[4], sem_far.at[5], place.device(dh=1)
    )
    last = blocks - 1
    get_two(last).start()
    start(*first)
    loop(last, lambda i: get_two(i).start())
    start(*soon, *late)
    place.met()
    cot_rest.start()
    wait(*first)

    def forward(i):
        rows = at(i, ROWS)
        get_two(i).wait()
        after_cross = two_s[rows, :] * gain[1:2, :] + bias[1:2, :]
        low = after_cross.astype(BF)
        low_s[rows, :] = low
        for c in range(units // 512):
            cols = slice(c * 512, (c + 1) * 512)
            inner = dot(low, inw_s[:, cols])
            square = inner * inner
            bent = jnp.tanh(inner * (scale + (scale * 0.044715) * square))
            part = 0.5 + 0.5 * bent
            hidden_s[rows, cols] = (inner * part).astype(BF)
            slope = part + inner * (0.5 - 0.5 * bent * bent) * (scale + (3 * scale * 0.044715) * square)
            slope_s[rows, cols] = slope.astype(BF)
        n, s = normalise(after_cross + dot(hidden_s[rows, :], outw_s[...]))
        normed_s[rows, :] = n
        inverse_s[rows, :] = s
        final = (n * gain[2:3, :] + bias[2:3, :]).astype(BF)
        pair_s[rows, :width] = final
        next_s[rows, :] = final.astype(F32)

    def backwards(body, sent):
        def one(i):
            body(last - i)
            pl.when(i == (blocks - 1) // 2)(sent)

        loop(blocks, one)

    backwards(forward, lambda: homeward[1].start())
    homeward[0].start()
    next_s[pl.ds(row_length, 8), :] = next_s[pl.ds(0, 8), :]
    wait(*soon)

    def slot(i):
        rows = at(i, ROWS)
        window = pl.ds(pl.multiple_of(i * ROWS, ROWS), ROWS + 8)
        alive = live_s[rows, 0:1].astype(F32)
        pair_s[rows, width:] = (next_s[window, :][1 : ROWS + 1] * alive).astype(BF)
        slots_s[rows, :] = dot(pair_s[rows, :], slotw_s[...]).astype(BF)
        back = (dot_nt(slot_s[rows, :], slotw_s[width:, :]) * alive).astype(BF)
        gnext_s[pl.ds(pl.multiple_of(i * ROWS + 8, 8), ROWS), :] = back.astype(F32)

    backwards(slot, lambda: homeward[3].start())
    homeward[2].start()
    gnext_s[pl.ds(0, 8), :] = gnext_s[pl.ds(row_length, 8), :]
    sums[...] = jnp.zeros(sums.shape, F32)
    fill(g_slot, width)
    for side in range(2):
        g_slot[side, :width, :] = dot_tn(pair_s[:, side * width : (side + 1) * width], slot_s[...]).astype(BF)
    work_slot.begin()
    wait(*late)
    cot_rest.wait()
    by_block = [moves.blocks(src, dst, blocks) for src, dst in ((res_two_s, res_two), (gmix_s, grad_mix))]

    def backward(i):
        @pl.when(i == 1)
        def slot_hop():
            work_slot.finish()
            plane_slot.begin_a()

        rows = at(i, ROWS)
        window = pl.ds(pl.multiple_of(i * ROWS, ROWS), ROWS + 8)
        gradient = (
            cot_s[rows, :].astype(F32)
            + dot_nt(slot_s[rows, :], slotw_s[:width, :])
            + gnext_s[window, :][7 : ROWS + 7]
        )
        n = normed_s[rows, :]
        sums[0:1, :] += jnp.sum(gradient * n, axis=0, keepdims=True)
        sums[1:2, :] += jnp.sum(gradient, axis=0, keepdims=True)
        res = norm_back(gradient, n, inverse_s[rows, :], gain[2:3, :])
        res_low = res.astype(BF)
        res_s[rows, :] = res_low
        for c in range(units // 512):
            cols = slice(c * 512, (c + 1) * 512)
            ginner_s[rows, cols] = (dot_nt(res_low, outw_s[cols, :]) * slope_s[rows, cols].astype(F32)).astype(BF)
        res = res + dot_nt(ginner_s[rows, :], inw_s[...])
        n = two_s[rows, :]
        sums[2:3, :] += jnp.sum(res * n, axis=0, keepdims=True)
        sums[3:4, :] += jnp.sum(res, axis=0, keepdims=True)
        res = norm_back(res, n, inverse_two_s[rows, :], gain[1:2, :])
        res_two_s[rows, :] = res
        res_low = res.astype(BF)
        res_low_s[rows, :] = res_low
        gmix_s[rows, :] = dot_nt(res_low, crossw_s[...]).astype(BF)
        start(*[copy(i) for copy in by_block])

    loop(blocks, backward)
    fill(g_out, units // 2 + width // 2)
    fill(g_in, width * units // 1024)
    for side in range(2):
        g_out[side, units // 2 : units // 2 + width // 2, :] = dot_tn(
            mix_s[:, side * 256 : (side + 1) * 256], res_low_s[...]
        ).astype(BF)
    for side in range(2):
        g_out[side, : units // 2, :] = dot_tn(hidden_s[:, side * (units // 2) : (side + 1) * (units // 2)], res_s[...]).astype(BF)
    work_out.begin()
    for c in range(units // 512):
        side, block = divmod(c, units // 1024)
        g_in[side, block * width : (block + 1) * width, :] = dot_tn(low_s[...], ginner_s[:, c * 512 : (c + 1) * 512]).astype(BF)
    work_in.begin()
    done = [moves.copy(src, dst) for src, dst in ((own_out, sum_out), (kept_slot, sum_slot), (own_in, sum_in))]
    for finish, copy in zip((work_out.finish, plane_slot.finish_a, work_in.finish), done):
        finish()
        copy.start()
    loop(blocks, lambda i: wait(*[copy(i) for copy in by_block]))
    wait(*done, *homeward)


def fill(grads, used):
    rest = grads.shape[1] - used
    if rest:
        grads[:, used:, :] = jnp.zeros((grads.shape[0], rest, grads.shape[2]), BF)


def weight_grads(grads, pairs, sources):
    for left, rights, first in sources:
        right = jnp.concatenate([d[:, p * 128 : (p + 1) * 128] for d in rights for p in pairs], axis=1)
        width = left.shape[1]
        block = dot_tn(left[...], right).astype(BF)
        for i in range(len(rights)):
            for side in range(len(pairs)):
                lane = (i * len(pairs) + side) * 128
                grads[side, (first + i) * width : (first + i + 1) * width, :] = block[:, lane : lane + 128]


PLAN = {
    "begin": (("out", 0), ("in", 0), ("slot", 0),),
    "c0": (("slot", 1),),
    "c1": (("slot", 2),),
    "c2": (("slot", 3),),
    "c3": (("d1", 0), ("slot", 4),),
    "c4": (("d1", 1), ("slot", 5),),
    "c6": (("d1", 2), ("in", 1),),
    "c7": (("out", 1), ("slot", 6),),
    "c8": (("d1", 3),),
    "c9": (("d2", 0),),
    "c10": (("d1", 4), ("in", 2), ("mem", 0),),
    "s0": (("d2", 1), ("d1", 5), ("in", 3),),
    "s1": (("out", 2),),
    "s2": (("d1", 6), ("in", 4),),
    "s3": (("e1", 0), ("d2", 2), ("d1", 7), ("out", 3),),
    "s4": (("e1", 1), ("d1", 8), ("in", 5),),
    "s5": (("e2", 0), ("d2", 3), ("out", 4),),
    "s6": (("e2", 1), ("e1", 2), ("d2", 4), ("in", 6),),
    "s7": (("d2", 5), ("out", 5),),
    "s8": (("f", 0), ("e1", 3),),
    "s9": (("e2", 2), ("row", 0),),
    "s10": (("f", 1), ("d2", 6),),
    "tail": (("e1", 4), ("in", 7), ("out", 6), ("f", 2), ("e1", 5), ("d2", 7), ("e2", 3), ("e1", 6), ("e2", 4), ("f", 3),
        ("e2", 5), ("e1", 7), ("f", 4), ("d2", 8), ("f", 5), ("e2", 6), ("e1", 8), ("out", 7), ("f", 6), ("out", 8),
        ("in", 8), ("slot", 7), ("d1", 9), ("d2", 9), ("e1", 9), ("e2", 7), ("row", 1), ("mem", 1), ("f", 7),),
}


def back_kernel(
    deep, own_out, own_in, own_slot, cq, ck, cv, cext, cmix, gcmix, memory, memory_came, cross_w, res_two, normed_one, inverse_one,
    q, k, v, ext, mix, out_w, tokens, tokens_came, self_w, ke, gain, bias, sums_two,
    done_out, done_in, done_slot, done_d1, done_d2, done_e, done_f, mem_mine, mem_came, row_mine, row_came,
    q_s, k_s, v_s, ext_s, mix_s, gmix_s, memory_s, row_s, low_s, dq_s, dk_s, dv_s, res_s, cross_ws, self_ws, outw_s,
    res_two_s, normed_s, res_one_s, inverse_s, sums, mine_s, theirs_s, row_theirs,
    kx_s, vx_s, qx_s, dx_s, extra_s, kt_s, dqt_s, sem, sem_far, *comm,
):
    row_length, width = row_s.shape
    blocks = row_length // ROWS
    half_blocks = blocks // 2
    half = row_length // 2
    lower, upper = pl.ds(0, half), pl.ds(half, half)
    place = Place(deep)
    place.greet("dh", "dy", "dz", "dcore")
    moves = Moves(sem)
    cross_pairs = moves.pairs((cq, ck, cv, cext, cmix, gcmix), (q_s, k_s, v_s, ext_s, mix_s, gmix_s))
    late = [
        moves.copy(src, dst)
        for src, dst in ((normed_one, normed_s), (memory.at[place.h], memory_s.at[lower]), (memory_came, memory_s.at[upper]),
                         (cross_w, cross_ws), (inverse_one, inverse_s), (res_two, res_two_s), (out_w, outw_s),
                         (tokens.at[place.h], row_s.at[lower]), (tokens_came, row_s.at[upper]), (self_w, self_ws))
    ]
    again = [moves.copy(src, dst) for src, dst in ((q, q_s), (k, k_s), (v, v_s), (ext, ext_s), (mix, mix_s))]
    loop(HEADS // 2, lambda i: start(*cross_pairs(i)))
    comm = list(comm)
    take = lambda n: [comm.pop(0) for _ in range(n)]
    get_slot = moves.copy(own_slot, comm[18])
    get_slot.start()
    chains = {
        "out": chain(place, "own", take(9), done_out, False, own=own_out),
        "in": chain(place, "own", take(9), done_in, False, own=own_in),
        "slot": chain(place, "kept", take(9), done_slot, False),
    }
    grads = {}
    for name, done, x_first, side in (("d1", done_d1, True, None), ("d2", done_d2, False, None), ("e1", done_e, False, None),
                                      ("e2", done_f, False, 0), ("f", done_f, False, 1)):
        buffers = take(13)
        grads[name] = buffers[0]
        chains[name] = chain(place, None, buffers, done, x_first, side)
    mem_send = remote(theirs_s, mem_came, sem_far.at[0], sem_far.at[1], place.device(dh=1))
    row_send = remote(row_theirs, row_came, sem_far.at[2], sem_far.at[3], place.device(dh=1))
    chains["mem"] = [mem_send.start, mem_send.wait]
    chains["row"] = [row_send.start, row_send.wait]

    def run(point):
        for name, stage in PLAN.get(point, ()):
            chains[name][stage]()

    def hooks(letter, extra):
        table = {}
        for step in range(HEADS):
            point = letter + str(step)
            if step in extra or point in PLAN:
                def hook(point=point, step=step):
                    if step in extra:
                        extra[step]()
                    run(point)

                table[step] = hook
        return table

    def low_rows():
        wait(*late)

        def one(i):
            rows = at(i, ROWS)
            low_s[rows, :] = (normed_s[rows, :] * gain[0:1, :] + bias[0:1, :]).astype(BF)

        loop(blocks, one)

    cross_sources = ((low_s, (dq_s,), 0), (memory_s, (dk_s, dv_s), 1))
    self_sources = ((row_s, (dq_s, dk_s, dv_s), 0),)
    for name, used in (("d1", 3 * width), ("d2", 5 * width), ("e1", 3 * width + 16), ("e2", 3 * width), ("f", 3 * width)):
        fill(grads[name], used)
    place.met()
    get_slot.wait()
    run("begin")
    start(*late)
    scratch = (dq_s, dk_s, dv_s, kx_s, vx_s, qx_s, dx_s, extra_s, kt_s, dqt_s)
    attend_back(
        q_s, k_s, v_s, ext_s, ke, mix_s, gmix_s, *scratch,
        hooks("c", {1: low_rows, 3: lambda: weight_grads(grads["d1"], (0, 2), cross_sources)}), cross_pairs,
    )
    start(*again)
    sums[...] = jnp.zeros(sums.shape, F32)

    def backward(i):
        rows = at(i, ROWS)
        n = normed_s[rows, :]
        gradient = res_two_s[rows, :] + dot_nt(dq_s[rows, :], cross_ws[0])
        sums[0:1, :] += jnp.sum(gradient * n, axis=0, keepdims=True)
        sums[1:2, :] += jnp.sum(gradient, axis=0, keepdims=True)
        res = norm_back(gradient, n, inverse_s[rows, :], gain[0:1, :])
        res_one_s[rows, :] = res
        res_low = res.astype(BF)
        res_s[rows, :] = res_low
        gmix_s[rows, :] = dot_nt(res_low, outw_s[...]).astype(BF)

    loop(blocks, backward)
    run("c8")
    weight_grads(grads["d2"], (1, 3), cross_sources)
    wait(*again)
    for side in range(2):
        block = dot_tn(mix_s[:, side * 256 : (side + 1) * 256], res_s[...]).astype(BF)
        for c in range(width // 128):
            grads["d2"][side, 3 * width + c * 256 : 3 * width + (c + 1) * 256, :] = block[:, c * 128 : (c + 1) * 128]
    run("c9")
    put_mem = moves.blocks(mine_s, mem_mine, half_blocks)
    put_row = moves.blocks(mine_s, row_mine, half_blocks)

    def memory_grad(i):
        rows = at(i, ROWS)
        return dot_nt(dk_s[rows, :], cross_ws[1]) + dot_nt(dv_s[rows, :], cross_ws[2])

    def memory_theirs(i):
        theirs_s[at(i, ROWS), :] = memory_grad(i + half_blocks).astype(BF)

    def memory_mine(i):
        mine_s[at(i, ROWS), :] = memory_grad(i)
        put_mem(i).start()

    loop(half_blocks, memory_theirs)
    run("c10")
    loop(half_blocks, memory_mine)

    def first_grads():
        weight_grads(grads["e1"], (0, 2), self_sources)
        norms = jnp.concatenate(
            [sums[0:1, :], sums_two[2:3, :], sums_two[0:1, :], sums[1:2, :], sums_two[3:4, :], sums_two[1:2, :]], axis=0
        ).astype(BF)
        for side in range(2):
            parts = [norms[:, side * 256 + c * 128 : side * 256 + (c + 1) * 128] for c in range(2)]
            grads["e1"][side, 3 * width : 3 * width + 16, :] = jnp.concatenate(parts + [jnp.zeros((4, 128), BF)], axis=0)

    attend_back(
        q_s, k_s, v_s, ext_s, ke, mix_s, gmix_s, *scratch,
        hooks("s", {3: first_grads, 5: lambda: weight_grads(grads["e2"], (1,), self_sources)}), lambda i: (),
    )
    weight_grads(grads["f"], (3,), self_sources)
    run("s8")

    def row_grad(i):
        rows = at(i, ROWS)
        return (
            res_one_s[rows, :] + dot_nt(dq_s[rows, :], self_ws[0]) + dot_nt(dk_s[rows, :], self_ws[1]) + dot_nt(dv_s[rows, :], self_ws[2])
        )

    def row_other(i):
        row_theirs[at(i, ROWS), :] = row_grad(i + half_blocks).astype(BF)

    def row_own(i):
        put_mem(i).wait()
        mine_s[at(i, ROWS), :] = row_grad(i)
        put_row(i).start()

    loop(half_blocks, row_other)
    run("s9")
    loop(half_blocks, row_own)
    run("s10")
    run("tail")
    loop(half_blocks, lambda i: put_row(i).wait())


def finish_kernel(
    deep, out, slots, row_mine, row_came, mem_mine, mem_came, done_in, done_out, done_slot, done_d1, done_d2, done_e, done_f, slot_mask,
    out_f, slots_f, tokens_f, memory_f, self_qkv_f, self_out_f, cross_qkv_f, cross_out_f, norms_f, ffn_in_f, ffn_out_f, slot_f,
    slots_s, row_s, mem_s, in_s, outs_s, slot_s, d1_s, d2_s, e_s, f_s, masked_s, row_w, mem_w, in_w, out_w, slot_w, cross_w,
    cqkv_w, sout_w, sqkv_w, out_b, mem_b, row_b, sem,
):
    h = lax.axis_index("head")
    moves = Moves(sem)
    width = out.shape[2]
    loads = [
        moves.copy(src, dst)
        for src, dst in ((done_out, outs_s), (done_in, in_s), (done_slot, slot_s), (slots, slots_s), (mem_came, mem_s), (done_d1, d1_s),
                         (done_d2, d2_s), (row_came, row_s), (done_e, e_s), (done_f, f_s), (out, out_b), (mem_mine, mem_b), (row_mine, row_b))
    ]
    start(*loads)
    stores = []

    def put(src, dst):
        copy = moves.copy(src, dst)
        copy.start()
        stores.append(copy)

    half = out_w.shape[0]
    loads[0].wait()
    out_w[...] = outs_s[:half, :].astype(F32)
    put(out_w, ffn_out_f)
    loads[1].wait()
    for c in range(in_w.shape[1] // 512):
        in_w[:, c * 512 : (c + 1) * 512] = in_s[c * width : (c + 1) * width, :].astype(F32)
    put(in_w, ffn_in_f)
    cross_w[...] = outs_s[half : half + width // 2, :].astype(F32)
    put(cross_w, cross_out_f)
    loads[2].wait()
    slot_w[...] = slot_s[:width, :].astype(F32)
    put(slot_w, slot_f)
    loads[3].wait()
    columns = slot_mask[...].astype(F32).T
    for r in range(2):
        masked_s[r] = slots_s[r] * columns[:, r : r + 1].astype(BF)
    put(masked_s, slots_f)
    loads[4].wait()
    mem_w[...] = mem_s[...].astype(F32)
    put(mem_w, memory_f.at[1 - h])
    wait(loads[5], loads[6])
    for c, part_s in enumerate((d1_s, d2_s)):
        for part in range(3):
            cqkv_w[part, :, c * 128 : (c + 1) * 128] = part_s[part * width : (part + 1) * width, :].astype(F32)
    put(cqkv_w, cross_qkv_f)
    for c in range(width // 128):
        sout_w[:, c * 128 : (c + 1) * 128] = d2_s[3 * width + c * 256 : 3 * width + (c + 1) * 256, :].astype(F32)
    put(sout_w, self_out_f)
    loads[7].wait()
    row_w[...] = row_s[...].astype(F32)
    put(row_w, tokens_f.at[1 - h])
    wait(loads[8], loads[9])
    for c, part_s in enumerate((e_s, f_s)):
        for part in range(3):
            sqkv_w[part, :, c * 128 : (c + 1) * 128] = part_s[part * width : (part + 1) * width, :].astype(F32)
    norms = e_s[3 * width : 3 * width + 16, :].astype(F32)
    for c in range(2):
        norms_f[:, c * 128 : (c + 1) * 128] = norms[6 * c : 6 * c + 6]
    put(sqkv_w, self_qkv_f)
    for load, src, dst in zip(loads[10:], (out_b, mem_b, row_b), (out_f, memory_f.at[h], tokens_f.at[h])):
        load.wait()
        put(src, dst)
    wait(*stores)


def call(kernel, name, cid, args, outs, scratch, flops):
    if cid is None:
        params = pltpu.CompilerParams(vmem_limit_bytes=VMEM)
    else:
        params = pltpu.CompilerParams(collective_id=cid, has_side_effects=True, vmem_limit_bytes=VMEM)
    return pl.pallas_call(
        kernel,
        out_shape=[jax.ShapeDtypeStruct(shape, kind) for shape, kind, _ in outs],
        in_specs=[spec for _, spec in args],
        out_specs=[spec for _, _, spec in outs],
        scratch_shapes=scratch,
        compiler_params=params,
        cost_estimate=pl.CostEstimate(flops=flops, bytes_accessed=2**20, transcendentals=0),
        name=name,
    )(*[arg for arg, _ in args])


def padded(count, unit):
    return -(-count // unit) * unit


def per_device(
    tokens, memory, lengths, slot_mask, self_qkv, self_out, cross_qkv, cross_out,
    norm_gain, norm_bias, ffn_in, ffn_out, slot_proj, out_cot, slot_cot,
):
    local_len, width = tokens.shape[1:]
    units = ffn_in.shape[1]
    deep = lax.axis_size("dp") // 4
    row_length = 2 * local_len
    unit = 64 * deep
    rows_out, rows_slot, rows_in = padded(units // 2 + width // 2, unit), padded(width, unit), padded(width * units // 1024, unit)
    rows_d1, rows_d2, rows_e = padded(3 * width, unit), padded(5 * width, unit), padded(3 * width + 16, unit)
    dense = 2 * row_length * width * width
    scores = 2 * row_length * row_length * width

    def inner(*values):
        return [(value, INNER) for value in values]

    def outer(*values):
        return [(value, ANY) for value in values]

    def new(*shape, kind=BF, spec=INNER):
        return (shape, kind, spec)

    def scratch(*shape, kind=BF):
        return pltpu.VMEM(shape, kind)

    row, wide, column = (
        new(row_length, width, spec=ANY), new(row_length, width, kind=F32, spec=ANY), new(row_length, 1, kind=F32, spec=ANY)
    )
    small = new(row_length, 128, spec=ANY)
    row_s, wide_s, two_s = scratch(row_length, width), scratch(row_length, width, kind=F32), scratch(row_length, 256)
    tall_s, ring_s = scratch(row_length, units), scratch(row_length + 8, width, kind=F32)
    column_s, small_s, half_s = scratch(row_length, 1, kind=F32), scratch(row_length, 128), scratch(local_len, width)
    square_s, three_s = scratch(width, width), scratch(3, width, width)
    half_wide_s = scratch(local_len, width, kind=F32)

    half, part = new(local_len, width, spec=ANY), new(local_len // 2, width, spec=ANY)
    tokens_came, memory_came, cot_first, q, k, v, mix, ext, normed_one, inverse_one, cq, qe, ke, live = call(
        functools.partial(self_fwd_kernel, deep), "self_fwd", 0,
        outer(tokens, memory, out_cot, self_qkv, self_out, cross_qkv) + [(lengths, SCALARS)] + inner(norm_gain, norm_bias),
        [half, half, part] + [row] * 5 + [wide, column, row] + [small] * 3,
        [row_s, three_s, square_s, square_s] + [row_s] * 5 + [wide_s, column_s, row_s]
        + [small_s] * 3 + [two_s, two_s, DMA((40,)), DMA((6,))], 5 * dense + 8 * scores,
    )
    slot_own, slot_came, ck, cv, cmix, cext, normed_two, inverse_two = call(
        functools.partial(cross_fwd_kernel, deep), "cross_fwd", 1,
        outer(slot_cot, memory, memory_came, cross_qkv, cq, qe, ke, cross_out, normed_one) + inner(slot_mask, norm_gain, norm_bias),
        [half, half] + [row] * 4 + [wide, column],
        [row_s, scratch(2, width, width), row_s, small_s, small_s, square_s, wide_s] + [row_s] * 4 + [wide_s, column_s]
        + [two_s, two_s, scratch(2, local_len, width), DMA((40,)), DMA((2,))], 3 * dense + 8 * scores,
    )
    home = new(2, local_len, width, spec=ANY)
    groups = ((rows_out, 512), (rows_slot, 512), (rows_in, 512))
    out, slots, res_two, grad_cmix, sum_out, sum_slot, sum_in, sums_two = call(
        functools.partial(ffn_kernel, deep), "ffn", 2,
        outer(normed_two, ffn_in, ffn_out, slot_proj, slot_own, slot_came, out_cot, cot_first, live, inverse_two, cross_out, cmix) + inner(norm_gain, norm_bias),
        [home, home, wide, row, new(2, 2, rows_out // 4, 512, spec=ANY), new(2, rows_slot // 4, 512, spec=ANY),
         new(2, 2, rows_in // 4, 512, spec=ANY), new(8, width, kind=F32)],
        [wide_s, scratch(width, units), scratch(units, width), scratch(2 * width, width), row_s, row_s, small_s, column_s, square_s, row_s]
        + [row_s, tall_s, tall_s, wide_s, column_s, scratch(row_length, 2 * width), ring_s, ring_s, row_s, tall_s, wide_s]
        + [row_s] * 3
        + [scratch(2, rows, lanes) for rows, lanes in groups] + [scratch(2, 2, rows // 4, lanes) for rows, lanes in groups]
        + [part for group in groups for part in CoreSum.scratch(*group)]
        + [scratch(2, rows_slot // 4, 512), scratch(2, rows_slot // 4, 512), DMA((5,)), DMA((40,)), DMA((6,))], 32 * dense,
    )
    back = [small_s] * 5 + [scratch(128, row_length), scratch(128, row_length, kind=F32)]

    half_wide = new(local_len, width, kind=F32, spec=ANY)
    late = ((rows_d1, 128, 2), (rows_d2, 128, 2), (rows_e, 128, 2), (rows_d1, 128, 1), (rows_d1, 128, 1))

    def whole(rows, lanes):
        return new(rows, lanes, spec=ANY)

    done_out, done_in, done_slot, done_d1, done_d2, done_e, done_f, mem_mine, mem_came, row_mine, row_came = call(
        functools.partial(back_kernel, deep), "back", 3,
        outer(sum_out, sum_in, sum_slot, cq, ck, cv, cext, cmix, grad_cmix, memory, memory_came, cross_qkv, res_two, normed_one,
              inverse_one, q, k, v, ext, mix, self_out, tokens, tokens_came, self_qkv) + inner(ke, norm_gain, norm_bias, sums_two),
        [whole(rows_out, 512), whole(rows_in, 512), whole(rows_slot, 512), whole(rows_d1, 128), whole(rows_d2, 128), whole(rows_e, 128),
         whole(rows_d1, 128), half_wide, half, half_wide, half],
        [row_s] * 13 + [three_s, three_s, square_s] + [wide_s] * 3 + [column_s, scratch(8, width, kind=F32), half_wide_s, half_s, half_s]
        + back + [DMA((60,)), DMA((4,))]
        + [part for rows in (rows_out, rows_in, rows_slot) for part in chain_scratch(deep, rows, 512, "own")]
        + [part for rows, lanes, sides in late for part in chain_scratch(deep, rows, lanes, None, sides)],
        22 * dense + 40 * scores,
    )

    def final(*shape, kind=F32):
        return new(*shape, kind=kind, spec=ANY)

    def wide_scratch(*shape):
        return scratch(*shape, kind=F32)

    pair_s = scratch(2, local_len, width)
    results = call(
        functools.partial(finish_kernel, deep), "finish", None,
        outer(out, slots, row_mine, row_came, mem_mine, mem_came, done_in, done_out, done_slot, done_d1, done_d2, done_e, done_f)
        + inner(slot_mask),
        [final(2, local_len, width, kind=BF)] * 2 + [final(2, local_len, width)] * 2
        + [final(3, width, 256), final(width // 2, width), final(3, width, 256), final(width // 2, width)]
        + [new(6, 256, kind=F32)] + [final(width, units // 2), final(units // 2, width), final(width, width)],
        [pair_s, half_s, half_s, scratch(rows_in, 512), scratch(rows_out, 512), scratch(rows_slot, 512), scratch(rows_d1, 128),
         scratch(rows_d2, 128), scratch(rows_e, 128), scratch(rows_d1, 128), pair_s, half_wide_s, half_wide_s, wide_scratch(width, units // 2),
         wide_scratch(units // 2, width), wide_scratch(width, width), wide_scratch(width // 2, width), wide_scratch(3, width, 256),
         wide_scratch(width // 2, width), wide_scratch(3, width, 256), pair_s, half_wide_s, half_wide_s, DMA((40,))], 0,
    )
    norms = results[8]
    return (*results[:8], norms[:3], norms[3:], *results[9:])


def solution(mesh):
    split = P("dp", "head", None)
    placed = (split, split, P("dp", None), P("dp", "head")) + (P(),) * 9 + (split, split)
    return jax.shard_map(
        per_device,
        mesh=mesh,
        in_specs=placed,
        out_specs=(
            split, split, split, split,
            P(None, None, "head"), P("head", None), P(None, None, "head"), P("head", None),
            P(None, "head"), P(None, "head"), P(None, "head"), P("head", None), P("head", None),
        ),
        check_vma=False,
    )
```

```python
import functools

import jax
import jax.numpy as jnp
from jax import lax
from jax.experimental import pallas as pl
from jax.experimental.pallas import tpu as pltpu
from jax.sharding import PartitionSpec as P

HEADS = 8
BF = jnp.bfloat16
F32 = jnp.float32
MESH = pl.DeviceIdType.MESH
NT = (((1,), (1,)), ((), ()))
TN = (((0,), (0,)), ((), ()))
BIG = 2.0**20
VMEM = 60 * 2**20
ROWS = 512
QBLOCK = 512
ANY = pl.BlockSpec(memory_space=pl.ANY)
INNER = pl.BlockSpec(memory_space=pltpu.VMEM)
SCALARS = pl.BlockSpec(memory_space=pltpu.SMEM)


def dot(a, b):
    return jnp.dot(a, b, preferred_element_type=F32)


def dot_nt(a, b):
    return lax.dot_general(a, b, NT, preferred_element_type=F32)


def dot_tn(a, b):
    return lax.dot_general(a, b, TN, preferred_element_type=F32)


def at(i, size):
    return pl.ds(pl.multiple_of(i * size, size), size)


def loop(count, body, first=0):
    def step(i, carry):
        body(i)
        return carry

    lax.fori_loop(first, count, step, 0)


def thirds(value):
    first = value.astype(BF)
    rest = value - first.astype(F32)
    second = rest.astype(BF)
    third = (rest - second.astype(F32)).astype(BF)
    return first, second, third


def normalise(value):
    average = jnp.mean(value, axis=-1, keepdims=True)
    centred = value - average
    inverse = lax.rsqrt(jnp.mean(centred * centred, axis=-1, keepdims=True) + 1e-05)
    return centred * inverse, inverse


def norm_back(gradient, normed, inverse, gain_row):
    scaled = gradient * gain_row
    inner_mean = jnp.mean(scaled, axis=-1, keepdims=True)
    cross_mean = jnp.mean(scaled * normed, axis=-1, keepdims=True)
    return inverse * (scaled - inner_mean - normed * cross_mean)


def run_hooks(hooks, step):
    for done, hook in hooks.items():
        if done >= 0:
            pl.when(step == done)(hook)


def attend(q_s, k_s, v_s, qe_ref, ke_ref, mix_s, ext_s, kx_s, vx_s):
    row_length = k_s.shape[0]
    block = 256
    wide_low = lax.broadcasted_iota(jnp.int32, (row_length, 128), 1) < 64
    lane = lax.broadcasted_iota(jnp.int32, (block, 128), 1)
    low = lane < 64
    spare = lax.rem(lane, 64)

    def pair(p):
        lanes = at(p, 128)
        parts = [slice(h * 128, (h + 1) * 128) for h in range(2)]
        for h in range(2):
            mine = wide_low if h == 0 else ~wide_low
            kx_s[:, parts[h]] = jnp.where(mine, k_s[:, lanes], ke_ref[...])
            vx_s[:, parts[h]] = jnp.where(mine, v_s[:, lanes], jnp.ones((), BF))

        def rows_of(t):
            return slice((t // 2) * block, (t // 2 + 1) * block)

        def scores_of(t):
            rows = rows_of(t)
            query = jnp.where(low if t % 2 == 0 else ~low, q_s[rows, lanes], qe_ref[rows, :])
            return dot_nt(query, kx_s[:, parts[t % 2]])

        many = 2 * (row_length // block)
        ahead, done = scores_of(0), []
        for t in range(many):
            scores = ahead
            if t + 1 < many:
                ahead = scores_of(t + 1)
            top = jnp.max(scores, axis=1, keepdims=True)
            probs = jnp.exp(scores - top).astype(BF)
            done.append((top, dot(probs, vx_s[:, parts[t % 2]])))
            if t % 2 == 1:
                rows = rows_of(t)
                (top_low, sum_low), (top_high, sum_high) = done[-2:]
                mixed = jnp.where(low, sum_low, sum_high)
                totals = jnp.where(low, sum_high, sum_low)
                first, second, third = thirds(jnp.where(low, top_high, top_low) + jnp.log(totals))
                ext_s[rows, lanes] = jnp.where(
                    spare == 4, -first, jnp.where(spare == 5, -second, jnp.where(spare == 6, -third, qe_ref[rows, :]))
                )
                mix_s[rows, lanes] = (mixed / pltpu.roll(totals, 64, 1)).astype(BF)

    loop(HEADS // 2, pair)


def head_pair(i):
    return lax.rem(i, 2) * 2 + lax.div(i, 2)


def attend_back(q_s, k_s, v_s, ext_s, ke_ref, mix_s, gmix_s, dq_s, dk_s, dv_s, kx_s, vx_s, qx_s, dx_s, extra_s, kt_s, dqt_s, hooks, get_pair):
    row_length = k_s.shape[0]
    block = QBLOCK
    lane = lax.broadcasted_iota(jnp.int32, (row_length, 128), 1)
    low = lane < 64
    spare = lax.rem(lane, 64)
    zero = jnp.zeros((), BF)

    def head(step):
        i, odd = lax.div(step, 2), lax.rem(step, 2)
        lanes = at(head_pair(i), 128)
        mine = lax.div(lane, 64) == odd

        @pl.when(odd == 0)
        def arrive():
            for copy in get_pair(i):
                copy.wait()
            product = gmix_s[:, lanes].astype(F32) * mix_s[:, lanes].astype(F32)
            inner_low = jnp.sum(jnp.where(low, product, 0.0), axis=1, keepdims=True)
            inner_high = jnp.sum(jnp.where(low, 0.0, product), axis=1, keepdims=True)
            first, second, third = thirds(jnp.where(low, inner_high, inner_low))
            extra_s[...] = jnp.where(spare == 0, -first, jnp.where(spare == 1, -second, jnp.where(spare == 2, -third, zero)))
            kt_s[...] = k_s[:, lanes].T

        kx_s[...] = jnp.where(mine, k_s[:, lanes], ke_ref[...])
        vx_s[...] = jnp.where(mine, v_s[:, lanes], jnp.ones((), BF))
        qx_s[...] = jnp.where(mine, q_s[:, lanes], ext_s[:, lanes])
        dx_s[...] = jnp.where(mine, gmix_s[:, lanes], extra_s[...])
        own = at(odd, 64)
        for j in range(row_length // block):
            cols = slice(j * block, (j + 1) * block)
            probs = jnp.exp(dot_nt(kx_s[...], qx_s[cols, :]))
            ds = (probs * dot_nt(vx_s[...], dx_s[cols, :])).astype(BF)
            dv = dot(probs.astype(BF), dx_s[cols, :])
            dk = dot(ds, qx_s[cols, :])
            acc_v, acc_k = (dv, dk) if j == 0 else (acc_v + dv, acc_k + dk)
            dqt_s[own, cols] = dot(kt_s[own, :], ds) * 0.125
        dk_s[:, lanes] = jnp.where(mine, acc_k.astype(BF), dk_s[:, lanes])
        dv_s[:, lanes] = jnp.where(mine, acc_v.astype(BF), dv_s[:, lanes])

        @pl.when(odd == 1)
        def turn():
            dq_s[:, lanes] = dqt_s[...].T.astype(BF)

        run_hooks(hooks, step)

    loop(HEADS, head)


class Place:
    def __init__(self, deep):
        dp = lax.axis_index("dp")
        self.deep = deep
        self.h = lax.axis_index("head")
        self.core = lax.rem(dp, 2)
        self.y = lax.rem(lax.div(dp, 2), 2)
        self.z = lax.div(dp, 4)

    def device(self, dh=0, dcore=0, dy=0, dz=None):
        h = 1 - self.h if dh else self.h
        core = 1 - self.core if dcore else self.core
        y = 1 - self.y if dy else self.y
        z = self.z if dz is None else lax.rem(self.z + dz, self.deep)
        return ((z * 2 + y) * 2 + core, h)

    def greet(self, *kinds):
        self.peers = []
        for kind in kinds:
            if kind == "dz":
                self.peers += [self.device(dz=j) for j in range(1, self.deep)]
            else:
                self.peers.append(self.device(**{kind: 1}))
        barrier = pltpu.get_barrier_semaphore()
        for peer in self.peers:
            pl.semaphore_signal(barrier, inc=1, device_id=peer, device_id_type=MESH)

    def met(self):
        pl.semaphore_wait(pltpu.get_barrier_semaphore(), len(self.peers))


def remote(src, dst, send, recv, device):
    return pltpu.make_async_remote_copy(
        src_ref=src, dst_ref=dst, send_sem=send, recv_sem=recv, device_id=device, device_id_type=MESH
    )


DMA = pltpu.SemaphoreType.DMA


class CoreSum:
    def __init__(self, place, src, own, came, sem):
        self.place, self.src, self.own, self.came, self.sem = place, src, own, came, sem

    @staticmethod
    def scratch(rows, width, sides=2):
        return [pltpu.VMEM((sides, rows // 2, width), BF), DMA((2,))]

    def cross(self):
        size = self.src.shape[1] // 2
        return remote(
            self.src.at[:, at(1 - self.place.core, size)], self.came, self.sem.at[0], self.sem.at[1], self.place.device(dcore=1)
        )

    def begin(self):
        self.cross().start()

    def finish(self):
        self.cross().wait()
        size = self.own.shape[2]
        for side in range(self.own.shape[0]):
            for yy in range(2):
                here = self.src[side, at(self.place.core * 2 + yy, size), :]
                self.own[side, yy] = here + self.came[side, yy * size : (yy + 1) * size, :]


class Plane:
    def __init__(self, place, own, kept, came_a, came_b, total, sem, x_first):
        self.place, self.own, self.kept, self.came_a, self.came_b = place, own, kept, came_a, came_b
        self.total, self.sem, self.x_first = total, sem, x_first

    @staticmethod
    def scratch(rows, width):
        block = rows // 4
        return [pltpu.VMEM((2, block, width), BF)] * 2 + [pltpu.VMEM((block, width), BF)] * 2 + [DMA((5,))]

    def load(self):
        p = self.place
        part = self.own.at[p.h] if self.x_first else self.own.at[:, p.y]
        return pltpu.make_async_copy(part, self.kept, self.sem.at[0])

    def hop_a(self):
        p = self.place
        if self.x_first:
            part, device = self.own.at[1 - p.h], p.device(dh=1)
        else:
            part, device = self.own.at[:, 1 - p.y], p.device(dy=1)
        return remote(part, self.came_a, self.sem.at[1], self.sem.at[2], device)

    def hop_b(self):
        p = self.place
        if self.x_first:
            part, device = self.kept.at[1 - p.y], p.device(dy=1)
        else:
            part, device = self.kept.at[1 - p.h], p.device(dh=1)
        return remote(part, self.came_b, self.sem.at[3], self.sem.at[4], device)

    def begin_a(self):
        self.hop_a().start()
        self.load().start()

    def finish_a(self):
        self.load().wait()
        self.hop_a().wait()
        self.kept[...] = self.kept[...] + self.came_a[...]

    def begin_b(self):
        self.hop_b().start()

    def finish_b(self):
        self.hop_b().wait()
        side = self.place.y if self.x_first else self.place.h
        self.total[...] = self.kept[side] + self.came_b[...]


class SidePlane:
    def __init__(self, place, own, kept, came_a, came_b, total, sem, side):
        self.place, self.own, self.kept, self.came_a, self.came_b = place, own, kept, came_a, came_b
        self.total, self.sem, self.side = total, sem, side

    @staticmethod
    def scratch(rows, width):
        return [pltpu.VMEM((rows // 4, width), BF)] * 4 + [DMA((4,))]

    def hop_a(self):
        p = self.place
        return remote(self.own.at[0, 1 - p.y], self.came_a, self.sem.at[0], self.sem.at[1], p.device(dy=1))

    def hop_b(self):
        return remote(self.kept, self.came_b, self.sem.at[2], self.sem.at[3], self.place.device(dh=1))

    def begin_a(self):
        self.hop_a().start()

    def finish_a(self):
        self.hop_a().wait()
        self.kept[...] = self.own[0, self.place.y] + self.came_a[...]

    def begin_b(self):
        pl.when(self.place.h != self.side)(lambda: self.hop_b().start())

    def finish_b(self):
        pl.when(self.place.h != self.side)(lambda: self.hop_b().wait_send())

        def arrived():
            self.hop_b().wait_recv()
            self.total[...] = self.kept[...] + self.came_b[...]

        pl.when(self.place.h == self.side)(arrived)


class Column:
    def __init__(self, place, total, came, held, sem):
        self.place, self.total, self.came, self.held, self.sem = place, total, came, held, sem
        self.steps = place.deep.bit_length() - 1

    @staticmethod
    def scratch(deep, rows, width):
        return [pltpu.VMEM((rows // 4, width), BF)] * 2 + [DMA((4 * deep,))]

    def block(self, k):
        size, first = self.total.shape[0], 0
        for i in range(k):
            size //= 2
            first = first + lax.rem(lax.div(self.place.z, 1 << i), 2) * size
        return first

    def partner(self, k):
        bit = lax.rem(lax.div(self.place.z, 1 << k), 2)
        return self.place.device(dz=self.place.deep + (1 << k) - 2 * (1 << k) * bit)

    def rows(self, first, k):
        size = self.total.shape[0] >> k
        return pl.ds(pl.multiple_of(first, size), size)

    def fold(self, k):
        size = self.total.shape[0] >> (k + 1)
        other = 2 * self.block(k) + size - self.block(k + 1)
        arrived = self.came.at[pl.ds(self.total.shape[0] - 2 * size, size)]
        return remote(self.total.at[self.rows(other, k + 1)], arrived, self.sem.at[2 * k], self.sem.at[2 * k + 1], self.partner(k))

    def unfold(self, k):
        mine = self.held.at[self.rows(self.block(k + 1), k + 1)]
        n = 2 * self.steps + 2 * k
        return remote(mine, mine, self.sem.at[n], self.sem.at[n + 1], self.partner(k))

    def folded(self, k):
        self.fold(k).wait()
        size = self.total.shape[0] >> (k + 1)
        rows = self.rows(self.block(k + 1), k + 1)
        out = self.held if k == self.steps - 1 else self.total
        out[rows, :] = self.total[rows, :] + self.came[self.total.shape[0] - 2 * size : self.total.shape[0] - size, :]

    def hops(self):
        down = [(lambda k=k: self.fold(k).start(), lambda k=k: self.folded(k)) for k in range(self.steps)]
        up = [(lambda k=k: self.unfold(k).start(), lambda k=k: self.unfold(k).wait()) for k in reversed(range(self.steps))]
        return down + up


class ColumnDirect:
    def __init__(self, place, total, came, held, sem):
        self.place, self.total, self.came, self.held, self.sem = place, total, came, held, sem
        self.size = total.shape[0] // place.deep

    def block(self, ref, z):
        return ref.at[at(z, self.size)]

    def split(self):
        p, n = self.place, self.place.deep
        return [
            remote(self.block(self.total, lax.rem(p.z + j, n)), self.came.at[pl.ds((j - 1) * self.size, self.size)],
                   self.sem.at[j], self.sem.at[n + j], p.device(dz=j))
            for j in range(1, n)
        ]

    def spread(self):
        p, n = self.place, self.place.deep
        mine = self.block(self.held, p.z)
        return [remote(mine, mine, self.sem.at[2 * n + j], self.sem.at[3 * n + j], p.device(dz=j)) for j in range(1, n)]

    def summed(self):
        copies = self.split()
        for copy in copies:
            copy.wait()
        rows = at(self.place.z, self.size)
        value = self.total[rows, :].astype(F32)
        for j in range(self.place.deep - 1):
            value = value + self.came[j * self.size : (j + 1) * self.size, :].astype(F32)
        self.held[rows, :] = value.astype(BF)

    def hops(self):
        return [
            (lambda: start(*self.split()), self.summed),
            (lambda: start(*self.spread()), lambda: wait(*self.spread())),
        ]


class Spread:
    def __init__(self, place, held, out, sem):
        self.place, self.held, self.out, self.sem = place, held, out, sem

    def quarter(self):
        return self.out.at[at(self.place.core * 2 + self.place.y, self.held.shape[0])]

    def keep(self):
        return pltpu.make_async_copy(self.held, self.quarter(), self.sem.at[0])

    def along(self):
        return remote(self.held, self.quarter(), self.sem.at[1], self.sem.at[2], self.place.device(dy=1))

    def cross(self):
        part = self.out.at[at(self.place.core, 2 * self.held.shape[0])]
        return remote(part, part, self.sem.at[3], self.sem.at[4], self.place.device(dcore=1))

    def begin_y(self):
        self.keep().start()
        self.along().start()

    def finish_y(self):
        self.keep().wait()
        self.along().wait()

    def hops(self):
        return [(self.begin_y, self.finish_y), (lambda: self.cross().start(), lambda: self.cross().wait())]


def chain(place, kind, buffers, done, x_first=False, side=None, own=None):
    buffers = list(buffers)
    take = lambda n: [buffers.pop(0) for _ in range(n)]
    hops = []
    if kind is None:
        grads, own, came, sem = take(4)
        core = CoreSum(place, grads, own, came, sem)
        hops.append((core.begin, core.finish))
    if side is None:
        plane = Plane(place, own, *take(5), x_first)
    else:
        plane = SidePlane(place, own, *take(5), side)
    came, held, column_sem, spread_sem = take(4)
    if kind != "kept":
        hops.append((plane.begin_a, plane.finish_a))
    hops.append((plane.begin_b, plane.finish_b))
    column = (Column if side is None else ColumnDirect)(place, plane.total, came, held, column_sem)
    rest = column.hops() + Spread(place, held, done, spread_sem).hops()
    if side is not None:
        here = lambda stage: lambda: pl.when(place.h == side)(stage)
        rest = [(here(begin), here(finish)) for begin, finish in rest]
    hops += rest

    def joint(finish, begin):
        def stage():
            finish()
            begin()

        return stage

    return [hops[0][0]] + [joint(a[1], b[0]) for a, b in zip(hops, hops[1:])] + [hops[-1][1]]


def chain_scratch(deep, rows, width, kind=None, sides=2):
    parts = []
    if kind is None:
        parts += [pltpu.VMEM((sides, rows, width), BF), pltpu.VMEM((sides, 2, rows // 4, width), BF)] + CoreSum.scratch(rows, width, sides)
    parts += (Plane if sides == 2 else SidePlane).scratch(rows, width)
    return parts + Column.scratch(deep, rows, width) + [DMA((5,))]


class Moves:
    def __init__(self, sem):
        self.sem, self.used = sem, 0

    def copy(self, src, dst):
        self.used += 1
        return pltpu.make_async_copy(src, dst, self.sem.at[self.used - 1])

    def blocks(self, src, dst, count, size=ROWS):
        first = self.used
        self.used += count
        return lambda i: pltpu.make_async_copy(src.at[at(i, size)], dst.at[at(i, size)], self.sem.at[first + i])

    def pairs(self, sources, targets):
        first, many = self.used, len(sources)
        self.used += many * (HEADS // 2)

        def copies(i):
            lanes = at(head_pair(i), 128)
            return [
                pltpu.make_async_copy(src.at[:, lanes], dst.at[:, lanes], self.sem.at[first + i * many + j])
                for j, (src, dst) in enumerate(zip(sources, targets))
            ]

        return copies


def start(*copies):
    for copy in copies:
        copy.start()


def wait(*copies):
    for copy in copies:
        copy.wait()


def self_fwd_kernel(
    deep, tokens, memory, out_cot, qkv_w, out_w, cq_w, lengths, gain, bias,
    row_came, memory_came, cot_came, key_own, value_own, q, k, v, mix, ext, normed, inverse, cq, qe, ke, live,
    row_s, qkv_s, out_s, cqw_s, q_s, k_s, v_s, mix_s, ext_s, normed_s, inverse_s, cq_s, qe_s, ke_s, live_s, kx_s, vx_s, memory_s, kv_s, key_s, value_s,
    sem, sem_far,
):
    place = Place(deep)
    h = place.h
    half = tokens.shape[1]
    row_length, width = row_s.shape
    blocks = row_length // ROWS
    lower, upper = pl.ds(0, half), pl.ds(half, half)
    place.greet("dh")
    moves = Moves(sem)
    own_row = moves.copy(tokens.at[h], row_s.at[lower])
    get_w = moves.copy(qkv_w, qkv_s)
    late = [moves.copy(out_w, out_s), moves.copy(cq_w.at[0], cqw_s)]
    get_memory = [moves.copy(memory.at[h], memory_s), moves.copy(cq_w.at[pl.ds(1, 2)], kv_s)]
    start(own_row, get_w)
    partner = place.device(dh=1)
    send_row = remote(tokens.at[1 - h], row_s.at[upper], sem_far.at[0], sem_far.at[1], partner)
    send_memory = remote(memory.at[1 - h], memory_came, sem_far.at[2], sem_far.at[3], partner)
    send_cot = remote(out_cot.at[1 - h, pl.ds(0, half // 2)], cot_came, sem_far.at[4], sem_far.at[5], partner)
    place.met()
    send_row.start()

    position = lax.broadcasted_iota(jnp.int32, (row_length, 128), 0)
    position = jnp.where(h == 0, position, lax.rem(position + half, row_length))
    segment = jnp.zeros((row_length, 128), jnp.int32)
    following = jnp.zeros((row_length, 128), jnp.int32)
    end = 0
    for j in range(lengths.shape[1]):
        end = end + lengths[h, j]
        segment = segment + (position >= end).astype(jnp.int32)
        following = following + (position + 1 >= end).astype(jnp.int32)
    live_s[...] = ((following == segment) & (position + 1 < row_length)).astype(F32).astype(BF)
    spare = lax.rem(lax.broadcasted_iota(jnp.int32, (row_length, 128), 1), 64)
    coded, hit = spare < lengths.shape[1], segment == spare
    qe_s[...] = jnp.where(coded & hit, BIG, 0.0).astype(BF)
    ke_s[...] = jnp.where(coded, jnp.where(hit, 0.0, -BIG), jnp.where(spare < 7, 1.0, 0.0)).astype(BF)

    def project(i):
        rows = at(i, ROWS)
        x = row_s[rows, :]
        q_s[rows, :] = dot(x, qkv_s[0]).astype(BF) * jnp.asarray(0.125, BF)
        k_s[rows, :] = dot(x, qkv_s[1]).astype(BF)
        v_s[rows, :] = dot(x, qkv_s[2]).astype(BF)

    wait(own_row, get_w)
    start(*get_memory)
    loop(blocks // 2, project)
    wait(*get_memory)
    key_s[...] = dot(memory_s[...], kv_s[0]).astype(BF)
    value_s[...] = dot(memory_s[...], kv_s[1]).astype(BF)
    send_row.wait()
    start(send_memory, send_cot)
    loop(blocks, project, blocks // 2)
    pairs = ((row_s.at[upper], row_came), (q_s, q), (k_s, k), (v_s, v), (qe_s, qe), (ke_s, ke), (live_s, live),
             (key_s, key_own), (value_s, value_own))
    outward = [moves.copy(src, dst) for src, dst in pairs]
    start(*outward, *late)
    attend(q_s, k_s, v_s, qe_s, ke_s, mix_s, ext_s, kx_s, vx_s)
    mixed = [moves.copy(mix_s, mix), moves.copy(ext_s, ext)]
    start(*mixed)
    wait(*late)
    by_block = [moves.blocks(src, dst, blocks) for src, dst in ((normed_s, normed), (inverse_s, inverse), (cq_s, cq))]

    def after(i):
        rows = at(i, ROWS)
        n, s = normalise(row_s[rows, :].astype(F32) + dot(mix_s[rows, :], out_s[...]))
        normed_s[rows, :] = n
        inverse_s[rows, :] = s
        low = (n * gain[0:1, :] + bias[0:1, :]).astype(BF)
        cq_s[rows, :] = dot(low, cqw_s[...]).astype(BF) * jnp.asarray(0.125, BF)
        start(*[copy(i) for copy in by_block])

    loop(blocks, after)
    wait(*outward, *mixed)
    loop(blocks, lambda i: wait(*[copy(i) for copy in by_block]))
    wait(send_memory, send_cot)


def cross_fwd_kernel(
    deep, slot_cot, memory_came, key_own, value_own, kv_w, cq, qe, ke, out_w, normed_one, slot_mask, gain, bias,
    slot_own, slot_came, k, v, mix, ext, normed, inverse,
    memory_s, kv_s, cq_s, qe_s, ke_s, out_s, first_s, k_s, v_s, mix_s, ext_s, normed_s, inverse_s, kx_s, vx_s, masked, sem, sem_far,
):
    place = Place(deep)
    h = place.h
    half = slot_cot.shape[1]
    place.greet("dh")
    moves = Moves(sem)
    blocks = k_s.shape[0] // ROWS
    get_slots = moves.copy(slot_cot, masked)
    get_memory = moves.copy(memory_came, memory_s)
    lower, upper = pl.ds(0, half), slice(half, 2 * half)
    get_own = [moves.copy(key_own, k_s.at[lower]), moves.copy(value_own, v_s.at[lower])]
    get_w = moves.copy(kv_w.at[pl.ds(1, 2)], kv_s)
    soon = [moves.copy(src, dst) for src, dst in ((cq, cq_s), (qe, qe_s), (ke, ke_s))]
    late = [moves.copy(src, dst) for src, dst in ((out_w, out_s), (normed_one, first_s))]
    send = remote(masked.at[1 - h], slot_came, sem_far.at[0], sem_far.at[1], place.device(dh=1))
    start(get_w, get_memory, get_slots, *get_own, *soon)
    wait(get_w, get_memory)

    place.met()
    get_slots.wait()
    columns = slot_mask[...].astype(F32).T
    for r in range(2):
        masked[r] = masked[r] * columns[:, r : r + 1].astype(BF)
    send.start()
    k_s[upper, :] = dot(memory_s[...], kv_s[0]).astype(BF)
    v_s[upper, :] = dot(memory_s[...], kv_s[1]).astype(BF)
    wait(*get_own)
    outward = [moves.copy(k_s, k), moves.copy(v_s, v), moves.copy(masked.at[h], slot_own)]
    wait(*soon)
    start(*outward, *late)
    attend(cq_s, k_s, v_s, qe_s, ke_s, mix_s, ext_s, kx_s, vx_s)
    mixed = [moves.copy(mix_s, mix), moves.copy(ext_s, ext)]
    start(*mixed)
    wait(*late)
    by_block = [moves.blocks(src, dst, blocks) for src, dst in ((normed_s, normed), (inverse_s, inverse))]

    def after(i):
        rows = at(i, ROWS)
        before = first_s[rows, :] * gain[0:1, :] + bias[0:1, :]
        n, s = normalise(before + dot(mix_s[rows, :], out_s[...]))
        normed_s[rows, :] = n
        inverse_s[rows, :] = s
        start(*[copy(i) for copy in by_block])

    loop(blocks, after)
    wait(*outward, *mixed)
    loop(blocks, lambda i: wait(*[copy(i) for copy in by_block]))
    send.wait()


def ffn_kernel(
    deep, normed_two, in_w, out_w, slot_w, slot_own, slot_came, out_cot, cot_first, live, inverse_two, cross_out_w, cross_mix,
    gain, bias,
    out_home, slots_home, res_two, grad_mix, sum_out, sum_slot, sum_in, sums,
    two_s, inw_s, outw_s, slotw_s, slot_s, cot_s, live_s, inverse_two_s, crossw_s, mix_s,
    low_s, hidden_s, slope_s, normed_s, inverse_s, pair_s, next_s, gnext_s, res_s, ginner_s, res_two_s, res_low_s, gmix_s, slots_s,
    g_out, g_slot, g_in, own_out, own_slot, own_in, came_out, sem_out, came_slot, sem_slot, came_in, sem_in,
    kept_slot, hop_slot, plane_sem, sem, sem_far,
):
    row_length, width = low_s.shape
    blocks = row_length // ROWS
    units = in_w.shape[1]
    half = row_length // 2
    place = Place(deep)
    place.greet("dh", "dcore", "dy")
    h = place.h
    scale = 0.7978845608028654
    moves = Moves(sem)
    get_two = moves.blocks(normed_two, two_s, blocks)
    first = [moves.copy(in_w, inw_s), moves.copy(out_w, outw_s)]
    lower, upper, quarter = pl.ds(0, half), pl.ds(half, half), half // 2
    soon = [
        moves.copy(src, dst)
        for src, dst in ((slot_w, slotw_s), (slot_own, slot_s.at[lower]), (slot_came, slot_s.at[upper]), (live, live_s))
    ]
    late = [
        moves.copy(src, dst)
        for src, dst in ((out_cot.at[h], cot_s.at[lower]), (cot_first, cot_s.at[pl.ds(half, quarter)]), (inverse_two, inverse_two_s), (cross_out_w, crossw_s), (cross_mix, mix_s))
    ]
    work_out = CoreSum(place, g_out, own_out, came_out, sem_out)
    work_slot = CoreSum(place, g_slot, own_slot, came_slot, sem_slot)
    work_in = CoreSum(place, g_in, own_in, came_in, sem_in)
    plane_slot = Plane(place, own_slot, kept_slot, hop_slot, None, None, plane_sem, False)

    def home(src, dst, i):
        lanes = pl.ds(0, width)
        return (
            moves.copy(src.at[lower, lanes], dst.at[h]),
            remote(src.at[upper, lanes], dst.at[h], sem_far.at[2 * i], sem_far.at[2 * i + 1], place.device(dh=1)),
        )

    homeward = home(pair_s, out_home, 0) + home(slots_s, slots_home, 1)
    cot_rest = remote(
        out_cot.at[1 - h, pl.ds(quarter, quarter)], cot_s.at[pl.ds(half + quarter, quarter)], sem_far.at[4], sem_far.at[5], place.device(dh=1)
    )
    last = blocks - 1
    get_two(last).start()
    start(*first)
    loop(last, lambda i: get_two(i).start())
    start(*soon, *late)
    place.met()
    cot_rest.start()
    wait(*first)

    def forward(i):
        rows = at(i, ROWS)
        get_two(i).wait()
        after_cross = two_s[rows, :] * gain[1:2, :] + bias[1:2, :]
        low = after_cross.astype(BF)
        low_s[rows, :] = low
        for c in range(units // 512):
            cols = slice(c * 512, (c + 1) * 512)
            inner = dot(low, inw_s[:, cols])
            square = inner * inner
            bent = jnp.tanh(inner * (scale + (scale * 0.044715) * square))
            part = 0.5 + 0.5 * bent
            hidden_s[rows, cols] = (inner * part).astype(BF)
            slope = part + inner * (0.5 - 0.5 * bent * bent) * (scale + (3 * scale * 0.044715) * square)
            slope_s[rows, cols] = slope.astype(BF)
        n, s = normalise(after_cross + dot(hidden_s[rows, :], outw_s[...]))
        normed_s[rows, :] = n
        inverse_s[rows, :] = s
        final = (n * gain[2:3, :] + bias[2:3, :]).astype(BF)
        pair_s[rows, :width] = final
        next_s[rows, :] = final.astype(F32)

    def backwards(body, sent):
        def one(i):
            body(last - i)
            pl.when(i == (blocks - 1) // 2)(sent)

        loop(blocks, one)

    backwards(forward, lambda: homeward[1].start())
    homeward[0].start()
    next_s[pl.ds(row_length, 8), :] = next_s[pl.ds(0, 8), :]
    wait(*soon)

    def slot(i):
        rows = at(i, ROWS)
        window = pl.ds(pl.multiple_of(i * ROWS, ROWS), ROWS + 8)
        alive = live_s[rows, 0:1].astype(F32)
        pair_s[rows, width:] = (next_s[window, :][1 : ROWS + 1] * alive).astype(BF)
        slots_s[rows, :] = dot(pair_s[rows, :], slotw_s[...]).astype(BF)
        back = (dot_nt(slot_s[rows, :], slotw_s[width:, :]) * alive).astype(BF)
        gnext_s[pl.ds(pl.multiple_of(i * ROWS + 8, 8), ROWS), :] = back.astype(F32)

    backwards(slot, lambda: homeward[3].start())
    homeward[2].start()
    gnext_s[pl.ds(0, 8), :] = gnext_s[pl.ds(row_length, 8), :]
    sums[...] = jnp.zeros(sums.shape, F32)
    fill(g_slot, width)
    for side in range(2):
        g_slot[side, :width, :] = dot_tn(pair_s[:, side * width : (side + 1) * width], slot_s[...]).astype(BF)
    work_slot.begin()
    wait(*late)
    cot_rest.wait()
    by_block = [moves.blocks(src, dst, blocks) for src, dst in ((res_two_s, res_two), (gmix_s, grad_mix))]

    def backward(i):
        @pl.when(i == 1)
        def slot_hop():
            work_slot.finish()
            plane_slot.begin_a()

        rows = at(i, ROWS)
        window = pl.ds(pl.multiple_of(i * ROWS, ROWS), ROWS + 8)
        gradient = (
            cot_s[rows, :].astype(F32)
            + dot_nt(slot_s[rows, :], slotw_s[:width, :])
            + gnext_s[window, :][7 : ROWS + 7]
        )
        n = normed_s[rows, :]
        sums[0:1, :] += jnp.sum(gradient * n, axis=0, keepdims=True)
        sums[1:2, :] += jnp.sum(gradient, axis=0, keepdims=True)
        res = norm_back(gradient, n, inverse_s[rows, :], gain[2:3, :])
        res_low = res.astype(BF)
        res_s[rows, :] = res_low
        for c in range(units // 512):
            cols = slice(c * 512, (c + 1) * 512)
            ginner_s[rows, cols] = (dot_nt(res_low, outw_s[cols, :]) * slope_s[rows, cols].astype(F32)).astype(BF)
        res = res + dot_nt(ginner_s[rows, :], inw_s[...])
        n = two_s[rows, :]
        sums[2:3, :] += jnp.sum(res * n, axis=0, keepdims=True)
        sums[3:4, :] += jnp.sum(res, axis=0, keepdims=True)
        res = norm_back(res, n, inverse_two_s[rows, :], gain[1:2, :])
        res_two_s[rows, :] = res
        res_low = res.astype(BF)
        res_low_s[rows, :] = res_low
        gmix_s[rows, :] = dot_nt(res_low, crossw_s[...]).astype(BF)
        start(*[copy(i) for copy in by_block])

    loop(blocks, backward)
    fill(g_out, units // 2 + width // 2)
    fill(g_in, width * units // 1024)
    for side in range(2):
        g_out[side, units // 2 : units // 2 + width // 2, :] = dot_tn(
            mix_s[:, side * 256 : (side + 1) * 256], res_low_s[...]
        ).astype(BF)
    for side in range(2):
        g_out[side, : units // 2, :] = dot_tn(hidden_s[:, side * (units // 2) : (side + 1) * (units // 2)], res_s[...]).astype(BF)
    work_out.begin()
    for c in range(units // 512):
        side, block = divmod(c, units // 1024)
        g_in[side, block * width : (block + 1) * width, :] = dot_tn(low_s[...], ginner_s[:, c * 512 : (c + 1) * 512]).astype(BF)
    work_in.begin()
    done = [moves.copy(src, dst) for src, dst in ((own_out, sum_out), (kept_slot, sum_slot), (own_in, sum_in))]
    for finish, copy in zip((work_out.finish, plane_slot.finish_a, work_in.finish), done):
        finish()
        copy.start()
    loop(blocks, lambda i: wait(*[copy(i) for copy in by_block]))
    wait(*done, *homeward)


def fill(grads, used):
    rest = grads.shape[1] - used
    if rest:
        grads[:, used:, :] = jnp.zeros((grads.shape[0], rest, grads.shape[2]), BF)


def weight_grads(grads, pairs, sources):
    for left, rights, first in sources:
        right = jnp.concatenate([d[:, p * 128 : (p + 1) * 128] for d in rights for p in pairs], axis=1)
        width = left.shape[1]
        block = dot_tn(left[...], right).astype(BF)
        for i in range(len(rights)):
            for side in range(len(pairs)):
                lane = (i * len(pairs) + side) * 128
                grads[side, (first + i) * width : (first + i + 1) * width, :] = block[:, lane : lane + 128]


PLAN = {
    "begin": (("out", 0), ("in", 0), ("slot", 0),),
    "c0": (("slot", 1),),
    "c1": (("slot", 2),),
    "c2": (("slot", 3),),
    "c3": (("d1", 0), ("slot", 4),),
    "c4": (("d1", 1), ("slot", 5),),
    "c6": (("d1", 2), ("in", 1),),
    "c7": (("out", 1), ("slot", 6),),
    "c8": (("d1", 3),),
    "c9": (("d2", 0), ("in", 2),),
    "c10": (("d1", 4), ("mem", 0),),
    "s0": (("d2", 1), ("d1", 5), ("in", 3),),
    "s1": (("out", 2),),
    "s2": (("d1", 6), ("in", 4),),
    "s3": (("e1", 0), ("d2", 2), ("d1", 7), ("out", 3),),
    "s4": (("e1", 1), ("d1", 8), ("in", 5),),
    "s5": (("e2", 0), ("d2", 3), ("out", 4),),
    "s6": (("e2", 1), ("e1", 2), ("d2", 4), ("in", 6),),
    "s7": (("d2", 5), ("out", 5),),
    "s8": (("f", 0), ("e1", 3),),
    "s9": (("e2", 2), ("row", 0),),
    "s10": (("f", 1), ("d2", 6),),
    "tail": (("e1", 4), ("in", 7), ("out", 6), ("e1", 5), ("f", 2), ("d2", 7), ("e2", 3), ("e1", 6), ("e2", 4), ("f", 3),
        ("e1", 7), ("e2", 5), ("f", 4), ("d2", 8), ("f", 5), ("e2", 6), ("e1", 8), ("out", 7), ("f", 6), ("out", 8),
        ("in", 8), ("slot", 7), ("d1", 9), ("d2", 9), ("e1", 9), ("e2", 7), ("row", 1), ("mem", 1), ("f", 7),),
}


def back_kernel(
    deep, own_out, own_in, own_slot, cq, ck, cv, cext, cmix, gcmix, memory, memory_came, cross_w, res_two, normed_one, inverse_one,
    q, k, v, ext, mix, out_w, tokens, tokens_came, self_w, ke, gain, bias, sums_two,
    done_out, done_in, done_slot, done_d1, done_d2, done_e, done_f, mem_mine, mem_came, row_mine, row_came,
    q_s, k_s, v_s, ext_s, mix_s, gmix_s, memory_s, row_s, low_s, dq_s, dk_s, dv_s, res_s, cross_ws, self_ws, outw_s,
    res_two_s, normed_s, res_one_s, inverse_s, sums, mine_s, theirs_s, row_theirs,
    kx_s, vx_s, qx_s, dx_s, extra_s, kt_s, dqt_s, sem, sem_far, *comm,
):
    row_length, width = row_s.shape
    blocks = row_length // ROWS
    half_blocks = blocks // 2
    half = row_length // 2
    lower, upper = pl.ds(0, half), pl.ds(half, half)
    place = Place(deep)
    place.greet("dh", "dy", "dz", "dcore")
    moves = Moves(sem)
    cross_pairs = moves.pairs((cq, ck, cv, cext, cmix, gcmix), (q_s, k_s, v_s, ext_s, mix_s, gmix_s))
    late = [
        moves.copy(src, dst)
        for src, dst in ((normed_one, normed_s), (memory.at[place.h], memory_s.at[lower]), (memory_came, memory_s.at[upper]),
                         (cross_w, cross_ws), (inverse_one, inverse_s), (res_two, res_two_s), (out_w, outw_s),
                         (tokens.at[place.h], row_s.at[lower]), (tokens_came, row_s.at[upper]), (self_w, self_ws))
    ]
    again = [moves.copy(src, dst) for src, dst in ((q, q_s), (k, k_s), (v, v_s), (ext, ext_s), (mix, mix_s))]
    loop(HEADS // 2, lambda i: start(*cross_pairs(i)))
    comm = list(comm)
    take = lambda n: [comm.pop(0) for _ in range(n)]
    get_slot = moves.copy(own_slot, comm[18])
    get_slot.start()
    chains = {
        "out": chain(place, "own", take(9), done_out, False, own=own_out),
        "in": chain(place, "own", take(9), done_in, False, own=own_in),
        "slot": chain(place, "kept", take(9), done_slot, False),
    }
    grads = {}
    for name, done, x_first, side in (("d1", done_d1, True, None), ("d2", done_d2, False, None), ("e1", done_e, False, None),
                                      ("e2", done_f, False, 0), ("f", done_f, False, 1)):
        buffers = take(13)
        grads[name] = buffers[0]
        chains[name] = chain(place, None, buffers, done, x_first, side)
    mem_send = remote(theirs_s, mem_came, sem_far.at[0], sem_far.at[1], place.device(dh=1))
    row_send = remote(row_theirs, row_came, sem_far.at[2], sem_far.at[3], place.device(dh=1))
    chains["mem"] = [mem_send.start, mem_send.wait]
    chains["row"] = [row_send.start, row_send.wait]

    def run(point):
        for name, stage in PLAN.get(point, ()):
            chains[name][stage]()

    def hooks(letter, extra):
        table = {}
        for step in range(HEADS):
            point = letter + str(step)
            if step in extra or point in PLAN:
                def hook(point=point, step=step):
                    if step in extra:
                        extra[step]()
                    run(point)

                table[step] = hook
        return table

    def low_rows():
        wait(*late)

        def one(i):
            rows = at(i, ROWS)
            low_s[rows, :] = (normed_s[rows, :] * gain[0:1, :] + bias[0:1, :]).astype(BF)

        loop(blocks, one)

    cross_sources = ((low_s, (dq_s,), 0), (memory_s, (dk_s, dv_s), 1))
    self_sources = ((row_s, (dq_s, dk_s, dv_s), 0),)
    for name, used in (("d1", 3 * width), ("d2", 5 * width), ("e1", 3 * width + 16), ("e2", 3 * width), ("f", 3 * width)):
        fill(grads[name], used)
    place.met()
    get_slot.wait()
    run("begin")
    start(*late)
    scratch = (dq_s, dk_s, dv_s, kx_s, vx_s, qx_s, dx_s, extra_s, kt_s, dqt_s)
    attend_back(
        q_s, k_s, v_s, ext_s, ke, mix_s, gmix_s, *scratch,
        hooks("c", {1: low_rows, 3: lambda: weight_grads(grads["d1"], (0, 2), cross_sources)}), cross_pairs,
    )
    start(*again)
    sums[...] = jnp.zeros(sums.shape, F32)

    def backward(i):
        rows = at(i, ROWS)
        n = normed_s[rows, :]
        gradient = res_two_s[rows, :] + dot_nt(dq_s[rows, :], cross_ws[0])
        sums[0:1, :] += jnp.sum(gradient * n, axis=0, keepdims=True)
        sums[1:2, :] += jnp.sum(gradient, axis=0, keepdims=True)
        res = norm_back(gradient, n, inverse_s[rows, :], gain[0:1, :])
        res_one_s[rows, :] = res
        res_low = res.astype(BF)
        res_s[rows, :] = res_low
        gmix_s[rows, :] = dot_nt(res_low, outw_s[...]).astype(BF)

    loop(blocks, backward)
    run("c8")
    weight_grads(grads["d2"], (1, 3), cross_sources)
    wait(*again)
    for side in range(2):
        block = dot_tn(mix_s[:, side * 256 : (side + 1) * 256], res_s[...]).astype(BF)
        for c in range(width // 128):
            grads["d2"][side, 3 * width + c * 256 : 3 * width + (c + 1) * 256, :] = block[:, c * 128 : (c + 1) * 128]
    run("c9")
    put_mem = moves.blocks(mine_s, mem_mine, half_blocks)
    put_row = moves.blocks(mine_s, row_mine, half_blocks)

    def memory_grad(i):
        rows = at(i, ROWS)
        return dot_nt(dk_s[rows, :], cross_ws[1]) + dot_nt(dv_s[rows, :], cross_ws[2])

    def memory_theirs(i):
        theirs_s[at(i, ROWS), :] = memory_grad(i + half_blocks).astype(BF)

    def memory_mine(i):
        mine_s[at(i, ROWS), :] = memory_grad(i)
        put_mem(i).start()

    loop(half_blocks, memory_theirs)
    run("c10")
    loop(half_blocks, memory_mine)

    def first_grads():
        weight_grads(grads["e1"], (0, 2), self_sources)
        norms = jnp.concatenate(
            [sums[0:1, :], sums_two[2:3, :], sums_two[0:1, :], sums[1:2, :], sums_two[3:4, :], sums_two[1:2, :]], axis=0
        ).astype(BF)
        for side in range(2):
            parts = [norms[:, side * 256 + c * 128 : side * 256 + (c + 1) * 128] for c in range(2)]
            grads["e1"][side, 3 * width : 3 * width + 16, :] = jnp.concatenate(parts + [jnp.zeros((4, 128), BF)], axis=0)

    attend_back(
        q_s, k_s, v_s, ext_s, ke, mix_s, gmix_s, *scratch,
        hooks("s", {3: first_grads, 5: lambda: weight_grads(grads["e2"], (1,), self_sources)}), lambda i: (),
    )
    weight_grads(grads["f"], (3,), self_sources)
    run("s8")

    def row_grad(i):
        rows = at(i, ROWS)
        return (
            res_one_s[rows, :] + dot_nt(dq_s[rows, :], self_ws[0]) + dot_nt(dk_s[rows, :], self_ws[1]) + dot_nt(dv_s[rows, :], self_ws[2])
        )

    def row_other(i):
        row_theirs[at(i, ROWS), :] = row_grad(i + half_blocks).astype(BF)

    def row_own(i):
        put_mem(i).wait()
        mine_s[at(i, ROWS), :] = row_grad(i)
        put_row(i).start()

    loop(half_blocks, row_other)
    run("s9")
    loop(half_blocks, row_own)
    run("s10")
    run("tail")
    loop(half_blocks, lambda i: put_row(i).wait())


def finish_kernel(
    deep, out, slots, row_mine, row_came, mem_mine, mem_came, done_in, done_out, done_slot, done_d1, done_d2, done_e, done_f, slot_mask,
    out_f, slots_f, tokens_f, memory_f, self_qkv_f, self_out_f, cross_qkv_f, cross_out_f, norms_f, ffn_in_f, ffn_out_f, slot_f,
    slots_s, row_s, mem_s, in_s, outs_s, slot_s, d1_s, d2_s, e_s, f_s, masked_s, row_w, mem_w, in_w, out_w, slot_w, cross_w,
    cqkv_w, sout_w, sqkv_w, out_b, mem_b, row_b, sem,
):
    h = lax.axis_index("head")
    moves = Moves(sem)
    width = out.shape[2]
    loads = [
        moves.copy(src, dst)
        for src, dst in ((done_out, outs_s), (done_in, in_s), (done_slot, slot_s), (slots, slots_s), (mem_came, mem_s), (done_d1, d1_s),
                         (done_d2, d2_s), (row_came, row_s), (done_e, e_s), (done_f, f_s), (out, out_b), (mem_mine, mem_b), (row_mine, row_b))
    ]
    start(*loads)
    stores = []

    def put(src, dst):
        copy = moves.copy(src, dst)
        copy.start()
        stores.append(copy)

    half = out_w.shape[0]
    loads[0].wait()
    out_w[...] = outs_s[:half, :].astype(F32)
    put(out_w, ffn_out_f)
    loads[1].wait()
    for c in range(in_w.shape[1] // 512):
        in_w[:, c * 512 : (c + 1) * 512] = in_s[c * width : (c + 1) * width, :].astype(F32)
    put(in_w, ffn_in_f)
    cross_w[...] = outs_s[half : half + width // 2, :].astype(F32)
    put(cross_w, cross_out_f)
    loads[2].wait()
    slot_w[...] = slot_s[:width, :].astype(F32)
    put(slot_w, slot_f)
    loads[3].wait()
    columns = slot_mask[...].astype(F32).T
    for r in range(2):
        masked_s[r] = slots_s[r] * columns[:, r : r + 1].astype(BF)
    put(masked_s, slots_f)
    loads[4].wait()
    mem_w[...] = mem_s[...].astype(F32)
    put(mem_w, memory_f.at[1 - h])
    wait(loads[5], loads[6])
    for c, part_s in enumerate((d1_s, d2_s)):
        for part in range(3):
            cqkv_w[part, :, c * 128 : (c + 1) * 128] = part_s[part * width : (part + 1) * width, :].astype(F32)
    put(cqkv_w, cross_qkv_f)
    for c in range(width // 128):
        sout_w[:, c * 128 : (c + 1) * 128] = d2_s[3 * width + c * 256 : 3 * width + (c + 1) * 256, :].astype(F32)
    put(sout_w, self_out_f)
    loads[7].wait()
    row_w[...] = row_s[...].astype(F32)
    put(row_w, tokens_f.at[1 - h])
    wait(loads[8], loads[9])
    for c, part_s in enumerate((e_s, f_s)):
        for part in range(3):
            sqkv_w[part, :, c * 128 : (c + 1) * 128] = part_s[part * width : (part + 1) * width, :].astype(F32)
    norms = e_s[3 * width : 3 * width + 16, :].astype(F32)
    for c in range(2):
        norms_f[:, c * 128 : (c + 1) * 128] = norms[6 * c : 6 * c + 6]
    put(sqkv_w, self_qkv_f)
    for load, src, dst in zip(loads[10:], (out_b, mem_b, row_b), (out_f, memory_f.at[h], tokens_f.at[h])):
        load.wait()
        put(src, dst)
    wait(*stores)


def call(kernel, name, cid, args, outs, scratch, flops):
    if cid is None:
        params = pltpu.CompilerParams(vmem_limit_bytes=VMEM)
    else:
        params = pltpu.CompilerParams(collective_id=cid, has_side_effects=True, vmem_limit_bytes=VMEM)
    return pl.pallas_call(
        kernel,
        out_shape=[jax.ShapeDtypeStruct(shape, kind) for shape, kind, _ in outs],
        in_specs=[spec for _, spec in args],
        out_specs=[spec for _, _, spec in outs],
        scratch_shapes=scratch,
        compiler_params=params,
        cost_estimate=pl.CostEstimate(flops=flops, bytes_accessed=2**20, transcendentals=0),
        name=name,
    )(*[arg for arg, _ in args])


def padded(count, unit):
    return -(-count // unit) * unit


def per_device(
    tokens, memory, lengths, slot_mask, self_qkv, self_out, cross_qkv, cross_out,
    norm_gain, norm_bias, ffn_in, ffn_out, slot_proj, out_cot, slot_cot,
):
    local_len, width = tokens.shape[1:]
    units = ffn_in.shape[1]
    deep = lax.axis_size("dp") // 4
    row_length = 2 * local_len
    unit = 64 * deep
    rows_out, rows_slot, rows_in = padded(units // 2 + width // 2, unit), padded(width, unit), padded(width * units // 1024, unit)
    rows_d1, rows_d2, rows_e = padded(3 * width, unit), padded(5 * width, unit), padded(3 * width + 16, unit)
    dense = 2 * row_length * width * width
    scores = 2 * row_length * row_length * width

    def inner(*values):
        return [(value, INNER) for value in values]

    def outer(*values):
        return [(value, ANY) for value in values]

    def new(*shape, kind=BF, spec=INNER):
        return (shape, kind, spec)

    def scratch(*shape, kind=BF):
        return pltpu.VMEM(shape, kind)

    row, wide, column = (
        new(row_length, width, spec=ANY), new(row_length, width, kind=F32, spec=ANY), new(row_length, 1, kind=F32, spec=ANY)
    )
    small = new(row_length, 128, spec=ANY)
    row_s, wide_s, two_s = scratch(row_length, width), scratch(row_length, width, kind=F32), scratch(row_length, 256)
    tall_s, ring_s = scratch(row_length, units), scratch(row_length + 8, width, kind=F32)
    column_s, small_s, half_s = scratch(row_length, 1, kind=F32), scratch(row_length, 128), scratch(local_len, width)
    square_s, three_s = scratch(width, width), scratch(3, width, width)
    half_wide_s = scratch(local_len, width, kind=F32)

    half, part = new(local_len, width, spec=ANY), new(local_len // 2, width, spec=ANY)
    tokens_came, memory_came, cot_first, key_own, value_own, q, k, v, mix, ext, normed_one, inverse_one, cq, qe, ke, live = call(
        functools.partial(self_fwd_kernel, deep), "self_fwd", 0,
        outer(tokens, memory, out_cot, self_qkv, self_out, cross_qkv) + [(lengths, SCALARS)] + inner(norm_gain, norm_bias),
        [half, half, part, half, half] + [row] * 5 + [wide, column, row] + [small] * 3,
        [row_s, three_s, square_s, square_s] + [row_s] * 5 + [wide_s, column_s, row_s]
        + [small_s] * 3 + [two_s, two_s, half_s, scratch(2, width, width), half_s, half_s, DMA((40,)), DMA((6,))], 5 * dense + 8 * scores,
    )
    slot_own, slot_came, ck, cv, cmix, cext, normed_two, inverse_two = call(
        functools.partial(cross_fwd_kernel, deep), "cross_fwd", 1,
        outer(slot_cot, memory_came, key_own, value_own, cross_qkv, cq, qe, ke, cross_out, normed_one) + inner(slot_mask, norm_gain, norm_bias),
        [half, half] + [row] * 4 + [wide, column],
        [half_s, scratch(2, width, width), row_s, small_s, small_s, square_s, wide_s] + [row_s] * 4 + [wide_s, column_s]
        + [two_s, two_s, scratch(2, local_len, width), DMA((40,)), DMA((2,))], 3 * dense + 8 * scores,
    )
    home = new(2, local_len, width, spec=ANY)
    groups = ((rows_out, 512), (rows_slot, 512), (rows_in, 512))
    out, slots, res_two, grad_cmix, sum_out, sum_slot, sum_in, sums_two = call(
        functools.partial(ffn_kernel, deep), "ffn", 2,
        outer(normed_two, ffn_in, ffn_out, slot_proj, slot_own, slot_came, out_cot, cot_first, live, inverse_two, cross_out, cmix) + inner(norm_gain, norm_bias),
        [home, home, wide, row, new(2, 2, rows_out // 4, 512, spec=ANY), new(2, rows_slot // 4, 512, spec=ANY),
         new(2, 2, rows_in // 4, 512, spec=ANY), new(8, width, kind=F32)],
        [wide_s, scratch(width, units), scratch(units, width), scratch(2 * width, width), row_s, row_s, small_s, column_s, square_s, row_s]
        + [row_s, tall_s, tall_s, wide_s, column_s, scratch(row_length, 2 * width), ring_s, ring_s, row_s, tall_s, wide_s]
        + [row_s] * 3
        + [scratch(2, rows, lanes) for rows, lanes in groups] + [scratch(2, 2, rows // 4, lanes) for rows, lanes in groups]
        + [part for group in groups for part in CoreSum.scratch(*group)]
        + [scratch(2, rows_slot // 4, 512), scratch(2, rows_slot // 4, 512), DMA((5,)), DMA((40,)), DMA((6,))], 32 * dense,
    )
    back = [small_s] * 5 + [scratch(128, row_length), scratch(128, row_length, kind=F32)]

    half_wide = new(local_len, width, kind=F32, spec=ANY)
    late = ((rows_d1, 128, 2), (rows_d2, 128, 2), (rows_e, 128, 2), (rows_d1, 128, 1), (rows_d1, 128, 1))

    def whole(rows, lanes):
        return new(rows, lanes, spec=ANY)

    done_out, done_in, done_slot, done_d1, done_d2, done_e, done_f, mem_mine, mem_came, row_mine, row_came = call(
        functools.partial(back_kernel, deep), "back", 3,
        outer(sum_out, sum_in, sum_slot, cq, ck, cv, cext, cmix, grad_cmix, memory, memory_came, cross_qkv, res_two, normed_one,
              inverse_one, q, k, v, ext, mix, self_out, tokens, tokens_came, self_qkv) + inner(ke, norm_gain, norm_bias, sums_two),
        [whole(rows_out, 512), whole(rows_in, 512), whole(rows_slot, 512), whole(rows_d1, 128), whole(rows_d2, 128), whole(rows_e, 128),
         whole(rows_d1, 128), half_wide, half, half_wide, half],
        [row_s] * 13 + [three_s, three_s, square_s] + [wide_s] * 3 + [column_s, scratch(8, width, kind=F32), half_wide_s, half_s, half_s]
        + back + [DMA((60,)), DMA((4,))]
        + [part for rows in (rows_out, rows_in, rows_slot) for part in chain_scratch(deep, rows, 512, "own")]
        + [part for rows, lanes, sides in late for part in chain_scratch(deep, rows, lanes, None, sides)],
        22 * dense + 40 * scores,
    )

    def final(*shape, kind=F32):
        return new(*shape, kind=kind, spec=ANY)

    def wide_scratch(*shape):
        return scratch(*shape, kind=F32)

    pair_s = scratch(2, local_len, width)
    results = call(
        functools.partial(finish_kernel, deep), "finish", None,
        outer(out, slots, row_mine, row_came, mem_mine, mem_came, done_in, done_out, done_slot, done_d1, done_d2, done_e, done_f)
        + inner(slot_mask),
        [final(2, local_len, width, kind=BF)] * 2 + [final(2, local_len, width)] * 2
        + [final(3, width, 256), final(width // 2, width), final(3, width, 256), final(width // 2, width)]
        + [new(6, 256, kind=F32)] + [final(width, units // 2), final(units // 2, width), final(width, width)],
        [pair_s, half_s, half_s, scratch(rows_in, 512), scratch(rows_out, 512), scratch(rows_slot, 512), scratch(rows_d1, 128),
         scratch(rows_d2, 128), scratch(rows_e, 128), scratch(rows_d1, 128), pair_s, half_wide_s, half_wide_s, wide_scratch(width, units // 2),
         wide_scratch(units // 2, width), wide_scratch(width, width), wide_scratch(width // 2, width), wide_scratch(3, width, 256),
         wide_scratch(width // 2, width), wide_scratch(3, width, 256), pair_s, half_wide_s, half_wide_s, DMA((40,))], 0,
    )
    norms = results[8]
    return (*results[:8], norms[:3], norms[3:], *results[9:])


def solution(mesh):
    split = P("dp", "head", None)
    placed = (split, split, P("dp", None), P("dp", "head")) + (P(),) * 9 + (split, split)
    return jax.shard_map(
        per_device,
        mesh=mesh,
        in_specs=placed,
        out_specs=(
            split, split, split, split,
            P(None, None, "head"), P("head", None), P(None, None, "head"), P("head", None),
            P(None, "head"), P(None, "head"), P(None, "head"), P("head", None), P("head", None),
        ),
        check_vma=False,
    )
```

```python
import functools

import jax
import jax.numpy as jnp
from jax import lax
from jax.experimental import pallas as pl
from jax.experimental.pallas import tpu as pltpu
from jax.sharding import PartitionSpec as P

HEADS = 8
BF = jnp.bfloat16
F32 = jnp.float32
MESH = pl.DeviceIdType.MESH
NT = (((1,), (1,)), ((), ()))
TN = (((0,), (0,)), ((), ()))
BIG = 2.0**20
VMEM = 60 * 2**20
ROWS = 512
QBLOCK = 512
ANY = pl.BlockSpec(memory_space=pl.ANY)
INNER = pl.BlockSpec(memory_space=pltpu.VMEM)
SCALARS = pl.BlockSpec(memory_space=pltpu.SMEM)


def dot(a, b):
    return jnp.dot(a, b, preferred_element_type=F32)


def dot_nt(a, b):
    return lax.dot_general(a, b, NT, preferred_element_type=F32)


def dot_tn(a, b):
    return lax.dot_general(a, b, TN, preferred_element_type=F32)


def at(i, size):
    return pl.ds(pl.multiple_of(i * size, size), size)


def loop(count, body, first=0):
    def step(i, carry):
        body(i)
        return carry

    lax.fori_loop(first, count, step, 0)


def thirds(value):
    first = value.astype(BF)
    rest = value - first.astype(F32)
    second = rest.astype(BF)
    third = (rest - second.astype(F32)).astype(BF)
    return first, second, third


def normalise(value):
    average = jnp.mean(value, axis=-1, keepdims=True)
    centred = value - average
    inverse = lax.rsqrt(jnp.mean(centred * centred, axis=-1, keepdims=True) + 1e-05)
    return centred * inverse, inverse


def norm_back(gradient, normed, inverse, gain_row):
    scaled = gradient * gain_row
    inner_mean = jnp.mean(scaled, axis=-1, keepdims=True)
    cross_mean = jnp.mean(scaled * normed, axis=-1, keepdims=True)
    return inverse * (scaled - inner_mean - normed * cross_mean)


def run_hooks(hooks, step):
    for done, hook in hooks.items():
        if done >= 0:
            pl.when(step == done)(hook)


def attend(q_s, k_s, v_s, qe_ref, ke_ref, mix_s, ext_s, kx_s, vx_s):
    row_length = k_s.shape[0]
    block = 256
    wide_low = lax.broadcasted_iota(jnp.int32, (row_length, 128), 1) < 64
    lane = lax.broadcasted_iota(jnp.int32, (block, 128), 1)
    low = lane < 64
    spare = lax.rem(lane, 64)

    def pair(p):
        lanes = at(p, 128)
        parts = [slice(h * 128, (h + 1) * 128) for h in range(2)]
        for h in range(2):
            mine = wide_low if h == 0 else ~wide_low
            kx_s[:, parts[h]] = jnp.where(mine, k_s[:, lanes], ke_ref[...])
            vx_s[:, parts[h]] = jnp.where(mine, v_s[:, lanes], jnp.ones((), BF))

        def rows_of(t):
            return slice((t // 2) * block, (t // 2 + 1) * block)

        def scores_of(t):
            rows = rows_of(t)
            query = jnp.where(low if t % 2 == 0 else ~low, q_s[rows, lanes], qe_ref[rows, :])
            return dot_nt(query, kx_s[:, parts[t % 2]])

        many = 2 * (row_length // block)
        ahead, done = scores_of(0), []
        for t in range(many):
            scores = ahead
            if t + 1 < many:
                ahead = scores_of(t + 1)
            top = jnp.max(scores, axis=1, keepdims=True)
            probs = jnp.exp(scores - top).astype(BF)
            done.append((top, dot(probs, vx_s[:, parts[t % 2]])))
            if t % 2 == 1:
                rows = rows_of(t)
                (top_low, sum_low), (top_high, sum_high) = done[-2:]
                mixed = jnp.where(low, sum_low, sum_high)
                totals = jnp.where(low, sum_high, sum_low)
                first, second, third = thirds(jnp.where(low, top_high, top_low) + jnp.log(totals))
                ext_s[rows, lanes] = jnp.where(
                    spare == 4, -first, jnp.where(spare == 5, -second, jnp.where(spare == 6, -third, qe_ref[rows, :]))
                )
                mix_s[rows, lanes] = (mixed / pltpu.roll(totals, 64, 1)).astype(BF)

    loop(HEADS // 2, pair)


def head_pair(i):
    return lax.rem(i, 2) * 2 + lax.div(i, 2)


def attend_back(q_s, k_s, v_s, ext_s, ke_ref, mix_s, gmix_s, dq_s, dk_s, dv_s, kx_s, vx_s, qx_s, dx_s, extra_s, kt_s, dqt_s, hooks, get_pair):
    row_length = k_s.shape[0]
    block = QBLOCK
    lane = lax.broadcasted_iota(jnp.int32, (row_length, 128), 1)
    low = lane < 64
    spare = lax.rem(lane, 64)
    zero = jnp.zeros((), BF)

    def head(step):
        i, odd = lax.div(step, 2), lax.rem(step, 2)
        lanes = at(head_pair(i), 128)
        mine = lax.div(lane, 64) == odd

        @pl.when(odd == 0)
        def arrive():
            for copy in get_pair(i):
                copy.wait()
            product = gmix_s[:, lanes].astype(F32) * mix_s[:, lanes].astype(F32)
            inner_low = jnp.sum(jnp.where(low, product, 0.0), axis=1, keepdims=True)
            inner_high = jnp.sum(jnp.where(low, 0.0, product), axis=1, keepdims=True)
            first, second, third = thirds(jnp.where(low, inner_high, inner_low))
            extra_s[...] = jnp.where(spare == 0, -first, jnp.where(spare == 1, -second, jnp.where(spare == 2, -third, zero)))
            kt_s[...] = k_s[:, lanes].T

        kx_s[...] = jnp.where(mine, k_s[:, lanes], ke_ref[...])
        vx_s[...] = jnp.where(mine, v_s[:, lanes], jnp.ones((), BF))
        qx_s[...] = jnp.where(mine, q_s[:, lanes], ext_s[:, lanes])
        dx_s[...] = jnp.where(mine, gmix_s[:, lanes], extra_s[...])
        own = at(odd, 64)
        for j in range(row_length // block):
            cols = slice(j * block, (j + 1) * block)
            probs = jnp.exp(dot_nt(kx_s[...], qx_s[cols, :]))
            ds = (probs * dot_nt(vx_s[...], dx_s[cols, :])).astype(BF)
            dv = dot(probs.astype(BF), dx_s[cols, :])
            dk = dot(ds, qx_s[cols, :])
            acc_v, acc_k = (dv, dk) if j == 0 else (acc_v + dv, acc_k + dk)
            dqt_s[own, cols] = dot(kt_s[own, :], ds) * 0.125
        dk_s[:, lanes] = jnp.where(mine, acc_k.astype(BF), dk_s[:, lanes])
        dv_s[:, lanes] = jnp.where(mine, acc_v.astype(BF), dv_s[:, lanes])

        @pl.when(odd == 1)
        def turn():
            dq_s[:, lanes] = dqt_s[...].T.astype(BF)

        run_hooks(hooks, step)

    loop(HEADS, head)


class Place:
    def __init__(self, deep):
        dp = lax.axis_index("dp")
        self.deep = deep
        self.h = lax.axis_index("head")
        self.core = lax.rem(dp, 2)
        self.y = lax.rem(lax.div(dp, 2), 2)
        self.z = lax.div(dp, 4)

    def device(self, dh=0, dcore=0, dy=0, dz=None):
        h = 1 - self.h if dh else self.h
        core = 1 - self.core if dcore else self.core
        y = 1 - self.y if dy else self.y
        z = self.z if dz is None else lax.rem(self.z + dz, self.deep)
        return ((z * 2 + y) * 2 + core, h)

    def greet(self, *kinds):
        self.peers = []
        for kind in kinds:
            if kind == "dz":
                self.peers += [self.device(dz=j) for j in range(1, self.deep)]
            else:
                self.peers.append(self.device(**{kind: 1}))
        barrier = pltpu.get_barrier_semaphore()
        for peer in self.peers:
            pl.semaphore_signal(barrier, inc=1, device_id=peer, device_id_type=MESH)

    def met(self):
        pl.semaphore_wait(pltpu.get_barrier_semaphore(), len(self.peers))


def remote(src, dst, send, recv, device):
    return pltpu.make_async_remote_copy(
        src_ref=src, dst_ref=dst, send_sem=send, recv_sem=recv, device_id=device, device_id_type=MESH
    )


DMA = pltpu.SemaphoreType.DMA


class CoreSum:
    def __init__(self, place, src, own, came, sem):
        self.place, self.src, self.own, self.came, self.sem = place, src, own, came, sem

    @staticmethod
    def scratch(rows, width, sides=2):
        return [pltpu.VMEM((sides, rows // 2, width), BF), DMA((2,))]

    def cross(self):
        size = self.src.shape[1] // 2
        return remote(
            self.src.at[:, at(1 - self.place.core, size)], self.came, self.sem.at[0], self.sem.at[1], self.place.device(dcore=1)
        )

    def begin(self):
        self.cross().start()

    def finish(self):
        self.cross().wait()
        size = self.own.shape[2]
        for side in range(self.own.shape[0]):
            for yy in range(2):
                here = self.src[side, at(self.place.core * 2 + yy, size), :]
                self.own[side, yy] = here + self.came[side, yy * size : (yy + 1) * size, :]


class Plane:
    def __init__(self, place, own, kept, came_a, came_b, total, sem, x_first):
        self.place, self.own, self.kept, self.came_a, self.came_b = place, own, kept, came_a, came_b
        self.total, self.sem, self.x_first = total, sem, x_first

    @staticmethod
    def scratch(rows, width):
        block = rows // 4
        return [pltpu.VMEM((2, block, width), BF)] * 2 + [pltpu.VMEM((block, width), BF)] * 2 + [DMA((5,))]

    def load(self):
        p = self.place
        part = self.own.at[p.h] if self.x_first else self.own.at[:, p.y]
        return pltpu.make_async_copy(part, self.kept, self.sem.at[0])

    def hop_a(self):
        p = self.place
        if self.x_first:
            part, device = self.own.at[1 - p.h], p.device(dh=1)
        else:
            part, device = self.own.at[:, 1 - p.y], p.device(dy=1)
        return remote(part, self.came_a, self.sem.at[1], self.sem.at[2], device)

    def hop_b(self):
        p = self.place
        if self.x_first:
            part, device = self.kept.at[1 - p.y], p.device(dy=1)
        else:
            part, device = self.kept.at[1 - p.h], p.device(dh=1)
        return remote(part, self.came_b, self.sem.at[3], self.sem.at[4], device)

    def begin_a(self):
        self.hop_a().start()
        self.load().start()

    def finish_a(self):
        self.load().wait()
        self.hop_a().wait()
        self.kept[...] = self.kept[...] + self.came_a[...]

    def begin_b(self):
        self.hop_b().start()

    def finish_b(self):
        self.hop_b().wait()
        side = self.place.y if self.x_first else self.place.h
        self.total[...] = self.kept[side] + self.came_b[...]


class SidePlane:
    def __init__(self, place, own, kept, came_a, came_b, total, sem, side):
        self.place, self.own, self.kept, self.came_a, self.came_b = place, own, kept, came_a, came_b
        self.total, self.sem, self.side = total, sem, side

    @staticmethod
    def scratch(rows, width):
        return [pltpu.VMEM((rows // 4, width), BF)] * 4 + [DMA((4,))]

    def hop_a(self):
        p = self.place
        return remote(self.own.at[0, 1 - p.y], self.came_a, self.sem.at[0], self.sem.at[1], p.device(dy=1))

    def hop_b(self):
        return remote(self.kept, self.came_b, self.sem.at[2], self.sem.at[3], self.place.device(dh=1))

    def begin_a(self):
        self.hop_a().start()

    def finish_a(self):
        self.hop_a().wait()
        self.kept[...] = self.own[0, self.place.y] + self.came_a[...]

    def begin_b(self):
        pl.when(self.place.h != self.side)(lambda: self.hop_b().start())

    def finish_b(self):
        pl.when(self.place.h != self.side)(lambda: self.hop_b().wait_send())

        def arrived():
            self.hop_b().wait_recv()
            self.total[...] = self.kept[...] + self.came_b[...]

        pl.when(self.place.h == self.side)(arrived)


class Column:
    def __init__(self, place, total, came, held, sem):
        self.place, self.total, self.came, self.held, self.sem = place, total, came, held, sem
        self.steps = place.deep.bit_length() - 1

    @staticmethod
    def scratch(deep, rows, width):
        return [pltpu.VMEM((rows // 4, width), BF)] * 2 + [DMA((4 * deep,))]

    def block(self, k):
        size, first = self.total.shape[0], 0
        for i in range(k):
            size //= 2
            first = first + lax.rem(lax.div(self.place.z, 1 << i), 2) * size
        return first

    def partner(self, k):
        bit = lax.rem(lax.div(self.place.z, 1 << k), 2)
        return self.place.device(dz=self.place.deep + (1 << k) - 2 * (1 << k) * bit)

    def rows(self, first, k):
        size = self.total.shape[0] >> k
        return pl.ds(pl.multiple_of(first, size), size)

    def fold(self, k):
        size = self.total.shape[0] >> (k + 1)
        other = 2 * self.block(k) + size - self.block(k + 1)
        arrived = self.came.at[pl.ds(self.total.shape[0] - 2 * size, size)]
        return remote(self.total.at[self.rows(other, k + 1)], arrived, self.sem.at[2 * k], self.sem.at[2 * k + 1], self.partner(k))

    def unfold(self, k):
        mine = self.held.at[self.rows(self.block(k + 1), k + 1)]
        n = 2 * self.steps + 2 * k
        return remote(mine, mine, self.sem.at[n], self.sem.at[n + 1], self.partner(k))

    def folded(self, k):
        self.fold(k).wait()
        size = self.total.shape[0] >> (k + 1)
        rows = self.rows(self.block(k + 1), k + 1)
        out = self.held if k == self.steps - 1 else self.total
        out[rows, :] = self.total[rows, :] + self.came[self.total.shape[0] - 2 * size : self.total.shape[0] - size, :]

    def hops(self):
        down = [(lambda k=k: self.fold(k).start(), lambda k=k: self.folded(k)) for k in range(self.steps)]
        up = [(lambda k=k: self.unfold(k).start(), lambda k=k: self.unfold(k).wait()) for k in reversed(range(self.steps))]
        return down + up


class ColumnDirect:
    def __init__(self, place, total, came, held, sem):
        self.place, self.total, self.came, self.held, self.sem = place, total, came, held, sem
        self.size = total.shape[0] // place.deep

    def block(self, ref, z):
        return ref.at[at(z, self.size)]

    def split(self):
        p, n = self.place, self.place.deep
        return [
            remote(self.block(self.total, lax.rem(p.z + j, n)), self.came.at[pl.ds((j - 1) * self.size, self.size)],
                   self.sem.at[j], self.sem.at[n + j], p.device(dz=j))
            for j in range(1, n)
        ]

    def spread(self):
        p, n = self.place, self.place.deep
        mine = self.block(self.held, p.z)
        return [remote(mine, mine, self.sem.at[2 * n + j], self.sem.at[3 * n + j], p.device(dz=j)) for j in range(1, n)]

    def summed(self):
        copies = self.split()
        for copy in copies:
            copy.wait()
        rows = at(self.place.z, self.size)
        value = self.total[rows, :].astype(F32)
        for j in range(self.place.deep - 1):
            value = value + self.came[j * self.size : (j + 1) * self.size, :].astype(F32)
        self.held[rows, :] = value.astype(BF)

    def hops(self):
        return [
            (lambda: start(*self.split()), self.summed),
            (lambda: start(*self.spread()), lambda: wait(*self.spread())),
        ]


class Spread:
    def __init__(self, place, held, out, sem):
        self.place, self.held, self.out, self.sem = place, held, out, sem

    def quarter(self):
        return self.out.at[at(self.place.core * 2 + self.place.y, self.held.shape[0])]

    def keep(self):
        return pltpu.make_async_copy(self.held, self.quarter(), self.sem.at[0])

    def along(self):
        return remote(self.held, self.quarter(), self.sem.at[1], self.sem.at[2], self.place.device(dy=1))

    def cross(self):
        part = self.out.at[at(self.place.core, 2 * self.held.shape[0])]
        return remote(part, part, self.sem.at[3], self.sem.at[4], self.place.device(dcore=1))

    def begin_y(self):
        self.keep().start()
        self.along().start()

    def finish_y(self):
        self.keep().wait()
        self.along().wait()

    def hops(self):
        return [(self.begin_y, self.finish_y), (lambda: self.cross().start(), lambda: self.cross().wait())]


def chain(place, kind, buffers, done, x_first=False, side=None, own=None):
    buffers = list(buffers)
    take = lambda n: [buffers.pop(0) for _ in range(n)]
    hops = []
    if kind is None:
        grads, own, came, sem = take(4)
        core = CoreSum(place, grads, own, came, sem)
        hops.append((core.begin, core.finish))
    if side is None:
        plane = Plane(place, own, *take(5), x_first)
    else:
        plane = SidePlane(place, own, *take(5), side)
    came, held, column_sem, spread_sem = take(4)
    if kind != "kept":
        hops.append((plane.begin_a, plane.finish_a))
    hops.append((plane.begin_b, plane.finish_b))
    column = (Column if side is None else ColumnDirect)(place, plane.total, came, held, column_sem)
    rest = column.hops() + Spread(place, held, done, spread_sem).hops()
    if side is not None:
        here = lambda stage: lambda: pl.when(place.h == side)(stage)
        rest = [(here(begin), here(finish)) for begin, finish in rest]
    hops += rest

    def joint(finish, begin):
        def stage():
            finish()
            begin()

        return stage

    return [hops[0][0]] + [joint(a[1], b[0]) for a, b in zip(hops, hops[1:])] + [hops[-1][1]]


def chain_scratch(deep, rows, width, kind=None, sides=2):
    parts = []
    if kind is None:
        parts += [pltpu.VMEM((sides, rows, width), BF), pltpu.VMEM((sides, 2, rows // 4, width), BF)] + CoreSum.scratch(rows, width, sides)
    parts += (Plane if sides == 2 else SidePlane).scratch(rows, width)
    return parts + Column.scratch(deep, rows, width) + [DMA((5,))]


class Moves:
    def __init__(self, sem):
        self.sem, self.used = sem, 0

    def copy(self, src, dst):
        self.used += 1
        return pltpu.make_async_copy(src, dst, self.sem.at[self.used - 1])

    def blocks(self, src, dst, count, size=ROWS):
        first = self.used
        self.used += count
        return lambda i: pltpu.make_async_copy(src.at[at(i, size)], dst.at[at(i, size)], self.sem.at[first + i])

    def pairs(self, sources, targets):
        first, many = self.used, len(sources)
        self.used += many * (HEADS // 2)

        def copies(i):
            lanes = at(head_pair(i), 128)
            return [
                pltpu.make_async_copy(src.at[:, lanes], dst.at[:, lanes], self.sem.at[first + i * many + j])
                for j, (src, dst) in enumerate(zip(sources, targets))
            ]

        return copies


def start(*copies):
    for copy in copies:
        copy.start()


def wait(*copies):
    for copy in copies:
        copy.wait()


def self_fwd_kernel(
    deep, tokens, memory, out_cot, qkv_w, out_w, cq_w, lengths, gain, bias,
    row_came, memory_came, cot_came, key_own, value_own, q, k, v, mix, ext, normed, inverse, cq, qe, ke, live,
    row_s, qkv_s, out_s, cqw_s, q_s, k_s, v_s, mix_s, ext_s, normed_s, inverse_s, cq_s, qe_s, ke_s, live_s, kx_s, vx_s, memory_s, kv_s, key_s, value_s,
    sem, sem_far,
):
    place = Place(deep)
    h = place.h
    half = tokens.shape[1]
    row_length, width = row_s.shape
    blocks = row_length // ROWS
    lower, upper = pl.ds(0, half), pl.ds(half, half)
    place.greet("dh")
    moves = Moves(sem)
    own_row = moves.copy(tokens.at[h], row_s.at[lower])
    get_w = moves.copy(qkv_w, qkv_s)
    late = [moves.copy(out_w, out_s), moves.copy(cq_w.at[0], cqw_s)]
    get_memory = [moves.copy(memory.at[h], memory_s), moves.copy(cq_w.at[pl.ds(1, 2)], kv_s)]
    start(own_row, get_w)
    partner = place.device(dh=1)
    send_row = remote(tokens.at[1 - h], row_s.at[upper], sem_far.at[0], sem_far.at[1], partner)
    send_memory = remote(memory.at[1 - h], memory_came, sem_far.at[2], sem_far.at[3], partner)
    send_cot = remote(out_cot.at[1 - h, pl.ds(0, half // 2)], cot_came, sem_far.at[4], sem_far.at[5], partner)
    place.met()
    send_row.start()

    position = lax.broadcasted_iota(jnp.int32, (row_length, 128), 0)
    position = jnp.where(h == 0, position, lax.rem(position + half, row_length))
    segment = jnp.zeros((row_length, 128), jnp.int32)
    following = jnp.zeros((row_length, 128), jnp.int32)
    end = 0
    for j in range(lengths.shape[1]):
        end = end + lengths[h, j]
        segment = segment + (position >= end).astype(jnp.int32)
        following = following + (position + 1 >= end).astype(jnp.int32)
    live_s[...] = ((following == segment) & (position + 1 < row_length)).astype(F32).astype(BF)
    spare = lax.rem(lax.broadcasted_iota(jnp.int32, (row_length, 128), 1), 64)
    coded, hit = spare < lengths.shape[1], segment == spare
    qe_s[...] = jnp.where(coded & hit, BIG, 0.0).astype(BF)
    ke_s[...] = jnp.where(coded, jnp.where(hit, 0.0, -BIG), jnp.where(spare < 7, 1.0, 0.0)).astype(BF)

    def project(i):
        rows = at(i, ROWS)
        x = row_s[rows, :]
        q_s[rows, :] = dot(x, qkv_s[0]).astype(BF) * jnp.asarray(0.125, BF)
        k_s[rows, :] = dot(x, qkv_s[1]).astype(BF)
        v_s[rows, :] = dot(x, qkv_s[2]).astype(BF)

    wait(own_row, get_w)
    start(*get_memory)
    loop(blocks // 2, project)
    wait(*get_memory)
    key_s[...] = dot(memory_s[...], kv_s[0]).astype(BF)
    value_s[...] = dot(memory_s[...], kv_s[1]).astype(BF)
    send_row.wait()
    start(send_memory, send_cot)
    loop(blocks, project, blocks // 2)
    pairs = ((row_s.at[upper], row_came), (q_s, q), (k_s, k), (v_s, v), (qe_s, qe), (ke_s, ke), (live_s, live),
             (key_s, key_own), (value_s, value_own))
    outward = [moves.copy(src, dst) for src, dst in pairs]
    start(*outward, *late)
    attend(q_s, k_s, v_s, qe_s, ke_s, mix_s, ext_s, kx_s, vx_s)
    mixed = [moves.copy(mix_s, mix), moves.copy(ext_s, ext)]
    start(*mixed)
    wait(*late)
    by_block = [moves.blocks(src, dst, blocks) for src, dst in ((normed_s, normed), (inverse_s, inverse), (cq_s, cq))]

    def after(i):
        rows = at(i, ROWS)
        n, s = normalise(row_s[rows, :].astype(F32) + dot(mix_s[rows, :], out_s[...]))
        normed_s[rows, :] = n
        inverse_s[rows, :] = s
        low = (n * gain[0:1, :] + bias[0:1, :]).astype(BF)
        cq_s[rows, :] = dot(low, cqw_s[...]).astype(BF) * jnp.asarray(0.125, BF)
        start(*[copy(i) for copy in by_block])

    loop(blocks, after)
    wait(*outward, *mixed)
    loop(blocks, lambda i: wait(*[copy(i) for copy in by_block]))
    wait(send_memory, send_cot)


def cross_fwd_kernel(
    deep, slot_cot, memory_came, key_own, value_own, kv_w, cq, qe, ke, out_w, normed_one, slot_mask, gain, bias,
    slot_own, slot_came, k, v, mix, ext, normed, inverse,
    memory_s, kv_s, cq_s, qe_s, ke_s, out_s, first_s, k_s, v_s, mix_s, ext_s, normed_s, inverse_s, kx_s, vx_s, masked, sem, sem_far,
):
    place = Place(deep)
    h = place.h
    half = slot_cot.shape[1]
    place.greet("dh")
    moves = Moves(sem)
    blocks = k_s.shape[0] // ROWS
    get_slots = moves.copy(slot_cot, masked)
    get_memory = moves.copy(memory_came, memory_s)
    lower, upper = pl.ds(0, half), slice(half, 2 * half)
    get_own = [moves.copy(key_own, k_s.at[lower]), moves.copy(value_own, v_s.at[lower])]
    get_w = moves.copy(kv_w.at[pl.ds(1, 2)], kv_s)
    soon = [moves.copy(src, dst) for src, dst in ((cq, cq_s), (qe, qe_s), (ke, ke_s))]
    late = [moves.copy(src, dst) for src, dst in ((out_w, out_s), (normed_one, first_s))]
    send = remote(masked.at[1 - h], slot_came, sem_far.at[0], sem_far.at[1], place.device(dh=1))
    start(get_w, get_memory, get_slots)
    wait(get_w, get_memory)
    start(*get_own, *soon)

    place.met()
    get_slots.wait()
    columns = slot_mask[...].astype(F32).T
    for r in range(2):
        masked[r] = masked[r] * columns[:, r : r + 1].astype(BF)
    send.start()
    k_s[upper, :] = dot(memory_s[...], kv_s[0]).astype(BF)
    v_s[upper, :] = dot(memory_s[...], kv_s[1]).astype(BF)
    wait(*get_own)
    outward = [moves.copy(k_s, k), moves.copy(v_s, v), moves.copy(masked.at[h], slot_own)]
    wait(*soon)
    start(*outward, *late)
    attend(cq_s, k_s, v_s, qe_s, ke_s, mix_s, ext_s, kx_s, vx_s)
    mixed = [moves.copy(mix_s, mix), moves.copy(ext_s, ext)]
    start(*mixed)
    wait(*late)
    by_block = [moves.blocks(src, dst, blocks) for src, dst in ((normed_s, normed), (inverse_s, inverse))]

    def after(i):
        rows = at(i, ROWS)
        before = first_s[rows, :] * gain[0:1, :] + bias[0:1, :]
        n, s = normalise(before + dot(mix_s[rows, :], out_s[...]))
        normed_s[rows, :] = n
        inverse_s[rows, :] = s
        start(*[copy(i) for copy in by_block])

    loop(blocks, after)
    wait(*outward, *mixed)
    loop(blocks, lambda i: wait(*[copy(i) for copy in by_block]))
    send.wait()


def ffn_kernel(
    deep, normed_two, in_w, out_w, slot_w, slot_own, slot_came, out_cot, cot_first, live, inverse_two, cross_out_w, cross_mix,
    gain, bias,
    out_home, slots_home, res_two, grad_mix, sum_out, sum_slot, sum_in, sums,
    two_s, inw_s, outw_s, slotw_s, slot_s, cot_s, live_s, inverse_two_s, crossw_s, mix_s,
    low_s, hidden_s, slope_s, normed_s, inverse_s, pair_s, next_s, gnext_s, res_s, ginner_s, res_two_s, res_low_s, gmix_s, slots_s,
    g_out, g_slot, g_in, own_out, own_slot, own_in, came_out, sem_out, came_slot, sem_slot, came_in, sem_in,
    kept_slot, hop_slot, plane_sem, sem, sem_far,
):
    row_length, width = low_s.shape
    blocks = row_length // ROWS
    units = in_w.shape[1]
    half = row_length // 2
    place = Place(deep)
    place.greet("dh", "dcore", "dy")
    h = place.h
    scale = 0.7978845608028654
    moves = Moves(sem)
    get_two = moves.blocks(normed_two, two_s, blocks)
    first = [moves.copy(in_w, inw_s), moves.copy(out_w, outw_s)]
    lower, upper, quarter = pl.ds(0, half), pl.ds(half, half), half // 2
    soon = [
        moves.copy(src, dst)
        for src, dst in ((slot_w, slotw_s), (slot_own, slot_s.at[lower]), (slot_came, slot_s.at[upper]), (live, live_s))
    ]
    late = [
        moves.copy(src, dst)
        for src, dst in ((out_cot.at[h], cot_s.at[lower]), (cot_first, cot_s.at[pl.ds(half, quarter)]), (inverse_two, inverse_two_s), (cross_out_w, crossw_s), (cross_mix, mix_s))
    ]
    work_out = CoreSum(place, g_out, own_out, came_out, sem_out)
    work_slot = CoreSum(place, g_slot, own_slot, came_slot, sem_slot)
    work_in = CoreSum(place, g_in, own_in, came_in, sem_in)
    plane_slot = Plane(place, own_slot, kept_slot, hop_slot, None, None, plane_sem, False)

    def home(src, dst, i):
        lanes = pl.ds(0, width)
        return (
            moves.copy(src.at[lower, lanes], dst.at[h]),
            remote(src.at[upper, lanes], dst.at[h], sem_far.at[2 * i], sem_far.at[2 * i + 1], place.device(dh=1)),
        )

    homeward = home(pair_s, out_home, 0) + home(slots_s, slots_home, 1)
    cot_rest = remote(
        out_cot.at[1 - h, pl.ds(quarter, quarter)], cot_s.at[pl.ds(half + quarter, quarter)], sem_far.at[4], sem_far.at[5], place.device(dh=1)
    )
    last = blocks - 1
    get_two(last).start()
    start(*first)
    place.met()
    cot_rest.start()
    wait(*first)
    loop(last, lambda i: get_two(i).start())
    start(*soon, *late)

    def forward(i):
        rows = at(i, ROWS)
        get_two(i).wait()
        after_cross = two_s[rows, :] * gain[1:2, :] + bias[1:2, :]
        low = after_cross.astype(BF)
        low_s[rows, :] = low
        for c in range(units // 512):
            cols = slice(c * 512, (c + 1) * 512)
            inner = dot(low, inw_s[:, cols])
            square = inner * inner
            bent = jnp.tanh(inner * (scale + (scale * 0.044715) * square))
            part = 0.5 + 0.5 * bent
            hidden_s[rows, cols] = (inner * part).astype(BF)
            slope = part + inner * (0.5 - 0.5 * bent * bent) * (scale + (3 * scale * 0.044715) * square)
            slope_s[rows, cols] = slope.astype(BF)
        n, s = normalise(after_cross + dot(hidden_s[rows, :], outw_s[...]))
        normed_s[rows, :] = n
        inverse_s[rows, :] = s
        final = (n * gain[2:3, :] + bias[2:3, :]).astype(BF)
        pair_s[rows, :width] = final
        next_s[rows, :] = final.astype(F32)

    def backwards(body, sent):
        def one(i):
            body(last - i)
            pl.when(i == (blocks - 1) // 2)(sent)

        loop(blocks, one)

    backwards(forward, lambda: homeward[1].start())
    homeward[0].start()
    next_s[pl.ds(row_length, 8), :] = next_s[pl.ds(0, 8), :]
    wait(*soon)

    def slot(i):
        rows = at(i, ROWS)
        window = pl.ds(pl.multiple_of(i * ROWS, ROWS), ROWS + 8)
        alive = live_s[rows, 0:1].astype(F32)
        pair_s[rows, width:] = (next_s[window, :][1 : ROWS + 1] * alive).astype(BF)
        slots_s[rows, :] = dot(pair_s[rows, :], slotw_s[...]).astype(BF)
        back = (dot_nt(slot_s[rows, :], slotw_s[width:, :]) * alive).astype(BF)
        gnext_s[pl.ds(pl.multiple_of(i * ROWS + 8, 8), ROWS), :] = back.astype(F32)

    backwards(slot, lambda: homeward[3].start())
    homeward[2].start()
    gnext_s[pl.ds(0, 8), :] = gnext_s[pl.ds(row_length, 8), :]
    sums[...] = jnp.zeros(sums.shape, F32)
    fill(g_slot, width)
    for side in range(2):
        g_slot[side, :width, :] = dot_tn(pair_s[:, side * width : (side + 1) * width], slot_s[...]).astype(BF)
    work_slot.begin()
    wait(*late)
    cot_rest.wait()
    by_block = [moves.blocks(src, dst, blocks) for src, dst in ((res_two_s, res_two), (gmix_s, grad_mix))]

    def backward(i):
        @pl.when(i == 1)
        def slot_hop():
            work_slot.finish()
            plane_slot.begin_a()

        rows = at(i, ROWS)
        window = pl.ds(pl.multiple_of(i * ROWS, ROWS), ROWS + 8)
        gradient = (
            cot_s[rows, :].astype(F32)
            + dot_nt(slot_s[rows, :], slotw_s[:width, :])
            + gnext_s[window, :][7 : ROWS + 7]
        )
        n = normed_s[rows, :]
        sums[0:1, :] += jnp.sum(gradient * n, axis=0, keepdims=True)
        sums[1:2, :] += jnp.sum(gradient, axis=0, keepdims=True)
        res = norm_back(gradient, n, inverse_s[rows, :], gain[2:3, :])
        res_low = res.astype(BF)
        res_s[rows, :] = res_low
        for c in range(units // 512):
            cols = slice(c * 512, (c + 1) * 512)
            ginner_s[rows, cols] = (dot_nt(res_low, outw_s[cols, :]) * slope_s[rows, cols].astype(F32)).astype(BF)
        res = res + dot_nt(ginner_s[rows, :], inw_s[...])
        n = two_s[rows, :]
        sums[2:3, :] += jnp.sum(res * n, axis=0, keepdims=True)
        sums[3:4, :] += jnp.sum(res, axis=0, keepdims=True)
        res = norm_back(res, n, inverse_two_s[rows, :], gain[1:2, :])
        res_two_s[rows, :] = res
        res_low = res.astype(BF)
        res_low_s[rows, :] = res_low
        gmix_s[rows, :] = dot_nt(res_low, crossw_s[...]).astype(BF)
        start(*[copy(i) for copy in by_block])

    loop(blocks, backward)
    fill(g_out, units // 2 + width // 2)
    fill(g_in, width * units // 1024)
    for side in range(2):
        g_out[side, units // 2 : units // 2 + width // 2, :] = dot_tn(
            mix_s[:, side * 256 : (side + 1) * 256], res_low_s[...]
        ).astype(BF)
    for side in range(2):
        g_out[side, : units // 2, :] = dot_tn(hidden_s[:, side * (units // 2) : (side + 1) * (units // 2)], res_s[...]).astype(BF)
    work_out.begin()
    for c in range(units // 512):
        side, block = divmod(c, units // 1024)
        g_in[side, block * width : (block + 1) * width, :] = dot_tn(low_s[...], ginner_s[:, c * 512 : (c + 1) * 512]).astype(BF)
    work_in.begin()
    done = [moves.copy(src, dst) for src, dst in ((own_out, sum_out), (kept_slot, sum_slot), (own_in, sum_in))]
    for finish, copy in zip((work_out.finish, plane_slot.finish_a, work_in.finish), done):
        finish()
        copy.start()
    loop(blocks, lambda i: wait(*[copy(i) for copy in by_block]))
    wait(*done, *homeward)


def fill(grads, used):
    rest = grads.shape[1] - used
    if rest:
        grads[:, used:, :] = jnp.zeros((grads.shape[0], rest, grads.shape[2]), BF)


def weight_grads(grads, pairs, sources):
    for left, rights, first in sources:
        right = jnp.concatenate([d[:, p * 128 : (p + 1) * 128] for d in rights for p in pairs], axis=1)
        width = left.shape[1]
        block = dot_tn(left[...], right).astype(BF)
        for i in range(len(rights)):
            for side in range(len(pairs)):
                lane = (i * len(pairs) + side) * 128
                grads[side, (first + i) * width : (first + i + 1) * width, :] = block[:, lane : lane + 128]


PLAN = {
    "begin": (("out", 0), ("in", 0), ("slot", 0),),
    "c0": (("slot", 1),),
    "c1": (("slot", 2),),
    "c2": (("slot", 3),),
    "c3": (("d1", 0), ("slot", 4),),
    "c4": (("d1", 1), ("slot", 5),),
    "c6": (("d1", 2), ("in", 1),),
    "c7": (("out", 1), ("slot", 6),),
    "c8": (("d1", 3),),
    "c9": (("d2", 0), ("in", 2),),
    "c10": (("d1", 4), ("mem", 0),),
    "s0": (("d2", 1), ("d1", 5), ("in", 3),),
    "s1": (("out", 2),),
    "s2": (("d1", 6), ("in", 4),),
    "s3": (("e1", 0), ("d2", 2), ("d1", 7), ("out", 3),),
    "s4": (("e1", 1), ("d1", 8), ("in", 5),),
    "s5": (("e2", 0), ("d2", 3), ("out", 4),),
    "s6": (("e2", 1), ("e1", 2), ("d2", 4), ("in", 6),),
    "s7": (("d2", 5), ("out", 5),),
    "s8": (("f", 0), ("e1", 3),),
    "s9": (("e2", 2), ("row", 0),),
    "s10": (("f", 1), ("d2", 6),),
    "tail": (("e1", 4), ("in", 7), ("out", 6), ("e1", 5), ("f", 2), ("d2", 7), ("e2", 3), ("e1", 6), ("e2", 4), ("f", 3),
        ("e1", 7), ("e2", 5), ("f", 4), ("d2", 8), ("f", 5), ("e2", 6), ("e1", 8), ("out", 7), ("f", 6), ("out", 8),
        ("in", 8), ("slot", 7), ("d1", 9), ("d2", 9), ("e1", 9), ("e2", 7), ("row", 1), ("mem", 1), ("f", 7),),
}


def back_kernel(
    deep, own_out, own_in, own_slot, cq, ck, cv, cext, cmix, gcmix, memory, memory_came, cross_w, res_two, normed_one, inverse_one,
    q, k, v, ext, mix, out_w, tokens, tokens_came, self_w, ke, gain, bias, sums_two,
    done_out, done_in, done_slot, done_d1, done_d2, done_e, done_f, mem_mine, mem_came, row_mine, row_came,
    q_s, k_s, v_s, ext_s, mix_s, gmix_s, memory_s, row_s, low_s, dq_s, dk_s, dv_s, res_s, cross_ws, self_ws, outw_s,
    res_two_s, normed_s, res_one_s, inverse_s, sums, mine_s, theirs_s, row_theirs,
    kx_s, vx_s, qx_s, dx_s, extra_s, kt_s, dqt_s, sem, sem_far, *comm,
):
    row_length, width = row_s.shape
    blocks = row_length // ROWS
    half_blocks = blocks // 2
    half = row_length // 2
    lower, upper = pl.ds(0, half), pl.ds(half, half)
    place = Place(deep)
    place.greet("dh", "dy", "dz", "dcore")
    moves = Moves(sem)
    cross_pairs = moves.pairs((cq, ck, cv, cext, cmix, gcmix), (q_s, k_s, v_s, ext_s, mix_s, gmix_s))
    late = [
        moves.copy(src, dst)
        for src, dst in ((normed_one, normed_s), (memory.at[place.h], memory_s.at[lower]), (memory_came, memory_s.at[upper]),
                         (cross_w, cross_ws), (inverse_one, inverse_s), (res_two, res_two_s), (out_w, outw_s),
                         (tokens.at[place.h], row_s.at[lower]), (tokens_came, row_s.at[upper]), (self_w, self_ws))
    ]
    again = [moves.copy(src, dst) for src, dst in ((q, q_s), (k, k_s), (v, v_s), (ext, ext_s), (mix, mix_s))]
    start(*cross_pairs(0))
    comm = list(comm)
    take = lambda n: [comm.pop(0) for _ in range(n)]
    get_slot = moves.copy(own_slot, comm[18])
    get_slot.start()
    chains = {
        "out": chain(place, "own", take(9), done_out, False, own=own_out),
        "in": chain(place, "own", take(9), done_in, False, own=own_in),
        "slot": chain(place, "kept", take(9), done_slot, False),
    }
    grads = {}
    for name, done, x_first, side in (("d1", done_d1, True, None), ("d2", done_d2, False, None), ("e1", done_e, False, None),
                                      ("e2", done_f, False, 0), ("f", done_f, False, 1)):
        buffers = take(13)
        grads[name] = buffers[0]
        chains[name] = chain(place, None, buffers, done, x_first, side)
    mem_send = remote(theirs_s, mem_came, sem_far.at[0], sem_far.at[1], place.device(dh=1))
    row_send = remote(row_theirs, row_came, sem_far.at[2], sem_far.at[3], place.device(dh=1))
    chains["mem"] = [mem_send.start, mem_send.wait]
    chains["row"] = [row_send.start, row_send.wait]

    def run(point):
        for name, stage in PLAN.get(point, ()):
            chains[name][stage]()

    def hooks(letter, extra):
        table = {}
        for step in range(HEADS):
            point = letter + str(step)
            if step in extra or point in PLAN:
                def hook(point=point, step=step):
                    if step in extra:
                        extra[step]()
                    run(point)

                table[step] = hook
        return table

    def low_rows():
        wait(*late)

        def one(i):
            rows = at(i, ROWS)
            low_s[rows, :] = (normed_s[rows, :] * gain[0:1, :] + bias[0:1, :]).astype(BF)

        loop(blocks, one)

    cross_sources = ((low_s, (dq_s,), 0), (memory_s, (dk_s, dv_s), 1))
    self_sources = ((row_s, (dq_s, dk_s, dv_s), 0),)
    for name, used in (("d1", 3 * width), ("d2", 5 * width), ("e1", 3 * width + 16), ("e2", 3 * width), ("f", 3 * width)):
        fill(grads[name], used)
    place.met()
    get_slot.wait()
    run("begin")
    loop(HEADS // 2, lambda i: start(*cross_pairs(i)), 1)
    start(*late)
    scratch = (dq_s, dk_s, dv_s, kx_s, vx_s, qx_s, dx_s, extra_s, kt_s, dqt_s)
    attend_back(
        q_s, k_s, v_s, ext_s, ke, mix_s, gmix_s, *scratch,
        hooks("c", {1: low_rows, 3: lambda: weight_grads(grads["d1"], (0, 2), cross_sources)}), cross_pairs,
    )
    start(*again)
    sums[...] = jnp.zeros(sums.shape, F32)

    def backward(i):
        rows = at(i, ROWS)
        n = normed_s[rows, :]
        gradient = res_two_s[rows, :] + dot_nt(dq_s[rows, :], cross_ws[0])
        sums[0:1, :] += jnp.sum(gradient * n, axis=0, keepdims=True)
        sums[1:2, :] += jnp.sum(gradient, axis=0, keepdims=True)
        res = norm_back(gradient, n, inverse_s[rows, :], gain[0:1, :])
        res_one_s[rows, :] = res
        res_low = res.astype(BF)
        res_s[rows, :] = res_low
        gmix_s[rows, :] = dot_nt(res_low, outw_s[...]).astype(BF)

    loop(blocks, backward)
    run("c8")
    weight_grads(grads["d2"], (1, 3), cross_sources)
    wait(*again)
    for side in range(2):
        block = dot_tn(mix_s[:, side * 256 : (side + 1) * 256], res_s[...]).astype(BF)
        for c in range(width // 128):
            grads["d2"][side, 3 * width + c * 256 : 3 * width + (c + 1) * 256, :] = block[:, c * 128 : (c + 1) * 128]
    run("c9")
    put_mem = moves.blocks(mine_s, mem_mine, half_blocks)
    put_row = moves.blocks(mine_s, row_mine, half_blocks)

    def memory_grad(i):
        rows = at(i, ROWS)
        return dot_nt(dk_s[rows, :], cross_ws[1]) + dot_nt(dv_s[rows, :], cross_ws[2])

    def memory_theirs(i):
        theirs_s[at(i, ROWS), :] = memory_grad(i + half_blocks).astype(BF)

    def memory_mine(i):
        mine_s[at(i, ROWS), :] = memory_grad(i)
        put_mem(i).start()

    loop(half_blocks, memory_theirs)
    run("c10")
    loop(half_blocks, memory_mine)

    def first_grads():
        weight_grads(grads["e1"], (0, 2), self_sources)
        norms = jnp.concatenate(
            [sums[0:1, :], sums_two[2:3, :], sums_two[0:1, :], sums[1:2, :], sums_two[3:4, :], sums_two[1:2, :]], axis=0
        ).astype(BF)
        for side in range(2):
            parts = [norms[:, side * 256 + c * 128 : side * 256 + (c + 1) * 128] for c in range(2)]
            grads["e1"][side, 3 * width : 3 * width + 16, :] = jnp.concatenate(parts + [jnp.zeros((4, 128), BF)], axis=0)

    attend_back(
        q_s, k_s, v_s, ext_s, ke, mix_s, gmix_s, *scratch,
        hooks("s", {3: first_grads, 5: lambda: weight_grads(grads["e2"], (1,), self_sources)}), lambda i: (),
    )
    weight_grads(grads["f"], (3,), self_sources)
    run("s8")

    def row_grad(i):
        rows = at(i, ROWS)
        return (
            res_one_s[rows, :] + dot_nt(dq_s[rows, :], self_ws[0]) + dot_nt(dk_s[rows, :], self_ws[1]) + dot_nt(dv_s[rows, :], self_ws[2])
        )

    def row_other(i):
        row_theirs[at(i, ROWS), :] = row_grad(i + half_blocks).astype(BF)

    def row_own(i):
        put_mem(i).wait()
        mine_s[at(i, ROWS), :] = row_grad(i)
        put_row(i).start()

    loop(half_blocks, row_other)
    run("s9")
    loop(half_blocks, row_own)
    run("s10")
    run("tail")
    loop(half_blocks, lambda i: put_row(i).wait())


def finish_kernel(
    deep, out, slots, row_mine, row_came, mem_mine, mem_came, done_in, done_out, done_slot, done_d1, done_d2, done_e, done_f, slot_mask,
    out_f, slots_f, tokens_f, memory_f, self_qkv_f, self_out_f, cross_qkv_f, cross_out_f, norms_f, ffn_in_f, ffn_out_f, slot_f,
    slots_s, row_s, mem_s, in_s, outs_s, slot_s, d1_s, d2_s, e_s, f_s, masked_s, row_w, mem_w, in_w, out_w, slot_w, cross_w,
    cqkv_w, sout_w, sqkv_w, out_b, mem_b, row_b, sem,
):
    h = lax.axis_index("head")
    moves = Moves(sem)
    width = out.shape[2]
    loads = [
        moves.copy(src, dst)
        for src, dst in ((done_out, outs_s), (done_in, in_s), (done_slot, slot_s), (slots, slots_s), (mem_came, mem_s), (done_d1, d1_s),
                         (done_d2, d2_s), (row_came, row_s), (done_e, e_s), (done_f, f_s), (out, out_b), (mem_mine, mem_b), (row_mine, row_b))
    ]
    start(*loads)
    stores = []

    def put(src, dst):
        copy = moves.copy(src, dst)
        copy.start()
        stores.append(copy)

    half = out_w.shape[0]
    loads[0].wait()
    out_w[...] = outs_s[:half, :].astype(F32)
    put(out_w, ffn_out_f)
    loads[1].wait()
    for c in range(in_w.shape[1] // 512):
        in_w[:, c * 512 : (c + 1) * 512] = in_s[c * width : (c + 1) * width, :].astype(F32)
    put(in_w, ffn_in_f)
    cross_w[...] = outs_s[half : half + width // 2, :].astype(F32)
    put(cross_w, cross_out_f)
    loads[2].wait()
    slot_w[...] = slot_s[:width, :].astype(F32)
    put(slot_w, slot_f)
    loads[3].wait()
    columns = slot_mask[...].astype(F32).T
    for r in range(2):
        masked_s[r] = slots_s[r] * columns[:, r : r + 1].astype(BF)
    put(masked_s, slots_f)
    loads[4].wait()
    mem_w[...] = mem_s[...].astype(F32)
    put(mem_w, memory_f.at[1 - h])
    wait(loads[5], loads[6])
    for c, part_s in enumerate((d1_s, d2_s)):
        for part in range(3):
            cqkv_w[part, :, c * 128 : (c + 1) * 128] = part_s[part * width : (part + 1) * width, :].astype(F32)
    put(cqkv_w, cross_qkv_f)
    for c in range(width // 128):
        sout_w[:, c * 128 : (c + 1) * 128] = d2_s[3 * width + c * 256 : 3 * width + (c + 1) * 256, :].astype(F32)
    put(sout_w, self_out_f)
    loads[7].wait()
    row_w[...] = row_s[...].astype(F32)
    put(row_w, tokens_f.at[1 - h])
    wait(loads[8], loads[9])
    for c, part_s in enumerate((e_s, f_s)):
        for part in range(3):
            sqkv_w[part, :, c * 128 : (c + 1) * 128] = part_s[part * width : (part + 1) * width, :].astype(F32)
    norms = e_s[3 * width : 3 * width + 16, :].astype(F32)
    for c in range(2):
        norms_f[:, c * 128 : (c + 1) * 128] = norms[6 * c : 6 * c + 6]
    put(sqkv_w, self_qkv_f)
    for load, src, dst in zip(loads[10:], (out_b, mem_b, row_b), (out_f, memory_f.at[h], tokens_f.at[h])):
        load.wait()
        put(src, dst)
    wait(*stores)


def call(kernel, name, cid, args, outs, scratch, flops):
    if cid is None:
        params = pltpu.CompilerParams(vmem_limit_bytes=VMEM)
    else:
        params = pltpu.CompilerParams(collective_id=cid, has_side_effects=True, vmem_limit_bytes=VMEM)
    return pl.pallas_call(
        kernel,
        out_shape=[jax.ShapeDtypeStruct(shape, kind) for shape, kind, _ in outs],
        in_specs=[spec for _, spec in args],
        out_specs=[spec for _, _, spec in outs],
        scratch_shapes=scratch,
        compiler_params=params,
        cost_estimate=pl.CostEstimate(flops=flops, bytes_accessed=2**20, transcendentals=0),
        name=name,
    )(*[arg for arg, _ in args])


def padded(count, unit):
    return -(-count // unit) * unit


def per_device(
    tokens, memory, lengths, slot_mask, self_qkv, self_out, cross_qkv, cross_out,
    norm_gain, norm_bias, ffn_in, ffn_out, slot_proj, out_cot, slot_cot,
):
    local_len, width = tokens.shape[1:]
    units = ffn_in.shape[1]
    deep = lax.axis_size("dp") // 4
    row_length = 2 * local_len
    unit = 64 * deep
    rows_out, rows_slot, rows_in = padded(units // 2 + width // 2, unit), padded(width, unit), padded(width * units // 1024, unit)
    rows_d1, rows_d2, rows_e = padded(3 * width, unit), padded(5 * width, unit), padded(3 * width + 16, unit)
    dense = 2 * row_length * width * width
    scores = 2 * row_length * row_length * width

    def inner(*values):
        return [(value, INNER) for value in values]

    def outer(*values):
        return [(value, ANY) for value in values]

    def new(*shape, kind=BF, spec=INNER):
        return (shape, kind, spec)

    def scratch(*shape, kind=BF):
        return pltpu.VMEM(shape, kind)

    row, wide, column = (
        new(row_length, width, spec=ANY), new(row_length, width, kind=F32, spec=ANY), new(row_length, 1, kind=F32, spec=ANY)
    )
    small = new(row_length, 128, spec=ANY)
    row_s, wide_s, two_s = scratch(row_length, width), scratch(row_length, width, kind=F32), scratch(row_length, 256)
    tall_s, ring_s = scratch(row_length, units), scratch(row_length + 8, width, kind=F32)
    column_s, small_s, half_s = scratch(row_length, 1, kind=F32), scratch(row_length, 128), scratch(local_len, width)
    square_s, three_s = scratch(width, width), scratch(3, width, width)
    half_wide_s = scratch(local_len, width, kind=F32)

    half, part = new(local_len, width, spec=ANY), new(local_len // 2, width, spec=ANY)
    tokens_came, memory_came, cot_first, key_own, value_own, q, k, v, mix, ext, normed_one, inverse_one, cq, qe, ke, live = call(
        functools.partial(self_fwd_kernel, deep), "self_fwd", 0,
        outer(tokens, memory, out_cot, self_qkv, self_out, cross_qkv) + [(lengths, SCALARS)] + inner(norm_gain, norm_bias),
        [half, half, part, half, half] + [row] * 5 + [wide, column, row] + [small] * 3,
        [row_s, three_s, square_s, square_s] + [row_s] * 5 + [wide_s, column_s, row_s]
        + [small_s] * 3 + [two_s, two_s, half_s, scratch(2, width, width), half_s, half_s, DMA((40,)), DMA((6,))], 5 * dense + 8 * scores,
    )
    slot_own, slot_came, ck, cv, cmix, cext, normed_two, inverse_two = call(
        functools.partial(cross_fwd_kernel, deep), "cross_fwd", 1,
        outer(slot_cot, memory_came, key_own, value_own, cross_qkv, cq, qe, ke, cross_out, normed_one) + inner(slot_mask, norm_gain, norm_bias),
        [half, half] + [row] * 4 + [wide, column],
        [half_s, scratch(2, width, width), row_s, small_s, small_s, square_s, wide_s] + [row_s] * 4 + [wide_s, column_s]
        + [two_s, two_s, scratch(2, local_len, width), DMA((40,)), DMA((2,))], 3 * dense + 8 * scores,
    )
    home = new(2, local_len, width, spec=ANY)
    groups = ((rows_out, 512), (rows_slot, 512), (rows_in, 512))
    out, slots, res_two, grad_cmix, sum_out, sum_slot, sum_in, sums_two = call(
        functools.partial(ffn_kernel, deep), "ffn", 2,
        outer(normed_two, ffn_in, ffn_out, slot_proj, slot_own, slot_came, out_cot, cot_first, live, inverse_two, cross_out, cmix) + inner(norm_gain, norm_bias),
        [home, home, wide, row, new(2, 2, rows_out // 4, 512, spec=ANY), new(2, rows_slot // 4, 512, spec=ANY),
         new(2, 2, rows_in // 4, 512, spec=ANY), new(8, width, kind=F32)],
        [wide_s, scratch(width, units), scratch(units, width), scratch(2 * width, width), row_s, row_s, small_s, column_s, square_s, row_s]
        + [row_s, tall_s, tall_s, wide_s, column_s, scratch(row_length, 2 * width), ring_s, ring_s, row_s, tall_s, wide_s]
        + [row_s] * 3
        + [scratch(2, rows, lanes) for rows, lanes in groups] + [scratch(2, 2, rows // 4, lanes) for rows, lanes in groups]
        + [part for group in groups for part in CoreSum.scratch(*group)]
        + [scratch(2, rows_slot // 4, 512), scratch(2, rows_slot // 4, 512), DMA((5,)), DMA((40,)), DMA((6,))], 32 * dense,
    )
    back = [small_s] * 5 + [scratch(128, row_length), scratch(128, row_length, kind=F32)]

    half_wide = new(local_len, width, kind=F32, spec=ANY)
    late = ((rows_d1, 128, 2), (rows_d2, 128, 2), (rows_e, 128, 2), (rows_d1, 128, 1), (rows_d1, 128, 1))

    def whole(rows, lanes):
        return new(rows, lanes, spec=ANY)

    done_out, done_in, done_slot, done_d1, done_d2, done_e, done_f, mem_mine, mem_came, row_mine, row_came = call(
        functools.partial(back_kernel, deep), "back", 3,
        outer(sum_out, sum_in, sum_slot, cq, ck, cv, cext, cmix, grad_cmix, memory, memory_came, cross_qkv, res_two, normed_one,
              inverse_one, q, k, v, ext, mix, self_out, tokens, tokens_came, self_qkv) + inner(ke, norm_gain, norm_bias, sums_two),
        [whole(rows_out, 512), whole(rows_in, 512), whole(rows_slot, 512), whole(rows_d1, 128), whole(rows_d2, 128), whole(rows_e, 128),
         whole(rows_d1, 128), half_wide, half, half_wide, half],
        [row_s] * 13 + [three_s, three_s, square_s] + [wide_s] * 3 + [column_s, scratch(8, width, kind=F32), half_wide_s, half_s, half_s]
        + back + [DMA((60,)), DMA((4,))]
        + [part for rows in (rows_out, rows_in, rows_slot) for part in chain_scratch(deep, rows, 512, "own")]
        + [part for rows, lanes, sides in late for part in chain_scratch(deep, rows, lanes, None, sides)],
        22 * dense + 40 * scores,
    )

    def final(*shape, kind=F32):
        return new(*shape, kind=kind, spec=ANY)

    def wide_scratch(*shape):
        return scratch(*shape, kind=F32)

    pair_s = scratch(2, local_len, width)
    results = call(
        functools.partial(finish_kernel, deep), "finish", None,
        outer(out, slots, row_mine, row_came, mem_mine, mem_came, done_in, done_out, done_slot, done_d1, done_d2, done_e, done_f)
        + inner(slot_mask),
        [final(2, local_len, width, kind=BF)] * 2 + [final(2, local_len, width)] * 2
        + [final(3, width, 256), final(width // 2, width), final(3, width, 256), final(width // 2, width)]
        + [new(6, 256, kind=F32)] + [final(width, units // 2), final(units // 2, width), final(width, width)],
        [pair_s, half_s, half_s, scratch(rows_in, 512), scratch(rows_out, 512), scratch(rows_slot, 512), scratch(rows_d1, 128),
         scratch(rows_d2, 128), scratch(rows_e, 128), scratch(rows_d1, 128), pair_s, half_wide_s, half_wide_s, wide_scratch(width, units // 2),
         wide_scratch(units // 2, width), wide_scratch(width, width), wide_scratch(width // 2, width), wide_scratch(3, width, 256),
         wide_scratch(width // 2, width), wide_scratch(3, width, 256), pair_s, half_wide_s, half_wide_s, DMA((40,))], 0,
    )
    norms = results[8]
    return (*results[:8], norms[:3], norms[3:], *results[9:])


def solution(mesh):
    split = P("dp", "head", None)
    placed = (split, split, P("dp", None), P("dp", "head")) + (P(),) * 9 + (split, split)
    return jax.shard_map(
        per_device,
        mesh=mesh,
        in_specs=placed,
        out_specs=(
            split, split, split, split,
            P(None, None, "head"), P("head", None), P(None, None, "head"), P("head", None),
            P(None, "head"), P(None, "head"), P(None, "head"), P("head", None), P("head", None),
        ),
        check_vma=False,
    )
```
